32 devices in a mesh: groups: 2 (over x), tensor: 16 (over z, y, core).
Axes of the slice: x: 2, y: 2, z: 4, core: 2. Of those that a mesh axis runs over, the one named last changes fastest.
Arguments:
- queries: bfloat16 [256, 4096], P(('groups', 'tensor')), parts along dimension 0, may hold values from -6 to 6
- corpus: bfloat16 [2048, 4, 4096], P(('groups', 'tensor')), parts along dimension 0, may hold values from -6 to 6
- block_owner: int32 [48, 1], P('groups'), parts along dimension 0, may hold values from 0 to 15; in each aligned block of 24 rows (0 to 23, 24 to 47, ...) at most 3 rows name the same one
- slot_row: int32 [48], P('groups'), parts along dimension 0, may hold values from 0 to 63
- segment: int32 [48], P('groups'), parts along dimension 0, may hold values from 0 to 3, never falling along the last dimension, each value on 1 to 12 neighbouring positions
- query_weight: bfloat16 [1024, 4096], P('tensor'), may hold values from -3 to 3
- key_weight: bfloat16 [1024, 4096], P('tensor'), may hold values from -3 to 3
- value_weight: bfloat16 [1024, 4096], P('tensor'), may hold values from -0.09375 to 0.09375
- out_weight: bfloat16 [1024, 4096], P('tensor'), may hold values from -0.1875 to 0.1875
- gain_attn: float32 [4096], replicated, may hold values from 0.1 to 1.9
- gain_ffn: float32 [4096], replicated, may hold values from 0.1 to 1.9
- gate_weight: bfloat16 [2560, 4096], P('tensor'), may hold values from -0.09375 to 0.09375
- up_weight: bfloat16 [2560, 4096], P('tensor'), may hold values from -0.09375 to 0.09375
- down_weight: bfloat16 [2560, 4096], P('tensor'), may hold values from -0.125 to 0.125
Outputs:
- encoded: bfloat16 [448, 4096], P(('groups', 'tensor')), parts along dimension 0
The draws below stay inside these ranges and needn't reach their ends.
There are 2 independent parts, one for each index of `groups`. The reference program is written for one: setup_inputs(seed, part) draws one part's arguments, and reference() takes and returns one part's arrays. A program takes and returns all parts, laid end to end along the dimension named above; an argument that names none is the same for every part. Nothing has to cross between parts.
Inputs may be any that keep to these rules, and one draw needn't show every extreme that they name: `block_owner`: every owner holds some block of the pack; no owner holds more than 3 of them, and some owner holds exactly 3. `segment`: never falls along the pack; each pair has 1 to 12 blocks, one exactly 12.
All inputs are finite; a program needn't handle non-finite values.
Results may differ from the reference program's by a relative error of at most 0.008.
Values may be sent and summed in bfloat16 or wider, within the bound.
No kernel may reach another device: no remote copies, remote signals or barrier semaphores. Data moves between devices by JAX's collectives and lax.ppermute only.
A program may use at most 64 MiB of HBM per device.

```python
import math
import jax
import jax.numpy as jnp
import numpy as np
from jax import lax

D = 4096
HDIM = 64
QLEN = 32
PAIRS = 4
BLK = 4
CAP = 3
CORP_DEV = 64
HEADS = 16
FF = 2560
NBLK = 24
MOSTB = 12
QROWS = 128
TOK = 224
CORPUS = 1024
N_TENSOR = 16


def shared_base(key):
    return jax.random.truncated_normal(jax.random.fold_in(key, 11), -4.0, 4.0, (HEADS * HDIM, D), jnp.float32) * D ** (-0.5)


def draw_query_weight(key, part):
    base_matrix = shared_base(key)
    return base_matrix.astype(jnp.bfloat16)


def draw_key_weight(key, part):
    other_matrix = jax.random.truncated_normal(jax.random.fold_in(key, 23), -4.0, 4.0, (HEADS * HDIM, D), jnp.float32) * D ** (-0.5)
    return other_matrix.astype(jnp.bfloat16)


def touch_ends(result, own_key, low, largest):
    spot = [jax.random.randint(jax.random.fold_in(own_key, axis), (), 0, length) for axis, length in enumerate(result.shape)]
    longest = result.shape.index(max(result.shape))
    next_to = spot[:longest] + [(spot[longest] + 1) % result.shape[longest]] + spot[longest + 1:]
    return result.at[tuple(spot)].set(low).at[tuple(next_to)].set(largest)


def block_scale(rng, extent, cuts, least, top_value):
    def one(position, shards_of):
        draws = jax.random.uniform(jax.random.fold_in(jax.random.fold_in(rng, 6), position), (shards_of,), jnp.float32, least / len(cuts), top_value / len(cuts))
        return jnp.repeat(jnp.exp(draws), extent[position] // shards_of).reshape((-1,) + (1,) * (len(extent) - position - 1))

    level = one(*cuts[0])
    for cut in cuts[1:]:
        level = level * one(*cut)
    return level


def length_profile(amount, total, limit, lean):
    loads = [(1 << 20) // math.isqrt(standing ** lean) + 1 for standing in range(2, amount + 1)]
    surplus, counts = total - limit - (amount - 1), [1] * (amount - 1)
    while surplus > 0:
        movable = [i for i in range(amount - 1) if counts[i] < limit]
        pool, left = sum([loads[i] for i in movable]), surplus
        for i in movable:
            extra = min(limit - counts[i], max(1, left * loads[i] // pool), surplus)
            counts[i] = counts[i] + extra
            surplus = surplus - extra
    return np.array([limit] + counts)


def ragged_sizes(stream_key, count, total, limit, skew):
    if count == 2:
        one = jax.random.randint(stream_key, (), max(1, total - limit), min(limit, total - 1) + 1)
        return jnp.stack([one, total - one])
    sizes = jnp.asarray(length_profile(count, total, limit, skew), jnp.int32)
    couples = (count - 1) // 2
    donor, sink = sizes[1:1 + 2 * couples:2], sizes[2:2 + 2 * couples:2]
    slack = jnp.minimum(donor - 1, limit - sink)
    passed = jax.random.randint(jax.random.fold_in(stream_key, 1), (couples,), 0, 1 << 20) % (slack + 1)
    sizes = sizes.at[1:1 + 2 * couples:2].set(donor - passed).at[2:2 + 2 * couples:2].set(sink + passed)
    return sizes[jax.random.permutation(jax.random.fold_in(stream_key, 2), count)]


def shared_out(rng, own, number, rows, count, top, bound, slope):
    order = jax.random.permutation(rng, count)
    heavy_load, ordinary = portions_of(count, rows * top, bound, slope, True), portions_of(count, rows * top, bound, slope, False)
    places = jnp.arange(count)

    def named(tallies, turn):
        used = int((tallies > 0).sum())
        fixed = max(1, used // 4)
        moved = fixed + (places - fixed + turn * (used - fixed)) % max(1, count - fixed)
        return jnp.zeros((count,), jnp.int32).at[order[jnp.where(places < fixed, places, moved)]].set(jnp.asarray(tallies, jnp.int32))

    tallies = jnp.where(number % 4 == 0, named(heavy_load, number // 4), named(ordinary, number - number // 4 - 1))
    mixed = jax.random.permutation(jax.random.fold_in(own, 3), count)
    giver, taker = mixed[0:count // 2 * 2:2], mixed[1:count // 2 * 2:2]
    margin = jnp.minimum(tallies[giver] - 1, bound - tallies[taker]) // 2
    margin = jnp.where((giver == order[0]) | (taker == order[0]) | (tallies[taker] == 0), 0, jnp.maximum(margin, 0))
    moved = jax.random.randint(jax.random.fold_in(own, 4), (count // 2,), 0, 1 << 20) % (margin + 1)
    tallies = tallies.at[giver].add(-moved).at[taker].add(moved)
    labels = jnp.searchsorted(jnp.cumsum(tallies), jnp.arange(rows * top), side="right").astype(jnp.int32)
    grid = labels.reshape(top, rows).T
    grid = grid[jax.random.permutation(jax.random.fold_in(own, 1), rows)]
    turn = jax.random.randint(jax.random.fold_in(own, 2), (rows, 1), 0, top)
    return jnp.take_along_axis(grid, (jnp.arange(top)[None, :] + turn) % top, axis=1)


def portions_of(amount, total, reach, slope, full):
    loads = [(1 << 20) // math.isqrt(standing ** slope) + 1 for standing in range(1, amount + 1)]
    largest = reach if full else min(reach, max(-(-total // amount), total * loads[0] // sum(loads)))
    least = 1 if total - largest >= amount - 1 else 0
    holding, surplus = [largest] + [least] * (amount - 1), total - largest - least * (amount - 1)
    while surplus > 0:
        candidates = [i for i in range(1, amount) if holding[i] < largest] or [i for i in range(1, amount) if holding[i] < reach]
        whole, left = sum([loads[i] for i in candidates]), surplus
        for i in candidates:
            more = min(reach - holding[i], max(1, left * loads[i] // whole), surplus)
            holding[i] = holding[i] + more
            surplus = surplus - more
    return np.array(holding)


def gaussian(rng, dims, spread, reach, pieces=(), held_as=jnp.bfloat16):
    level = block_scale(rng, dims, pieces, -0.22, 0.18) if pieces else 1.0
    values = jax.random.normal(rng, dims, jnp.float32) * spread * level
    return jnp.minimum(jnp.maximum(values, -reach), reach).astype(held_as)


def setup_inputs(seed: int = 0, part: int = 0) -> dict:
    streams_of = jax.random.split(jax.random.key(seed), 15)
    part_keys = jax.random.split(jax.random.fold_in(streams_of[14], part), 15)
    queries = gaussian(part_keys[0], (QROWS, D), 1.0, 6.0, ((0, 16),))
    corpus = gaussian(part_keys[1], (CORPUS, BLK, D), 1.0, 6.0, ((0, 16),))
    block_owner_keys = jax.random.split(jax.random.fold_in(part_keys[2], 1), NBLK // NBLK)
    block_owner_turns = jax.random.permutation(jax.random.fold_in(part_keys[2], 3), NBLK // NBLK)
    block_owner = jax.vmap(lambda own, number: shared_out(jax.random.fold_in(part_keys[2], 2), own, number, NBLK, N_TENSOR, 1, CAP, 2))(block_owner_keys, block_owner_turns).reshape((NBLK, 1))
    slot_row = touch_ends(jax.random.randint(part_keys[3], (NBLK,), 0, CORP_DEV), jax.random.fold_in(part_keys[3], 1), 0, CORP_DEV - 1).astype(jnp.int32)
    segment = jnp.searchsorted(jnp.cumsum(ragged_sizes(part_keys[4], PAIRS, NBLK, MOSTB, 1)), jnp.arange(NBLK), side="right").astype(jnp.int32)
    query_weight = draw_query_weight(jax.random.fold_in(streams_of[14], 71), part)
    key_weight = draw_key_weight(jax.random.fold_in(streams_of[14], 71), part)
    value_weight = gaussian(streams_of[7], (HEADS * HDIM, D), D ** -0.5, 0.09375, ((0, 16),))
    out_weight = gaussian(streams_of[8], (HEADS * HDIM, D), (HEADS * HDIM) ** -0.5, 0.1875, ((0, 16),))
    gain_attn = jnp.clip(1.0 + 0.18 * jax.random.normal(streams_of[9], (D,), jnp.float32), 0.1, 1.9)
    gain_ffn = jnp.clip(1.0 + 0.18 * jax.random.normal(streams_of[10], (D,), jnp.float32), 0.1, 1.9)
    gate_weight = gaussian(streams_of[11], (FF, D), D ** -0.5, 0.09375, ((0, 16),))
    up_weight = gaussian(streams_of[12], (FF, D), D ** -0.5, 0.09375, ((0, 16),))
    down_weight = gaussian(streams_of[13], (FF, D), FF ** -0.5, 0.125, ((0, 16),))
    return dict(queries=queries, corpus=corpus, block_owner=block_owner, slot_row=slot_row, segment=segment, query_weight=query_weight, key_weight=key_weight, value_weight=value_weight, out_weight=out_weight, gain_attn=gain_attn, gain_ffn=gain_ffn, gate_weight=gate_weight, up_weight=up_weight, down_weight=down_weight)


def normed(stream, gain):
    values = stream.astype(jnp.float32)
    mean_square = lax.optimization_barrier(jnp.mean(values * values, axis=-1, keepdims=True))
    return (values * lax.rsqrt(mean_square + 1e-06) * gain).astype(jnp.bfloat16)

def by_rows(left, weight):
    return lax.dot_general(left, weight, (((1,), (1,)), ((), ())), preferred_element_type=jnp.float32)

def reference(queries, corpus, block_owner, slot_row, segment, query_weight, key_weight, value_weight, out_weight, gain_attn, gain_ffn, gate_weight, up_weight, down_weight):
    block_index = (block_owner[:, 0] * CORP_DEV + slot_row).astype(jnp.int32)
    fetched = jnp.take(corpus, block_index, axis=0).reshape(NBLK * BLK, D)
    stream_in = jnp.concatenate([queries, fetched], axis=0)
    pair_ids = jnp.concatenate([jnp.arange(QROWS, dtype=jnp.int32) // QLEN, jnp.repeat(segment, BLK).astype(jnp.int32)])
    same_pair = pair_ids[:, None] == pair_ids[None, :]
    normal_in = normed(stream_in, gain_attn)

    def heads_of(weight):
        projected = by_rows(normal_in, weight).astype(jnp.bfloat16)
        return projected.reshape(TOK, HEADS, HDIM).transpose(1, 0, 2)
    stacked = (heads_of(query_weight), heads_of(key_weight), heads_of(value_weight))

    def one_head(head_parts):
        scores = jnp.dot(head_parts[0], head_parts[1].T, preferred_element_type=jnp.float32) * HDIM ** (-0.5)
        scores = jnp.where(same_pair, scores, -1e+30)
        row_max = lax.optimization_barrier(jnp.max(scores, axis=-1, keepdims=True))
        weights = jnp.exp(scores - row_max)
        probability = (weights / lax.optimization_barrier(jnp.sum(weights, axis=-1, keepdims=True))).astype(jnp.bfloat16)
        return jnp.dot(probability, head_parts[2], preferred_element_type=jnp.float32).astype(jnp.bfloat16)
    context = lax.map(one_head, stacked).transpose(1, 0, 2).reshape(TOK, HEADS * HDIM)
    attended = jnp.dot(context, out_weight, preferred_element_type=jnp.float32)
    stream_mid = (stream_in.astype(jnp.float32) + attended).astype(jnp.bfloat16)
    normal_mid = normed(stream_mid, gain_ffn)
    gate_value = by_rows(normal_mid, gate_weight)
    up_value = by_rows(normal_mid, up_weight)
    hidden = (jax.nn.gelu(gate_value, approximate=True) * up_value).astype(jnp.bfloat16)
    ffn_result = jnp.dot(hidden, down_weight, preferred_element_type=jnp.float32)
    return (stream_mid.astype(jnp.float32) + ffn_result).astype(jnp.bfloat16)
```

```python
import jax
import jax.numpy as jnp
from jax import lax
from jax.sharding import PartitionSpec as P

HDIM = 64
QLEN = 32
BLK = 4
CAP = 3
AXIS = "tensor"


def by_rows(left, weight):
    return lax.dot_general(
        left, weight, (((1,), (1,)), ((), ())), preferred_element_type=jnp.float32
    )


def dot(left, right):
    return jnp.dot(left, right, preferred_element_type=jnp.float32)


def body(
    queries,
    corpus,
    block_owner,
    slot_row,
    segment,
    query_weight,
    key_weight,
    value_weight,
    out_weight,
    gain_attn,
    gain_ffn,
    gate_weight,
    up_weight,
    down_weight,
):
    devices = lax.axis_size(AXIS)
    me = lax.axis_index(AXIS)
    nz = devices // 4
    zi, yi, ci = me // 4, (me // 2) % 2, me % 2
    z_order = sorted(range(1, nz), key=lambda k: -min(k, nz - k))

    def along_z(value, k):
        return lax.ppermute(value, AXIS, [(i, (i + 4 * k) % devices) for i in range(devices)])

    def across_y(value):
        return lax.ppermute(value, AXIS, [(i, i ^ 2) for i in range(devices)])

    def across_core(value):
        return lax.ppermute(value, AXIS, [(i, i ^ 1) for i in range(devices)])

    def plane_gather(value):
        near = {0: value}
        for k in z_order:
            near[k] = along_z(value, k)
        far = {k: across_y(near[k]) for k in [0] + z_order}
        return [piece for k in range(nz) for piece in (near[k], far[k])]

    owners = block_owner[:, 0]
    blocks_total = owners.shape[0]
    features = queries.shape[1]
    half = features // 2
    query_rows = queries.shape[0]
    query_total = query_rows * devices
    tokens = query_total + blocks_total * BLK
    width = features // devices
    heads_rows = query_weight.shape[0]
    hidden_here = gate_weight.shape[0]
    rows_here = tokens // devices
    chunk_rows = -(-rows_here // 16) * 16

    positions = jnp.arange(blocks_total, dtype=jnp.int32)
    earlier = (owners[:, None] == owners[None, :]) & (positions[:, None] < positions[None, :])
    slot_rank = jnp.sum(earlier.astype(jnp.int32), axis=0)
    slot_ids = jnp.arange(CAP, dtype=jnp.int32)
    choose_slot = (owners[None, :] == me) & (slot_rank[None, :] == slot_ids[:, None])
    local_rows = jnp.sum(jnp.where(choose_slot, slot_row[None, :], 0), axis=1)
    outgoing = jnp.take(corpus, local_rows, axis=0).reshape(CAP * BLK, features)
    piece_rows = -(-(query_rows + CAP * BLK) // 8) * 8
    piece = jnp.concatenate(
        [
            queries,
            outgoing,
            jnp.zeros((piece_rows - query_rows - CAP * BLK, features), jnp.bfloat16),
        ],
        axis=0,
    )

    row_ids = jnp.arange(query_total, dtype=jnp.int32)
    token_owner = jnp.concatenate([row_ids // query_rows, jnp.repeat(owners, BLK)])
    token_row = jnp.concatenate(
        [
            row_ids % query_rows,
            (query_rows + slot_rank[:, None] * BLK + jnp.arange(BLK)[None, :]).reshape(-1),
        ]
    )
    token_place = (
        ((token_owner % 2) ^ ci) * (2 * nz)
        + ((zi - token_owner // 4) % nz) * 2
        + ((token_owner // 2) % 2 ^ yi)
    ) * piece_rows + token_row
    pair_ids = jnp.concatenate([row_ids // QLEN, jnp.repeat(segment, BLK)])
    same_pair = pair_ids[:, None] == pair_ids[None, :]

    projection = jnp.concatenate([query_weight, key_weight, value_weight], axis=0)
    projection_other = across_core(projection)
    own_half = ci * half
    other_half = (1 - ci) * half
    gate_up = jnp.concatenate([gate_weight, up_weight], axis=0)
    gate_up_mine = lax.dynamic_slice_in_dim(gate_up, own_half, half, 1)
    gate_up_other = across_core(lax.dynamic_slice_in_dim(gate_up, other_half, half, 1))
    down_other = across_core(down_weight)

    def out_block(dz, dy):
        chip = 2 * ((zi + dz) % nz) + (yi ^ dy)
        return jnp.concatenate(
            [
                lax.dynamic_slice_in_dim(out_weight, chip * width, width, 1),
                lax.dynamic_slice_in_dim(out_weight, half + chip * width, width, 1),
            ],
            axis=1,
        )

    out_far = across_y(jnp.concatenate([out_block(dz, 1) for dz in range(nz)], axis=0))
    out_pairs = [
        jnp.concatenate(
            [out_block(dz, 0), out_far[dz * heads_rows : (dz + 1) * heads_rows]], axis=0
        )
        for dz in range(nz)
    ]
    out_columns = jnp.concatenate(
        [out_pairs[0]] + [along_z(out_pairs[k], k) for k in range(1, nz)], axis=0
    )

    stream = jnp.concatenate(plane_gather(piece), axis=0)
    values = stream.astype(jnp.float32)
    mean_square = jnp.mean(values * values, axis=-1, keepdims=True)
    normal = (values * lax.rsqrt(mean_square + 1e-06) * gain_attn).astype(jnp.bfloat16)
    projected = by_rows(normal, projection).astype(jnp.bfloat16)
    projected_other = by_rows(normal, projection_other).astype(jnp.bfloat16)
    chip = 2 * zi + yi
    columns = lax.dynamic_slice_in_dim(stream, own_half + chip * width, width, 1)
    columns_other = lax.dynamic_slice_in_dim(stream, other_half + chip * width, width, 1)
    arrived = across_core(jnp.concatenate([projected_other, columns_other], axis=1))
    both = jnp.concatenate([jnp.concatenate([projected, columns], axis=1), arrived], axis=0)
    packed = jnp.take(both, token_place, axis=0)

    query, key, value = (packed[:, i * HDIM : (i + 1) * HDIM] for i in range(3))
    scores = by_rows(query, key) * HDIM ** (-0.5)
    scores = jnp.where(same_pair, scores, -1e30)
    weights = jnp.exp(scores - jnp.max(scores, axis=-1, keepdims=True))
    probability = (weights / jnp.sum(weights, axis=-1, keepdims=True)).astype(jnp.bfloat16)
    context = dot(probability, value).astype(jnp.bfloat16)

    contexts = plane_gather(
        jnp.concatenate([context[: tokens // 2], context[tokens // 2 :]], axis=1)
    )
    context_all = jnp.concatenate(
        [jnp.concatenate([x[:, :HDIM], x[:, HDIM:]], axis=0) for x in contexts], axis=1
    )
    attended = dot(context_all, out_columns)
    attended_mine = lax.dynamic_slice_in_dim(attended, ci * width, width, 1)
    attended_other = across_core(lax.dynamic_slice_in_dim(attended, (1 - ci) * width, width, 1))
    middle = (
        packed[:, 3 * HDIM :].astype(jnp.float32) + attended_mine + attended_other
    ).astype(jnp.bfloat16)

    blocks = jnp.stack(plane_gather(middle), axis=0)
    chips = jnp.arange(2 * nz, dtype=jnp.int32)
    middle_half = (
        jnp.take(blocks, ((zi - chips // 2) % nz) * 2 + (chips % 2 ^ yi), axis=0)
        .transpose(1, 0, 2)
        .reshape(tokens, half)
    )
    middle_values = middle_half.astype(jnp.float32)
    squares = jnp.sum(middle_values * middle_values, axis=-1, keepdims=True)
    gained = (middle_values * lax.dynamic_slice_in_dim(gain_ffn, own_half, half, 0)).astype(
        jnp.bfloat16
    )
    gate_up_value = by_rows(gained, gate_up_mine)
    gate_up_value_other = by_rows(gained, gate_up_other)

    def rows_of(core):
        chunks = jnp.arange(2 * nz, dtype=jnp.int32)
        device = ((zi + chunks // 2) % nz) * 4 + ((chunks % 2) ^ yi) * 2 + core
        row = jnp.minimum(jnp.arange(chunk_rows, dtype=jnp.int32), rows_here - 1)
        return (device[:, None] * rows_here + row[None, :]).reshape(-1)

    rows_mine, rows_other = rows_of(ci), rows_of(1 - ci)
    received = across_core(
        jnp.take(
            jnp.concatenate([gate_up_value_other, gate_up_value, squares], axis=1),
            rows_other,
            axis=0,
        )
    )
    summed = (
        jnp.take(
            jnp.concatenate([gate_up_value, gate_up_value_other, squares], axis=1),
            rows_mine,
            axis=0,
        )
        + received
    )
    summed = summed[:, :-1] * lax.rsqrt(summed[:, -1:] / features + 1e-06)
    parts = [summed[:, i * hidden_here : (i + 1) * hidden_here] for i in range(4)]
    gate_value = jnp.concatenate([parts[0], parts[2]], axis=1)
    up_value = jnp.concatenate([parts[1], parts[3]], axis=1)
    hidden = (jax.nn.gelu(gate_value, approximate=True) * up_value).astype(jnp.bfloat16)

    first_mine = me * rows_here
    kept = lax.dynamic_slice_in_dim(middle_half, first_mine, rows_here, 0)
    kept_other = across_core(
        lax.dynamic_slice_in_dim(middle_half, (me ^ 1) * rows_here, rows_here, 0)
    )
    kept_all = jnp.where(
        ci == 0,
        jnp.concatenate([kept, kept_other], axis=1),
        jnp.concatenate([kept_other, kept], axis=1),
    )

    result = dot(hidden, jnp.concatenate([down_weight, down_other], axis=0)).astype(jnp.bfloat16)
    result = result.reshape(nz, 2, chunk_rows, features)
    sums = {}
    for k in z_order + [0]:
        sums[k] = result[k, 0].astype(jnp.float32) + across_y(result[k, 1]).astype(jnp.float32)
    total = sums[0]
    for k in z_order:
        total = total + along_z(sums[k].astype(jnp.bfloat16), k).astype(jnp.float32)
    return (kept_all.astype(jnp.float32) + total[:rows_here]).astype(jnp.bfloat16)


def solution(mesh):
    placed = (
        P(("groups", "tensor"), None),
        P(("groups", "tensor"), None, None),
        P("groups", None),
        P("groups"),
        P("groups"),
        P("tensor", None),
        P("tensor", None),
        P("tensor", None),
        P("tensor", None),
        P(),
        P(),
        P("tensor", None),
        P("tensor", None),
        P("tensor", None),
    )
    return jax.shard_map(
        body, mesh=mesh, in_specs=placed, out_specs=P(("groups", "tensor"), None), check_vma=False
    )
```

```python
import functools

import jax
import jax.numpy as jnp
from jax import lax
from jax.experimental import pallas as pl
from jax.experimental.pallas import tpu as pltpu
from jax.sharding import PartitionSpec as P

HDIM = 64
QLEN = 32
BLK = 4
CAP = 3
AXIS = "tensor"
VMEM_LIMIT = 60 * 1024 * 1024


def by_rows(left, weight):
    return lax.dot_general(
        left, weight, (((1,), (1,)), ((), ())), preferred_element_type=jnp.float32
    )


def dot(left, right):
    return jnp.dot(left, right, preferred_element_type=jnp.float32)


def place():
    me = lax.axis_index(AXIS)
    return me, me // 4, (me // 2) % 2, me % 2


def kernel_call(kernel, out_shape, in_specs, scratch=(), name=None):
    return pl.pallas_call(
        kernel,
        out_shape=out_shape,
        in_specs=in_specs,
        out_specs=jax.tree.map(lambda _: pl.BlockSpec(memory_space=pltpu.VMEM), out_shape),
        scratch_shapes=scratch,
        compiler_params=pltpu.CompilerParams(vmem_limit_bytes=VMEM_LIMIT),
        name=name,
    )


SMEM = pl.BlockSpec(memory_space=pltpu.SMEM)
VMEM = pl.BlockSpec(memory_space=pltpu.VMEM)
ANY = pl.BlockSpec(memory_space=pl.ANY)


def piece_layout(rows):
    full, rest = divmod(rows, 8)
    if 0 < rest <= 4:
        return full, True
    return full + (rest > 0), False


def fetch_kernel(owner_ref, row_ref, corpus_ref, query_ref, piece_ref, blocks, rows, sems):
    me = place()[0]
    features = query_ref.shape[1]
    query_rows = query_ref.shape[0]

    def look(b, carry):
        count, found = carry[0], carry[1:]
        mine = owner_ref[b] == me
        found = tuple(
            jnp.where(mine & (count == k), row_ref[b], found[k]) for k in range(CAP)
        )
        return (count + mine.astype(jnp.int32),) + found

    zero = jnp.int32(0)
    found = lax.fori_loop(0, owner_ref.shape[0], look, (zero,) * (CAP + 1))[1:]
    copies = [
        pltpu.make_async_copy(corpus_ref.at[found[k]], blocks.at[k], sems.at[k])
        for k in range(CAP)
    ]
    for copy in copies:
        copy.start()
    total = query_rows + CAP * BLK
    full, halved = piece_layout(total)
    rows[0:query_rows, :] = query_ref[...].astype(jnp.float32)
    for k in range(CAP):
        copies[k].wait()
        first = query_rows + k * BLK
        rows[first : first + BLK, :] = blocks[k].astype(jnp.float32)
    if not halved and total < full * 8:
        rows[total : full * 8, :] = jnp.zeros((full * 8 - total, features), jnp.float32)
    for i in range(full):
        piece_ref[:, i * features : (i + 1) * features] = rows[i * 8 : i * 8 + 8, :].astype(
            jnp.bfloat16
        )
    if halved:
        half = features // 2
        last = rows[full * 8 : full * 8 + 4, :]
        if total % 8 < 4:
            last = jnp.where(
                lax.broadcasted_iota(jnp.int32, last.shape, 0) < total % 8, last, 0.0
            )
        piece_ref[:, full * features :] = jnp.concatenate(
            [last[:, :half], last[:, half:]], axis=0
        ).astype(jnp.bfloat16)


def columns_at(ref, start, width):
    if width % 128 == 0:
        return ref[:, pl.ds(pl.multiple_of(start, 128), width)].astype(jnp.float32)
    base = pl.multiple_of(start // 128 * 128, 128)
    window = ref[:, pl.ds(base, 128)].astype(jnp.float32)
    return pltpu.roll(window, (128 - start % 128) % 128, 1)[:, :width]


def projection_kernel(piece_rows, *refs):
    count = len(refs) - 10
    pieces, rest = refs[:count], refs[count:]
    gain_ref, mine, other, out_ref, out_other_ref, normal = (
        rest[0],
        rest[1:4],
        rest[4:7],
        rest[7],
        rest[8],
        rest[9],
    )
    _, zi, yi, ci = place()
    features = gain_ref.shape[1]
    half = features // 2
    full, halved = piece_layout(piece_rows)
    width = features // lax.axis_size(AXIS)
    chip = 2 * zi + yi
    gain = gain_ref[...]
    spot = 256
    own_column = ci * half + chip * width
    other_column = (1 - ci) * half + chip * width

    def scaled(values, squares):
        return values * lax.rsqrt(squares / features + 1e-06)

    def put(row, groups):
        normal[row : row + 16, :] = jnp.concatenate(groups, axis=0).astype(jnp.bfloat16)

    chunks = [(p, i) for p in range(count) for i in range(full)]
    for first in range(0, len(chunks), 2):
        groups, own, away = [], [], []
        for p, i in chunks[first : first + 2]:
            values = pieces[p][:, i * features : (i + 1) * features].astype(jnp.float32)
            squares = jnp.sum(values * values, axis=-1, keepdims=True)
            groups.append(scaled(values, squares) * gain)
            own.append(columns_at(pieces[p], i * features + own_column, width))
            away.append(columns_at(pieces[p], i * features + other_column, width))
        row = first * 8
        put(row, groups)
        out_ref[row : row + 16, spot : spot + width] = jnp.concatenate(own, axis=0).astype(
            jnp.bfloat16
        )
        out_other_ref[row : row + 16, spot : spot + width] = jnp.concatenate(
            away, axis=0
        ).astype(jnp.bfloat16)
    if halved:
        for first in range(0, count, 4):
            groups, own, away = [], [], []
            for p in range(first, first + 4, 2):
                a, b = (
                    pieces[q][:, full * features :].astype(jnp.float32) for q in (p, p + 1)
                )
                low = jnp.concatenate([a[0:4], b[0:4]], axis=0)
                high = jnp.concatenate([a[4:8], b[4:8]], axis=0)
                squares = jnp.sum(low * low, axis=-1, keepdims=True) + jnp.sum(
                    high * high, axis=-1, keepdims=True
                )
                groups.append(
                    jnp.concatenate([scaled(low, squares), scaled(high, squares)], axis=1)
                    * gain
                )
                a, b = (
                    columns_at(pieces[q], full * features + chip * width, width)
                    for q in (p, p + 1)
                )
                low = jnp.concatenate([a[0:4], b[0:4]], axis=0)
                high = jnp.concatenate([a[4:8], b[4:8]], axis=0)
                own.append(jnp.where(ci == 0, low, high))
                away.append(jnp.where(ci == 0, high, low))
            row = len(chunks) * 8 + first * 4
            put(row, groups)
            out_ref[row : row + 16, spot : spot + width] = jnp.concatenate(
                own, axis=0
            ).astype(jnp.bfloat16)
            out_other_ref[row : row + 16, spot : spot + width] = jnp.concatenate(
                away, axis=0
            ).astype(jnp.bfloat16)
    rows = normal[...]
    for target, weights in ((out_other_ref, other), (out_ref, mine)):
        value = jnp.concatenate([by_rows(rows, w[...]) for w in weights], axis=1)
        target[:, 0 : value.shape[1]] = value.astype(jnp.bfloat16)


def attention_kernel(query_rows, width, owner_ref, segment_ref, own_ref, away_ref, ctx_ref, col_ref):
    _, zi, yi, ci = place()
    nz = lax.axis_size(AXIS) // 4
    query_total = query_rows * 4 * nz
    blocks_total = owner_ref.shape[0]
    tokens = query_total + blocks_total * BLK
    piece_rows = query_rows + CAP * BLK
    full, halved = piece_layout(piece_rows)
    plane_rows = own_ref.shape[0]

    def lay(shape, axis):
        token = lax.broadcasted_iota(jnp.int32, shape, axis)
        block = (token - query_total) // BLK
        is_query = token < query_total
        owner = jnp.where(is_query, token // query_rows, 0)
        pair = jnp.where(is_query, token // QLEN, 0)

        def fill(b, carry):
            here = (block == b) & (token >= query_total)
            return (
                jnp.where(here, owner_ref[b], carry[0]),
                jnp.where(here, segment_ref[b], carry[1]),
            )

        owner, pair = lax.fori_loop(0, blocks_total, fill, (owner, pair))
        return token, block, owner, pair

    token, block, owner, pair = lay((tokens, 1), 0)
    token_row, block_row, owner_row, pair_row = lay((1, tokens), 1)
    ahead = (
        (owner == owner_row)
        & (block_row < block)
        & (token_row >= query_total)
        & (token >= query_total)
    )
    before = jnp.sum(ahead.astype(jnp.float32), axis=-1, keepdims=True).astype(jnp.int32)
    local = jnp.where(
        token < query_total,
        token % query_rows,
        query_rows + before + (token - query_total) % BLK,
    )
    source = ((zi - owner // 4 + 4 * nz) % nz) * 2 + (((owner // 2) % 2) ^ yi)
    pieces = 2 * nz
    spot = source * (full * 8) + local
    if halved:
        spot = jnp.where(
            local < full * 8, spot, pieces * full * 8 + source * 4 + local - full * 8
        )
    spot = spot + ((owner % 2) ^ ci) * plane_rows
    lanes = lax.broadcasted_iota(jnp.int32, (tokens, plane_rows), 1)
    pick_own = (lanes == spot).astype(jnp.bfloat16)
    pick_away = (lanes == spot - plane_rows).astype(jnp.bfloat16)
    packed = dot(pick_own, own_ref[...]) + dot(pick_away, away_ref[...])
    col_ref[...] = packed[:, 256 : 256 + width].astype(jnp.bfloat16)
    query, key, value = (
        packed[:, i * HDIM : (i + 1) * HDIM].astype(jnp.bfloat16) for i in range(3)
    )
    scores = by_rows(query, key) * HDIM ** (-0.5)
    scores = jnp.where(pair == pair_row, scores, -1e30)
    weights = jnp.exp(scores - jnp.max(scores, axis=-1, keepdims=True))
    probability = (weights / jnp.sum(weights, axis=-1, keepdims=True)).astype(jnp.bfloat16)
    context = dot(probability, value)
    ctx_ref[...] = jnp.concatenate(
        [context[: tokens // 2], context[tokens // 2 :]], axis=1
    ).astype(jnp.bfloat16)


def gate_kernel(rows_here, chunk_rows, *refs):
    count = len(refs) - 11
    pieces = refs[:count]
    (
        gain_ref,
        gate_ref,
        up_ref,
        gate_other_ref,
        up_other_ref,
        keep_ref,
        send_ref,
        kept_ref,
        kept_send_ref,
        order_ref,
        rows_ref,
    ) = refs[count:]
    _, zi, yi, ci = place()
    nz = lax.axis_size(AXIS) // 4
    tokens, width = pieces[0].shape
    half = 2 * nz * width
    total = order_ref.shape[0]
    slots = total // 2
    row = lax.broadcasted_iota(jnp.int32, (total, 1), 0)
    core = jnp.where(row < slots, ci, 1 - ci)
    chunk = (row % slots) // chunk_rows
    device = ((zi + chunk // 2) % nz) * 4 + ((chunk % 2) ^ yi) * 2 + core
    wanted = device * rows_here + jnp.minimum(row % chunk_rows, rows_here - 1)
    lanes = lax.broadcasted_iota(jnp.int32, (total, tokens), 1)
    order_ref[...] = (lanes == wanted).astype(jnp.bfloat16)
    squares = jnp.zeros((total, 1), jnp.float32)
    for dz in range(nz):
        near, far = pieces[2 * dz][...], pieces[2 * dz + 1][...]
        pair = jnp.where(
            yi == 0,
            jnp.concatenate([near, far], axis=1),
            jnp.concatenate([far, near], axis=1),
        )
        start = pl.multiple_of(((zi - dz + nz) % nz) * (2 * width), 128)
        values = dot(order_ref[...], pair)
        squares = squares + jnp.sum(values * values, axis=-1, keepdims=True)
        kept_ref[:, pl.ds(start, 2 * width)] = values[0:chunk_rows].astype(jnp.bfloat16)
        kept_send_ref[:, pl.ds(start, 2 * width)] = values[slots : slots + chunk_rows].astype(
            jnp.bfloat16
        )
        gain = gain_ref[:, pl.ds(pl.multiple_of(ci * half + start, 128), 2 * width)]
        rows_ref[:, pl.ds(start, 2 * width)] = (values * gain).astype(jnp.bfloat16)
    mine = pl.ds(pl.multiple_of(ci * half, 128), half)
    rows = rows_ref[...]
    units = gate_ref.shape[0]
    gate = by_rows(rows, gate_ref[:, mine])
    up = by_rows(rows, up_ref[:, mine])
    gate_other = by_rows(rows, gate_other_ref[...])
    up_other = by_rows(rows, up_other_ref[...])
    wide = keep_ref.shape[1] - 4 * units
    spread = jnp.broadcast_to(squares, (total, wide))
    keep_ref[...] = jnp.concatenate(
        [gate[:slots], gate_other[:slots], up[:slots], up_other[:slots], spread[:slots]], axis=1
    )
    send_ref[...] = jnp.concatenate(
        [gate_other[slots:], gate[slots:], up_other[slots:], up[slots:], spread[slots:]], axis=1
    )


def hidden_kernel(features, keep_ref, came_ref, down_ref, down_other_ref, *refs):
    chunk_rows = refs[0].shape[0]
    hidden_ref = refs[-1]
    units = down_ref.shape[0]
    summed = keep_ref[...] + came_ref[...]
    scale = lax.rsqrt(summed[:, 4 * units : 4 * units + 1] / features + 1e-06)
    gate = summed[:, 0 : 2 * units] * scale
    up = summed[:, 2 * units : 4 * units] * scale
    hidden = (jax.nn.gelu(gate, approximate=True) * up).astype(jnp.bfloat16)
    hidden_ref[...] = hidden
    far = jnp.concatenate(
        [
            hidden[(2 * dz + 1) * chunk_rows : (2 * dz + 2) * chunk_rows]
            for dz in range(len(refs) - 1)
        ],
        axis=0,
    )
    result = dot(far[:, :units], down_ref[...]) + dot(far[:, units:], down_other_ref[...])
    for dz in range(len(refs) - 1):
        refs[dz][...] = result[dz * chunk_rows : (dz + 1) * chunk_rows].astype(jnp.bfloat16)


def down_kernel(chunk_rows, hidden_ref, down_ref, down_other_ref, out_ref):
    units = down_ref.shape[0]
    hidden = hidden_ref[...]
    near = jnp.concatenate(
        [
            hidden[2 * dz * chunk_rows : (2 * dz + 1) * chunk_rows]
            for dz in range(hidden.shape[0] // chunk_rows // 2)
        ],
        axis=0,
    )
    out_ref[...] = dot(near[:, :units], down_ref[...]) + dot(near[:, units:], down_other_ref[...])


def add_kernel(first_row, near_ref, far_ref, out_ref):
    rows = out_ref.shape[0]
    out_ref[...] = (
        near_ref[first_row : first_row + rows, :] + far_ref[...].astype(jnp.float32)
    ).astype(jnp.bfloat16)


def last_kernel(count, *refs):
    near_ref, far_ref = refs[0], refs[1]
    arrived = refs[2 : 2 + count]
    kept_ref, kept_other_ref, out_ref = refs[2 + count :]
    ci = place()[3]
    rows = out_ref.shape[0]
    half = kept_ref.shape[1]
    kept, other = kept_ref[...].astype(jnp.float32), kept_other_ref[...].astype(jnp.float32)
    total = near_ref[0 : far_ref.shape[0], :] + far_ref[...].astype(jnp.float32)
    for ref in arrived:
        total = total + ref[...].astype(jnp.float32)
    low, high = jnp.where(ci == 0, kept, other), jnp.where(ci == 0, other, kept)
    out_ref[:, :half] = (low + total[:, :half])[:rows].astype(jnp.bfloat16)
    out_ref[:, half:] = (high + total[:, half:])[:rows].astype(jnp.bfloat16)


def body(
    queries,
    corpus,
    block_owner,
    slot_row,
    segment,
    query_weight,
    key_weight,
    value_weight,
    out_weight,
    gain_attn,
    gain_ffn,
    gate_weight,
    up_weight,
    down_weight,
):
    devices = lax.axis_size(AXIS)
    nz = devices // 4
    _, zi, yi, ci = place()
    z_order = sorted(range(1, nz), key=lambda k: -min(k, nz - k))

    def along_z(value, k):
        return lax.ppermute(value, AXIS, [(i, (i + 4 * k) % devices) for i in range(devices)])

    def across_y(value):
        return lax.ppermute(value, AXIS, [(i, i ^ 2) for i in range(devices)])

    def across_core(value):
        return lax.ppermute(value, AXIS, [(i, i ^ 1) for i in range(devices)])

    def plane_gather(value):
        near = {0: value}
        for k in z_order:
            near[k] = along_z(value, k)
        far = {k: across_y(near[k]) for k in [0] + z_order}
        return [piece for k in range(nz) for piece in (near[k], far[k])]

    owners = block_owner[:, 0]
    features = queries.shape[1]
    half = features // 2
    query_rows = queries.shape[0]
    tokens = query_rows * devices + owners.shape[0] * BLK
    width = features // devices
    heads_rows = query_weight.shape[0]
    units = gate_weight.shape[0]
    rows_here = tokens // devices
    chunk_rows = -(-rows_here // 16) * 16
    bf16, f32 = jnp.bfloat16, jnp.float32
    shape = jax.ShapeDtypeStruct

    full, halved = piece_layout(query_rows + CAP * BLK)
    piece = kernel_call(
        fetch_kernel,
        shape((8, full * features + halved * half), bf16),
        [SMEM, SMEM, ANY, VMEM],
        [
            pltpu.VMEM((CAP, BLK, features), bf16),
            pltpu.VMEM((full * 8 + halved * 8, features), f32),
            pltpu.SemaphoreType.DMA((CAP,)),
        ],
        name="fetch",
    )(owners, slot_row, corpus, queries)

    projections = [query_weight, key_weight, value_weight]
    projections_other = [across_core(w) for w in projections]
    other_half = (1 - ci) * half
    gate_other = across_core(lax.dynamic_slice_in_dim(gate_weight, other_half, half, 1))
    up_other = across_core(lax.dynamic_slice_in_dim(up_weight, other_half, half, 1))
    down_other = across_core(down_weight)

    def out_block(dz, dy):
        chip = 2 * ((zi + dz) % nz) + (yi ^ dy)
        return jnp.concatenate(
            [
                lax.dynamic_slice_in_dim(out_weight, chip * width, width, 1),
                lax.dynamic_slice_in_dim(out_weight, half + chip * width, width, 1),
            ],
            axis=1,
        )

    out_far = across_y(jnp.concatenate([out_block(dz, 1) for dz in range(nz)], axis=0))
    out_pairs = [
        jnp.concatenate(
            [out_block(dz, 0), out_far[dz * heads_rows : (dz + 1) * heads_rows]], axis=0
        )
        for dz in range(nz)
    ]
    out_columns = jnp.concatenate(
        [out_pairs[0]] + [along_z(out_pairs[k], k) for k in range(1, nz)], axis=0
    )

    plane_rows = 2 * nz * (full * 8 + halved * 4)
    wide = 256 + -(-width // 128) * 128
    own, away = kernel_call(
        functools.partial(projection_kernel, query_rows + CAP * BLK),
        (shape((plane_rows, wide), bf16), shape((plane_rows, wide), bf16)),
        [VMEM] * (2 * nz + 7),
        [pltpu.VMEM((plane_rows, features), bf16)],
        name="project",
    )(*plane_gather(piece), gain_attn[None, :], *projections, *projections_other)

    context, columns = kernel_call(
        functools.partial(attention_kernel, query_rows, width),
        (shape((tokens // 2, 2 * HDIM), bf16), shape((tokens, width), bf16)),
        [SMEM, SMEM, VMEM, VMEM],
        name="attend",
    )(owners, segment, own, across_core(away))

    contexts = plane_gather(context)
    context_all = jnp.concatenate(
        [jnp.concatenate([x[:, :HDIM], x[:, HDIM:]], axis=0) for x in contexts], axis=1
    )
    attended = dot(context_all, out_columns)
    attended_mine = lax.dynamic_slice_in_dim(attended, ci * width, width, 1)
    attended_other = across_core(lax.dynamic_slice_in_dim(attended, (1 - ci) * width, width, 1))
    middle = (columns.astype(f32) + attended_mine + attended_other).astype(bf16)

    slots = 2 * nz * chunk_rows
    lanes = -(-(4 * units + 1) // 128) * 128
    keep, send, kept, kept_send = kernel_call(
        functools.partial(gate_kernel, rows_here, chunk_rows),
        (
            shape((slots, lanes), f32),
            shape((slots, lanes), f32),
            shape((chunk_rows, half), bf16),
            shape((chunk_rows, half), bf16),
        ),
        [VMEM] * (2 * nz + 5),
        [pltpu.VMEM((2 * slots, tokens), bf16), pltpu.VMEM((2 * slots, half), bf16)],
        name="gate_up",
    )(*plane_gather(middle), gain_ffn[None, :], gate_weight, up_weight, gate_other, up_other)
    came = across_core(send)
    kept_other = across_core(kept_send)

    chunk = shape((chunk_rows, features), bf16)
    *far, hidden = kernel_call(
        functools.partial(hidden_kernel, features),
        (chunk,) * nz + (shape((slots, 2 * units), bf16),),
        [VMEM] * 4,
        name="hidden",
    )(keep, came, down_weight, down_other)
    moved = {k: across_y(far[k]) for k in z_order + [0]}
    near = kernel_call(
        functools.partial(down_kernel, chunk_rows),
        shape((nz * chunk_rows, features), f32),
        [VMEM] * 3,
        name="down",
    )(hidden, down_weight, down_other)
    arrived = []
    for k in z_order:
        part = kernel_call(
            functools.partial(add_kernel, k * chunk_rows), chunk, [VMEM, VMEM], name="add"
        )(near, moved[k])
        arrived.append(along_z(part, k))
    return kernel_call(
        functools.partial(last_kernel, len(arrived)),
        shape((rows_here, features), bf16),
        [VMEM] * (len(arrived) + 4),
        name="last",
    )(near, moved[0], *arrived, kept, kept_other)


def solution(mesh):
    placed = (
        P(("groups", "tensor"), None),
        P(("groups", "tensor"), None, None),
        P("groups", None),
        P("groups"),
        P("groups"),
        P("tensor", None),
        P("tensor", None),
        P("tensor", None),
        P("tensor", None),
        P(),
        P(),
        P("tensor", None),
        P("tensor", None),
        P("tensor", None),
    )
    return jax.shard_map(
        body, mesh=mesh, in_specs=placed, out_specs=P(("groups", "tensor"), None), check_vma=False
    )
```

```python
import functools

import jax
import jax.numpy as jnp
from jax import lax
from jax.experimental import pallas as pl
from jax.experimental.pallas import tpu as pltpu
from jax.sharding import PartitionSpec as P

HDIM = 64
QLEN = 32
BLK = 4
CAP = 3
AXIS = "tensor"
VMEM_LIMIT = 28 * 1024 * 1024


def by_rows(left, weight):
    return lax.dot_general(
        left, weight, (((1,), (1,)), ((), ())), preferred_element_type=jnp.float32
    )


def dot(left, right):
    return jnp.dot(left, right, preferred_element_type=jnp.float32)


def place():
    me = lax.axis_index(AXIS)
    return me, me // 4, (me // 2) % 2, me % 2


def kernel_call(kernel, out_shape, in_specs, scratch=(), name=None):
    return pl.pallas_call(
        kernel,
        out_shape=out_shape,
        in_specs=in_specs,
        out_specs=jax.tree.map(lambda _: pl.BlockSpec(memory_space=pltpu.VMEM), out_shape),
        scratch_shapes=scratch,
        compiler_params=pltpu.CompilerParams(vmem_limit_bytes=VMEM_LIMIT),
        name=name,
    )


SMEM = pl.BlockSpec(memory_space=pltpu.SMEM)
VMEM = pl.BlockSpec(memory_space=pltpu.VMEM)
ANY = pl.BlockSpec(memory_space=pl.ANY)


def piece_layout(rows):
    full, rest = divmod(rows, 8)
    if 0 < rest <= 4:
        return full, True
    return full + (rest > 0), False


def fetch_kernel(owner_ref, row_ref, corpus_ref, query_ref, piece_ref, blocks, rows, sems):
    me = place()[0]
    features = query_ref.shape[1]
    query_rows = query_ref.shape[0]

    def look(b, carry):
        count, found = carry[0], carry[1:]
        mine = owner_ref[b] == me
        found = tuple(
            jnp.where(mine & (count == k), row_ref[b], found[k]) for k in range(CAP)
        )
        return (count + mine.astype(jnp.int32),) + found

    zero = jnp.int32(0)
    found = lax.fori_loop(0, owner_ref.shape[0], look, (zero,) * (CAP + 1))[1:]
    copies = [
        pltpu.make_async_copy(corpus_ref.at[found[k]], blocks.at[k], sems.at[k])
        for k in range(CAP)
    ]
    for copy in copies:
        copy.start()
    total = query_rows + CAP * BLK
    full, halved = piece_layout(total)
    rows[0:query_rows, :] = query_ref[...].astype(jnp.float32)
    for k in range(CAP):
        copies[k].wait()
        first = query_rows + k * BLK
        rows[first : first + BLK, :] = blocks[k].astype(jnp.float32)
    if not halved and total < full * 8:
        rows[total : full * 8, :] = jnp.zeros((full * 8 - total, features), jnp.float32)
    for i in range(full):
        piece_ref[:, i * features : (i + 1) * features] = rows[i * 8 : i * 8 + 8, :].astype(
            jnp.bfloat16
        )
    if halved:
        half = features // 2
        last = rows[full * 8 : full * 8 + 4, :]
        if total % 8 < 4:
            last = jnp.where(
                lax.broadcasted_iota(jnp.int32, last.shape, 0) < total % 8, last, 0.0
            )
        piece_ref[:, full * features :] = jnp.concatenate(
            [last[:, :half], last[:, half:]], axis=0
        ).astype(jnp.bfloat16)


def columns_at(ref, start, width):
    if width % 128 == 0:
        return ref[:, pl.ds(pl.multiple_of(start, 128), width)].astype(jnp.float32)
    base = pl.multiple_of(start // 128 * 128, 128)
    window = ref[:, pl.ds(base, 128)].astype(jnp.float32)
    return pltpu.roll(window, (128 - start % 128) % 128, 1)[:, :width]


def slab_kernel(weight_ref, *out_refs):
    zi = place()[1]
    features = weight_ref.shape[1]
    wide = out_refs[0].shape[1] // 2
    for d, out_ref in enumerate(out_refs):
        for core in range(2):
            start = pl.multiple_of(core * (features // 2) + (zi ^ d) * wide, 128)
            out_ref[:, core * wide : (core + 1) * wide] = weight_ref[:, pl.ds(start, wide)]


def half_kernel(gate_ref, up_ref, gate_out_ref, up_out_ref):
    half = gate_out_ref.shape[1]
    other = pl.ds(pl.multiple_of((1 - place()[3]) * half, 128), half)
    gate_out_ref[...] = gate_ref[:, other]
    up_out_ref[...] = up_ref[:, other]


def strip_kernel(*refs):
    slabs, (keep_ref, send_ref) = refs[:-2], refs[-2:]
    yi = place()[2]
    rows, wide = slabs[0].shape
    width = wide // 4
    for d, slab in enumerate(slabs):
        parts = [slab[:, i * width : (i + 1) * width] for i in range(4)]
        low = jnp.concatenate([parts[0], parts[2]], axis=1)
        high = jnp.concatenate([parts[1], parts[3]], axis=1)
        keep_ref[d * rows : (d + 1) * rows, :] = jnp.where(yi == 0, low, high)
        send_ref[d * rows : (d + 1) * rows, :] = jnp.where(yi == 0, high, low)


def out_kernel(*refs):
    contexts, (near_ref, far_ref, mine_ref, other_ref) = refs[:-4], refs[-4:]
    width = mine_ref.shape[1]
    ci = place()[3]
    half = contexts[0].shape[0] // 2

    def heads(first):
        values = [ref[first : first + half, :] for ref in contexts]
        return jnp.concatenate(
            [
                jnp.concatenate([v[:, :HDIM] for v in values], axis=1),
                jnp.concatenate([v[:, HDIM:] for v in values], axis=1),
            ],
            axis=0,
        )

    attended = dot(heads(0), near_ref[...]) + dot(heads(half), far_ref[...])
    low, high = attended[:, :width], attended[:, width:]
    mine_ref[...] = jnp.where(ci == 0, low, high)
    other_ref[...] = jnp.where(ci == 0, high, low)


def projection_kernel(piece_rows, *refs):
    count = len(refs) - 10
    pieces, rest = refs[:count], refs[count:]
    gain_ref, mine, other, out_ref, out_other_ref, normal = (
        rest[0],
        rest[1:4],
        rest[4:7],
        rest[7],
        rest[8],
        rest[9],
    )
    _, zi, yi, ci = place()
    features = gain_ref.shape[1]
    half = features // 2
    full, halved = piece_layout(piece_rows)
    width = features // lax.axis_size(AXIS)
    chip = 2 * zi + yi
    gain = gain_ref[...]
    spot = 256
    own_column = ci * half + chip * width
    other_column = (1 - ci) * half + chip * width

    def scaled(values, squares):
        return values * lax.rsqrt(squares / features + 1e-06)

    def put(row, groups):
        normal[row : row + 16, :] = jnp.concatenate(groups, axis=0).astype(jnp.bfloat16)

    chunks = [(p, i) for p in range(count) for i in range(full)]
    for first in range(0, len(chunks), 2):
        groups, own, away = [], [], []
        for p, i in chunks[first : first + 2]:
            values = pieces[p][:, i * features : (i + 1) * features].astype(jnp.float32)
            squares = jnp.sum(values * values, axis=-1, keepdims=True)
            groups.append(scaled(values, squares) * gain)
            own.append(columns_at(pieces[p], i * features + own_column, width))
            away.append(columns_at(pieces[p], i * features + other_column, width))
        row = first * 8
        put(row, groups)
        out_ref[row : row + 16, spot : spot + width] = jnp.concatenate(own, axis=0).astype(
            jnp.bfloat16
        )
        out_other_ref[row : row + 16, spot : spot + width] = jnp.concatenate(
            away, axis=0
        ).astype(jnp.bfloat16)
    if halved:
        for first in range(0, count, 4):
            groups, own, away = [], [], []
            for p in range(first, first + 4, 2):
                a, b = (
                    pieces[q][:, full * features :].astype(jnp.float32) for q in (p, p + 1)
                )
                low = jnp.concatenate([a[0:4], b[0:4]], axis=0)
                high = jnp.concatenate([a[4:8], b[4:8]], axis=0)
                squares = jnp.sum(low * low, axis=-1, keepdims=True) + jnp.sum(
                    high * high, axis=-1, keepdims=True
                )
                groups.append(
                    jnp.concatenate([scaled(low, squares), scaled(high, squares)], axis=1)
                    * gain
                )
                a, b = (
                    columns_at(pieces[q], full * features + chip * width, width)
                    for q in (p, p + 1)
                )
                low = jnp.concatenate([a[0:4], b[0:4]], axis=0)
                high = jnp.concatenate([a[4:8], b[4:8]], axis=0)
                own.append(jnp.where(ci == 0, low, high))
                away.append(jnp.where(ci == 0, high, low))
            row = len(chunks) * 8 + first * 4
            put(row, groups)
            out_ref[row : row + 16, spot : spot + width] = jnp.concatenate(
                own, axis=0
            ).astype(jnp.bfloat16)
            out_other_ref[row : row + 16, spot : spot + width] = jnp.concatenate(
                away, axis=0
            ).astype(jnp.bfloat16)
    rows = normal[...]
    for target, weights in ((out_other_ref, other), (out_ref, mine)):
        value = jnp.concatenate([by_rows(rows, w[...]) for w in weights], axis=1)
        target[:, 0 : value.shape[1]] = value.astype(jnp.bfloat16)


def attention_kernel(query_rows, width, owner_ref, segment_ref, own_ref, away_ref, ctx_ref, col_ref):
    _, zi, yi, ci = place()
    nz = lax.axis_size(AXIS) // 4
    query_total = query_rows * 4 * nz
    blocks_total = owner_ref.shape[0]
    tokens = query_total + blocks_total * BLK
    piece_rows = query_rows + CAP * BLK
    full, halved = piece_layout(piece_rows)
    plane_rows = own_ref.shape[0]

    def lay(shape, axis):
        token = lax.broadcasted_iota(jnp.int32, shape, axis)
        block = (token - query_total) // BLK
        is_query = token < query_total
        owner = jnp.where(is_query, token // query_rows, 0)
        pair = jnp.where(is_query, token // QLEN, 0)

        def fill(b, carry):
            here = (block == b) & (token >= query_total)
            return (
                jnp.where(here, owner_ref[b], carry[0]),
                jnp.where(here, segment_ref[b], carry[1]),
            )

        owner, pair = lax.fori_loop(0, blocks_total, fill, (owner, pair))
        return token, block, owner, pair

    token, block, owner, pair = lay((tokens, 1), 0)
    token_row, block_row, owner_row, pair_row = lay((1, tokens), 1)
    ahead = (
        (owner == owner_row)
        & (block_row < block)
        & (token_row >= query_total)
        & (token >= query_total)
    )
    before = jnp.sum(ahead.astype(jnp.float32), axis=-1, keepdims=True).astype(jnp.int32)
    local = jnp.where(
        token < query_total,
        token % query_rows,
        query_rows + before + (token - query_total) % BLK,
    )
    source = (zi ^ (owner // 4)) * 2 + (((owner // 2) % 2) ^ yi)
    pieces = 2 * nz
    spot = source * (full * 8) + local
    if halved:
        spot = jnp.where(
            local < full * 8, spot, pieces * full * 8 + source * 4 + local - full * 8
        )
    spot = spot + ((owner % 2) ^ ci) * plane_rows
    lanes = lax.broadcasted_iota(jnp.int32, (tokens, plane_rows), 1)
    pick_own = (lanes == spot).astype(jnp.bfloat16)
    pick_away = (lanes == spot - plane_rows).astype(jnp.bfloat16)
    packed = dot(pick_own, own_ref[...]) + dot(pick_away, away_ref[...])
    col_ref[...] = packed[:, 256 : 256 + width].astype(jnp.bfloat16)
    query, key, value = (
        packed[:, i * HDIM : (i + 1) * HDIM].astype(jnp.bfloat16) for i in range(3)
    )
    scores = by_rows(query, key) * HDIM ** (-0.5)
    scores = jnp.where(pair == pair_row, scores, -1e30)
    weights = jnp.exp(scores - jnp.max(scores, axis=-1, keepdims=True))
    probability = (weights / jnp.sum(weights, axis=-1, keepdims=True)).astype(jnp.bfloat16)
    context = dot(probability, value)
    ctx_ref[...] = jnp.concatenate(
        [context[: tokens // 2], context[tokens // 2 :]], axis=1
    ).astype(jnp.bfloat16)


def gate_kernel(rows_here, chunk_rows, *refs):
    count = len(refs) - 11
    pieces = refs[:count]
    (
        gain_ref,
        gate_ref,
        up_ref,
        gate_other_ref,
        up_other_ref,
        keep_ref,
        send_ref,
        kept_ref,
        kept_send_ref,
        order_ref,
        rows_ref,
    ) = refs[count:]
    _, zi, yi, ci = place()
    nz = lax.axis_size(AXIS) // 4
    tokens, width = pieces[0].shape
    half = 2 * nz * width
    total = order_ref.shape[0]
    slots = total // 2
    row = lax.broadcasted_iota(jnp.int32, (total, 1), 0)
    core = jnp.where(row < slots, ci, 1 - ci)
    chunk = (row % slots) // chunk_rows
    device = (zi ^ (chunk // 2)) * 4 + ((chunk % 2) ^ yi) * 2 + core
    wanted = device * rows_here + jnp.minimum(row % chunk_rows, rows_here - 1)
    lanes = lax.broadcasted_iota(jnp.int32, (total, tokens), 1)
    order_ref[...] = (lanes == wanted).astype(jnp.bfloat16)
    squares = jnp.zeros((total, 1), jnp.float32)
    for dz in range(nz):
        near, far = pieces[2 * dz][...], pieces[2 * dz + 1][...]
        pair = jnp.where(
            yi == 0,
            jnp.concatenate([near, far], axis=1),
            jnp.concatenate([far, near], axis=1),
        )
        start = pl.multiple_of((zi ^ dz) * (2 * width), 128)
        values = dot(order_ref[...], pair)
        squares = squares + jnp.sum(values * values, axis=-1, keepdims=True)
        kept_ref[:, pl.ds(start, 2 * width)] = values[0:chunk_rows].astype(jnp.bfloat16)
        kept_send_ref[:, pl.ds(start, 2 * width)] = values[slots : slots + chunk_rows].astype(
            jnp.bfloat16
        )
        gain = gain_ref[:, pl.ds(pl.multiple_of(ci * half + start, 128), 2 * width)]
        rows_ref[:, pl.ds(start, 2 * width)] = (values * gain).astype(jnp.bfloat16)
    mine = pl.ds(pl.multiple_of(ci * half, 128), half)
    rows = rows_ref[...]
    units = gate_ref.shape[0]
    gate = by_rows(rows, gate_ref[:, mine])
    up = by_rows(rows, up_ref[:, mine])
    gate_other = by_rows(rows, gate_other_ref[...])
    up_other = by_rows(rows, up_other_ref[...])
    wide = keep_ref.shape[1] - 4 * units
    spread = jnp.broadcast_to(squares, (total, wide))
    keep_ref[...] = jnp.concatenate(
        [gate[:slots], gate_other[:slots], up[:slots], up_other[:slots], spread[:slots]], axis=1
    )
    send_ref[...] = jnp.concatenate(
        [gate_other[slots:], gate[slots:], up_other[slots:], up[slots:], spread[slots:]], axis=1
    )


def hidden_kernel(features, keep_ref, came_ref, down_ref, down_other_ref, *refs):
    chunk_rows = refs[0].shape[0]
    hidden_ref = refs[-1]
    units = down_ref.shape[0]
    summed = keep_ref[...] + came_ref[...]
    scale = lax.rsqrt(summed[:, 4 * units : 4 * units + 1] / features + 1e-06)
    gate = summed[:, 0 : 2 * units] * scale
    up = summed[:, 2 * units : 4 * units] * scale
    hidden = (jax.nn.gelu(gate, approximate=True) * up).astype(jnp.bfloat16)
    hidden_ref[...] = hidden
    far = jnp.concatenate(
        [
            hidden[(2 * dz + 1) * chunk_rows : (2 * dz + 2) * chunk_rows]
            for dz in range(len(refs) - 1)
        ],
        axis=0,
    )
    result = dot(far[:, :units], down_ref[...]) + dot(far[:, units:], down_other_ref[...])
    for dz in range(len(refs) - 1):
        refs[dz][...] = result[dz * chunk_rows : (dz + 1) * chunk_rows].astype(jnp.bfloat16)


def down_kernel(hidden_ref, down_ref, down_other_ref, *out_refs):
    chunk_rows = out_refs[0].shape[0]
    units = down_ref.shape[0]
    hidden = hidden_ref[...]
    near = jnp.concatenate(
        [
            hidden[2 * dz * chunk_rows : (2 * dz + 1) * chunk_rows]
            for dz in range(len(out_refs))
        ],
        axis=0,
    )
    result = dot(near[:, :units], down_ref[...]) + dot(near[:, units:], down_other_ref[...])
    for dz in range(len(out_refs)):
        out_refs[dz][...] = result[dz * chunk_rows : (dz + 1) * chunk_rows]


def add_kernel(near_ref, far_ref, out_ref):
    out_ref[...] = (near_ref[...] + far_ref[...].astype(jnp.float32)).astype(jnp.bfloat16)


def last_kernel(count, *refs):
    near_ref, far_ref = refs[0], refs[1]
    arrived = refs[2 : 2 + count]
    kept_ref, kept_other_ref, out_ref = refs[2 + count :]
    ci = place()[3]
    rows = out_ref.shape[0]
    half = kept_ref.shape[1]
    kept, other = kept_ref[...].astype(jnp.float32), kept_other_ref[...].astype(jnp.float32)
    total = near_ref[...] + far_ref[...].astype(jnp.float32)
    for ref in arrived:
        total = total + ref[...].astype(jnp.float32)
    low, high = jnp.where(ci == 0, kept, other), jnp.where(ci == 0, other, kept)
    out_ref[:, :half] = (low + total[:, :half])[:rows].astype(jnp.bfloat16)
    out_ref[:, half:] = (high + total[:, half:])[:rows].astype(jnp.bfloat16)


def body(
    queries,
    corpus,
    block_owner,
    slot_row,
    segment,
    query_weight,
    key_weight,
    value_weight,
    out_weight,
    gain_attn,
    gain_ffn,
    gate_weight,
    up_weight,
    down_weight,
):
    devices = lax.axis_size(AXIS)
    nz = devices // 4
    _, zi, yi, ci = place()
    z_order = [k for k in (2, 1) if k < nz] + list(range(3, nz))

    def along_z(value, k):
        return lax.ppermute(value, AXIS, [(i, i ^ (4 * k)) for i in range(devices)])

    def across_y(value):
        return lax.ppermute(value, AXIS, [(i, i ^ 2) for i in range(devices)])

    def across_core(value):
        return lax.ppermute(value, AXIS, [(i, i ^ 1) for i in range(devices)])

    def plane_gather(value):
        near = {0: value}
        for k in z_order:
            near[k] = along_z(value, k)
        return near, {k: across_y(near[k]) for k in [0] + z_order}

    def paired(near, far):
        return [piece for k in range(nz) for piece in (near[k], far[k])]

    owners = block_owner[:, 0]
    features = queries.shape[1]
    half = features // 2
    query_rows = queries.shape[0]
    tokens = query_rows * devices + owners.shape[0] * BLK
    width = features // devices
    heads_rows = query_weight.shape[0]
    units = gate_weight.shape[0]
    rows_here = tokens // devices
    chunk_rows = -(-rows_here // 16) * 16
    bf16, f32 = jnp.bfloat16, jnp.float32
    shape = jax.ShapeDtypeStruct

    full, halved = piece_layout(query_rows + CAP * BLK)
    piece = kernel_call(
        fetch_kernel,
        shape((8, full * features + halved * half), bf16),
        [SMEM, SMEM, ANY, VMEM],
        [
            pltpu.VMEM((CAP, BLK, features), bf16),
            pltpu.VMEM((full * 8 + halved * 8, features), f32),
            pltpu.SemaphoreType.DMA((CAP,)),
        ],
        name="fetch",
    )(owners, slot_row, corpus, queries)

    projections = [query_weight, key_weight, value_weight]
    projections_other = [across_core(w) for w in projections]
    down_other = across_core(down_weight)
    slab = shape((heads_rows, 4 * width), bf16)
    slabs = kernel_call(
        slab_kernel, (slab,) * nz, [VMEM], name="slabs"
    )(out_weight)
    gate_half, up_half = kernel_call(
        half_kernel,
        (shape((units, half), bf16),) * 2,
        [VMEM, VMEM],
        name="halves",
    )(gate_weight, up_weight)
    gate_other, up_other = across_core(gate_half), across_core(up_half)

    plane_rows = 2 * nz * (full * 8 + halved * 4)
    wide = 256 + -(-width // 128) * 128
    near, far = plane_gather(piece)
    own, away = kernel_call(
        functools.partial(projection_kernel, query_rows + CAP * BLK),
        (shape((plane_rows, wide), bf16), shape((plane_rows, wide), bf16)),
        [VMEM] * (2 * nz + 7),
        [pltpu.VMEM((plane_rows, features), bf16)],
        name="project",
    )(*paired(near, far), gain_attn[None, :], *projections, *projections_other)

    slabs = list(slabs)
    slabs[1:], _ = lax.optimization_barrier((slabs[1:], near[z_order[0]]))
    slabs = [slabs[0]] + [along_z(slabs[k], k) for k in range(1, nz)]
    strip = shape((nz * heads_rows, 2 * width), bf16)
    strip_near, strip_send = kernel_call(
        strip_kernel, (strip, strip), [VMEM] * nz, name="strips"
    )(*slabs)
    strip_far = across_y(strip_send)

    context, columns = kernel_call(
        functools.partial(attention_kernel, query_rows, width),
        (shape((tokens // 2, 2 * HDIM), bf16), shape((tokens, width), bf16)),
        [SMEM, SMEM, VMEM, VMEM],
        name="attend",
    )(owners, segment, own, across_core(away))

    contexts = jnp.concatenate([context, across_y(context)], axis=0)
    contexts = [contexts] + [along_z(contexts, k) for k in range(1, nz)]
    attended_mine, attended_other = kernel_call(
        out_kernel,
        (shape((tokens, width), f32),) * 2,
        [VMEM] * (nz + 2),
        name="out",
    )(*contexts, strip_near, strip_far)
    middle = (columns.astype(f32) + attended_mine + across_core(attended_other)).astype(bf16)

    slots = 2 * nz * chunk_rows
    lanes = -(-(4 * units + 1) // 128) * 128
    keep, send, kept, kept_send = kernel_call(
        functools.partial(gate_kernel, rows_here, chunk_rows),
        (
            shape((slots, lanes), f32),
            shape((slots, lanes), f32),
            shape((chunk_rows, half), bf16),
            shape((chunk_rows, half), bf16),
        ),
        [VMEM] * (2 * nz + 5),
        [pltpu.VMEM((2 * slots, tokens), bf16), pltpu.VMEM((2 * slots, half), bf16)],
        name="gate_up",
    )(*paired(*plane_gather(middle)), gain_ffn[None, :], gate_weight, up_weight, gate_other, up_other)
    came = across_core(send)
    kept_other = across_core(kept_send)

    chunk = shape((chunk_rows, features), bf16)
    *far, hidden = kernel_call(
        functools.partial(hidden_kernel, features),
        (chunk,) * nz + (shape((slots, 2 * units), bf16),),
        [VMEM] * 4,
        name="hidden",
    )(keep, came, down_weight, down_other)
    moved = {k: across_y(far[k]) for k in z_order + [0]}
    near = kernel_call(
        down_kernel,
        (shape((chunk_rows, features), f32),) * nz,
        [VMEM] * 3,
        name="down",
    )(hidden, down_weight, down_other)
    arrived = []
    for k in z_order:
        part = kernel_call(add_kernel, chunk, [VMEM, VMEM], name="add")(near[k], moved[k])
        arrived.append(along_z(part, k))
    return kernel_call(
        functools.partial(last_kernel, len(arrived)),
        shape((rows_here, features), bf16),
        [VMEM] * (len(arrived) + 4),
        name="last",
    )(near[0], moved[0], *arrived, kept, kept_other)


def solution(mesh):
    placed = (
        P(("groups", "tensor"), None),
        P(("groups", "tensor"), None, None),
        P("groups", None),
        P("groups"),
        P("groups"),
        P("tensor", None),
        P("tensor", None),
        P("tensor", None),
        P("tensor", None),
        P(),
        P(),
        P("tensor", None),
        P("tensor", None),
        P("tensor", None),
    )
    return jax.shard_map(
        body, mesh=mesh, in_specs=placed, out_specs=P(("groups", "tensor"), None), check_vma=False
    )
```

```python
import functools

import jax
import jax.numpy as jnp
from jax import lax
from jax.experimental import pallas as pl
from jax.experimental.pallas import tpu as pltpu
from jax.sharding import PartitionSpec as P

HDIM = 64
QLEN = 32
BLK = 4
CAP = 3
AXIS = "tensor"
VMEM_LIMIT = 28 * 1024 * 1024


def by_rows(left, weight):
    return lax.dot_general(
        left, weight, (((1,), (1,)), ((), ())), preferred_element_type=jnp.float32
    )


def dot(left, right):
    return jnp.dot(left, right, preferred_element_type=jnp.float32)


def place():
    me = lax.axis_index(AXIS)
    return me, me // 4, (me // 2) % 2, me % 2


def kernel_call(kernel, out_shape, in_specs, scratch=(), name=None, limit=VMEM_LIMIT, micros=1):
    return pl.pallas_call(
        kernel,
        out_shape=out_shape,
        cost_estimate=pl.CostEstimate(
            flops=micros * 1_000_000_000, bytes_accessed=micros * 3_000_000, transcendentals=0
        ),
        in_specs=in_specs,
        out_specs=jax.tree.map(lambda _: pl.BlockSpec(memory_space=pltpu.VMEM), out_shape),
        scratch_shapes=scratch,
        compiler_params=pltpu.CompilerParams(vmem_limit_bytes=limit),
        name=name,
    )


SMEM = pl.BlockSpec(memory_space=pltpu.SMEM)
VMEM = pl.BlockSpec(memory_space=pltpu.VMEM)
ANY = pl.BlockSpec(memory_space=pl.ANY)


def piece_layout(rows):
    full, rest = divmod(rows, 8)
    if 0 < rest <= 4:
        return full, True
    return full + (rest > 0), False


def fetch_kernel(owner_ref, row_ref, corpus_ref, query_ref, piece_ref, blocks, rows, sems):
    me = place()[0]
    features = query_ref.shape[1]
    query_rows = query_ref.shape[0]

    def look(b, carry):
        count, found = carry[0], carry[1:]
        mine = owner_ref[b] == me
        found = tuple(
            jnp.where(mine & (count == k), row_ref[b], found[k]) for k in range(CAP)
        )
        return (count + mine.astype(jnp.int32),) + found

    zero = jnp.int32(0)
    found = lax.fori_loop(0, owner_ref.shape[0], look, (zero,) * (CAP + 1))[1:]
    copies = [
        pltpu.make_async_copy(corpus_ref.at[found[k]], blocks.at[k], sems.at[k])
        for k in range(CAP)
    ]
    for copy in copies:
        copy.start()
    total = query_rows + CAP * BLK
    full, halved = piece_layout(total)
    rows[0:query_rows, :] = query_ref[...].astype(jnp.float32)
    for k in range(CAP):
        copies[k].wait()
        first = query_rows + k * BLK
        rows[first : first + BLK, :] = blocks[k].astype(jnp.float32)
    if not halved and total < full * 8:
        rows[total : full * 8, :] = jnp.zeros((full * 8 - total, features), jnp.float32)
    for i in range(full):
        piece_ref[:, i * features : (i + 1) * features] = rows[i * 8 : i * 8 + 8, :].astype(
            jnp.bfloat16
        )
    if halved:
        half = features // 2
        last = rows[full * 8 : full * 8 + 4, :]
        if total % 8 < 4:
            last = jnp.where(
                lax.broadcasted_iota(jnp.int32, last.shape, 0) < total % 8, last, 0.0
            )
        piece_ref[:, full * features :] = jnp.concatenate(
            [last[:, :half], last[:, half:]], axis=0
        ).astype(jnp.bfloat16)


def columns_at(ref, start, width):
    if width % 128 == 0:
        return ref[:, pl.ds(pl.multiple_of(start, 128), width)].astype(jnp.float32)
    base = pl.multiple_of(start // 128 * 128, 128)
    window = ref[:, pl.ds(base, 128)].astype(jnp.float32)
    return pltpu.roll(window, (128 - start % 128) % 128, 1)[:, :width]


def across_kernel(piece_ref, weight_ref, out_ref):
    _, zi, yi, _ = place()
    nz = lax.axis_size(AXIS) // 4
    rows, features = weight_ref.shape
    width = features // (4 * nz)
    first = piece_ref.shape[1]
    wide = 2 * nz * width
    out_ref[:, :first] = piece_ref[...]
    columns = jnp.concatenate(
        [
            columns_at(
                weight_ref, core * (features // 2) + (2 * (zi ^ d) + 1 - yi) * width, width
            )
            for d in range(nz)
            for core in range(2)
        ],
        axis=1,
    )
    for g in range(rows // 8):
        out_ref[:, first + g * wide : first + (g + 1) * wide] = columns[
            g * 8 : g * 8 + 8
        ].astype(jnp.bfloat16)


def pair_kernel(first, weight_ref, far_ref, keep_ref, send_ref):
    _, zi, yi, ci = place()
    rows, features = weight_ref.shape
    nz = lax.axis_size(AXIS) // 4
    width = features // (4 * nz)
    wide = 2 * nz * width
    for core, out_ref in ((ci, keep_ref), (1 - ci, send_ref)):
        own = [
            columns_at(
                weight_ref, core * (features // 2) + (2 * (zi ^ d) + yi) * width, width
            )
            for d in range(nz)
        ]
        out_ref[:rows, :] = jnp.concatenate(own, axis=1).astype(jnp.bfloat16)
        groups = []
        for g in range(rows // 8):
            parts = []
            for d in range(nz):
                start = first + g * wide + 2 * d * width
                both = far_ref[:, start : start + 2 * width].astype(jnp.float32)
                parts.append(jnp.where(core == 0, both[:, :width], both[:, width:]))
            groups.append(jnp.concatenate(parts, axis=1))
        out_ref[rows:, :] = jnp.concatenate(groups, axis=0).astype(jnp.bfloat16)


def stack_kernel(*refs):
    rows = refs[0].shape[0]
    for i, ref in enumerate(refs[:-1]):
        refs[-1][i * rows : (i + 1) * rows, :] = ref[...]


def share_kernel(gate_ref, up_ref, down_ref, out_ref):
    units, features = down_ref.shape
    half = features // 2
    other = pl.ds(pl.multiple_of((1 - place()[3]) * half, 128), half)
    out_ref[:units, :half] = gate_ref[:, other]
    out_ref[:units, half:] = up_ref[:, other]
    out_ref[units:, :] = down_ref[...]


def out_kernel(own_ref, other_ref, weight_ref, weight_other_ref, mine_ref, *send_refs):
    width = mine_ref.shape[1]
    half = own_ref.shape[0] // 2

    def heads(ref):
        near, far = ref[:half, :], ref[half:, :]
        return jnp.concatenate(
            [
                jnp.concatenate([near[:, :HDIM], far[:, :HDIM]], axis=1),
                jnp.concatenate([near[:, HDIM:], far[:, HDIM:]], axis=1),
            ],
            axis=0,
        )

    attended = dot(heads(own_ref), weight_ref[...]) + dot(heads(other_ref), weight_other_ref[...])
    mine_ref[...] = attended[:, :width]
    for d, ref in enumerate(send_refs, 1):
        ref[...] = attended[:, d * width : (d + 1) * width].astype(jnp.bfloat16)


def projection_kernel(piece_rows, *refs):
    count = len(refs) - 8
    pieces, rest = refs[:count], refs[count:]
    gain_ref, *mine, other_ref, out_ref, out_other_ref, normal = rest
    _, zi, yi, ci = place()
    features = gain_ref.shape[1]
    half = features // 2
    full, halved = piece_layout(piece_rows)
    width = features // lax.axis_size(AXIS)
    chip = 2 * zi + yi
    gain = gain_ref[...]
    spot = 256
    own_column = ci * half + chip * width
    other_column = (1 - ci) * half + chip * width

    def scaled(values, squares):
        return values * lax.rsqrt(squares / features + 1e-06)

    def put(row, groups):
        normal[row : row + 16, :] = jnp.concatenate(groups, axis=0).astype(jnp.bfloat16)

    chunks = [(p, i) for p in range(count) for i in range(full)]
    for first in range(0, len(chunks), 2):
        groups, own, away = [], [], []
        for p, i in chunks[first : first + 2]:
            values = pieces[p][:, i * features : (i + 1) * features].astype(jnp.float32)
            squares = jnp.sum(values * values, axis=-1, keepdims=True)
            groups.append(scaled(values, squares) * gain)
            own.append(columns_at(pieces[p], i * features + own_column, width))
            away.append(columns_at(pieces[p], i * features + other_column, width))
        row = first * 8
        put(row, groups)
        out_ref[row : row + 16, spot : spot + width] = jnp.concatenate(own, axis=0).astype(
            jnp.bfloat16
        )
        out_other_ref[row : row + 16, spot : spot + width] = jnp.concatenate(
            away, axis=0
        ).astype(jnp.bfloat16)
    if halved:
        for first in range(0, count, 4):
            groups, own, away = [], [], []
            for p in range(first, first + 4, 2):
                a, b = (
                    pieces[q][:, full * features : full * features + half].astype(jnp.float32)
                    for q in (p, p + 1)
                )
                low = jnp.concatenate([a[0:4], b[0:4]], axis=0)
                high = jnp.concatenate([a[4:8], b[4:8]], axis=0)
                squares = jnp.sum(low * low, axis=-1, keepdims=True) + jnp.sum(
                    high * high, axis=-1, keepdims=True
                )
                groups.append(
                    jnp.concatenate([scaled(low, squares), scaled(high, squares)], axis=1)
                    * gain
                )
                a, b = (
                    columns_at(pieces[q], full * features + chip * width, width)
                    for q in (p, p + 1)
                )
                low = jnp.concatenate([a[0:4], b[0:4]], axis=0)
                high = jnp.concatenate([a[4:8], b[4:8]], axis=0)
                own.append(jnp.where(ci == 0, low, high))
                away.append(jnp.where(ci == 0, high, low))
            row = len(chunks) * 8 + first * 4
            put(row, groups)
            out_ref[row : row + 16, spot : spot + width] = jnp.concatenate(
                own, axis=0
            ).astype(jnp.bfloat16)
            out_other_ref[row : row + 16, spot : spot + width] = jnp.concatenate(
                away, axis=0
            ).astype(jnp.bfloat16)
    rows = normal[...]
    for target, weights in ((out_other_ref, [other_ref]), (out_ref, mine)):
        value = jnp.concatenate([by_rows(rows, w[...]) for w in weights], axis=1)
        target[:, 0 : value.shape[1]] = value.astype(jnp.bfloat16)


def attention_kernel(query_rows, width, owner_ref, segment_ref, own_ref, away_ref, ctx_ref, col_ref):
    _, zi, yi, ci = place()
    nz = lax.axis_size(AXIS) // 4
    query_total = query_rows * 4 * nz
    blocks_total = owner_ref.shape[0]
    tokens = query_total + blocks_total * BLK
    piece_rows = query_rows + CAP * BLK
    full, halved = piece_layout(piece_rows)
    plane_rows = own_ref.shape[0]

    def lay(shape, axis):
        token = lax.broadcasted_iota(jnp.int32, shape, axis)
        block = (token - query_total) // BLK
        is_query = token < query_total
        owner = jnp.where(is_query, token // query_rows, 0)
        pair = jnp.where(is_query, token // QLEN, 0)

        def fill(b, carry):
            here = (block == b) & (token >= query_total)
            return (
                jnp.where(here, owner_ref[b], carry[0]),
                jnp.where(here, segment_ref[b], carry[1]),
            )

        owner, pair = lax.fori_loop(0, blocks_total, fill, (owner, pair))
        return token, block, owner, pair

    token, block, owner, pair = lay((tokens, 1), 0)
    token_row, block_row, owner_row, pair_row = lay((1, tokens), 1)
    ahead = (
        (owner == owner_row)
        & (block_row < block)
        & (token_row >= query_total)
        & (token >= query_total)
    )
    before = jnp.sum(ahead.astype(jnp.float32), axis=-1, keepdims=True).astype(jnp.int32)
    local = jnp.where(
        token < query_total,
        token % query_rows,
        query_rows + before + (token - query_total) % BLK,
    )
    source = (zi ^ (owner // 4)) * 2 + (((owner // 2) % 2) ^ yi)
    pieces = 2 * nz
    spot = source * (full * 8) + local
    if halved:
        spot = jnp.where(
            local < full * 8, spot, pieces * full * 8 + source * 4 + local - full * 8
        )
    spot = spot + ((owner % 2) ^ ci) * plane_rows
    lanes = lax.broadcasted_iota(jnp.int32, (tokens, plane_rows), 1)
    pick_own = (lanes == spot).astype(jnp.bfloat16)
    pick_away = (lanes == spot - plane_rows).astype(jnp.bfloat16)
    packed = dot(pick_own, own_ref[...]) + dot(pick_away, away_ref[...])
    col_ref[...] = packed[:, 256 : 256 + width].astype(jnp.bfloat16)
    query, key, value = (
        packed[:, i * HDIM : (i + 1) * HDIM].astype(jnp.bfloat16) for i in range(3)
    )
    scores = by_rows(query, key) * HDIM ** (-0.5)
    scores = jnp.where(pair == pair_row, scores, -1e30)
    weights = jnp.exp(scores - jnp.max(scores, axis=-1, keepdims=True))
    probability = (weights / jnp.sum(weights, axis=-1, keepdims=True)).astype(jnp.bfloat16)
    context = dot(probability, value)
    ctx_ref[...] = jnp.concatenate(
        [context[: tokens // 2], context[tokens // 2 :]], axis=1
    ).astype(jnp.bfloat16)


def gate_kernel(rows_here, chunk_rows, *refs):
    count = len(refs) - 10
    pieces = refs[:count]
    (
        gain_ref,
        gate_ref,
        up_ref,
        share_ref,
        keep_ref,
        send_ref,
        kept_ref,
        kept_send_ref,
        order_ref,
        rows_ref,
    ) = refs[count:]
    _, zi, yi, ci = place()
    nz = lax.axis_size(AXIS) // 4
    tokens, width = pieces[0].shape
    half = 2 * nz * width
    total = order_ref.shape[0]
    slots = total // 2
    row = lax.broadcasted_iota(jnp.int32, (total, 1), 0)
    core = jnp.where(row < slots, ci, 1 - ci)
    chunk = (row % slots) // chunk_rows
    device = (zi ^ (chunk // 2)) * 4 + ((chunk % 2) ^ yi) * 2 + core
    wanted = device * rows_here + jnp.minimum(row % chunk_rows, rows_here - 1)
    lanes = lax.broadcasted_iota(jnp.int32, (total, tokens), 1)
    order_ref[...] = (lanes == wanted).astype(jnp.bfloat16)
    squares = jnp.zeros((total, 1), jnp.float32)
    for dz in range(nz):
        near, far = pieces[2 * dz][...], pieces[2 * dz + 1][...]
        pair = jnp.where(
            yi == 0,
            jnp.concatenate([near, far], axis=1),
            jnp.concatenate([far, near], axis=1),
        )
        start = pl.multiple_of((zi ^ dz) * (2 * width), 128)
        values = dot(order_ref[...], pair)
        squares = squares + jnp.sum(values * values, axis=-1, keepdims=True)
        kept_ref[:, pl.ds(start, 2 * width)] = values[0:chunk_rows].astype(jnp.bfloat16)
        kept_send_ref[:, pl.ds(start, 2 * width)] = values[slots : slots + chunk_rows].astype(
            jnp.bfloat16
        )
        gain = gain_ref[:, pl.ds(pl.multiple_of(ci * half + start, 128), 2 * width)]
        rows_ref[:, pl.ds(start, 2 * width)] = (values * gain).astype(jnp.bfloat16)
    mine = pl.ds(pl.multiple_of(ci * half, 128), half)
    rows = rows_ref[...]
    units = gate_ref.shape[0]
    gate = by_rows(rows, gate_ref[:, mine])
    up = by_rows(rows, up_ref[:, mine])
    gate_other = by_rows(rows, share_ref[:units, :half])
    up_other = by_rows(rows, share_ref[:units, half:])
    wide = keep_ref.shape[1] - 4 * units
    spread = jnp.broadcast_to(squares, (total, wide))
    keep_ref[...] = jnp.concatenate(
        [gate[:slots], gate_other[:slots], up[:slots], up_other[:slots], spread[:slots]], axis=1
    )
    send_ref[...] = jnp.concatenate(
        [gate_other[slots:], gate[slots:], up_other[slots:], up[slots:], spread[slots:]], axis=1
    )


def hidden_kernel(features, keep_ref, came_ref, down_ref, share_ref, *refs):
    chunk_rows = refs[0].shape[0]
    hidden_ref = refs[-1]
    units = down_ref.shape[0]
    summed = keep_ref[...] + came_ref[...]
    scale = lax.rsqrt(summed[:, 4 * units : 4 * units + 1] / features + 1e-06)
    gate = summed[:, 0 : 2 * units] * scale
    up = summed[:, 2 * units : 4 * units] * scale
    hidden = (jax.nn.gelu(gate, approximate=True) * up).astype(jnp.bfloat16)
    hidden_ref[...] = hidden
    far = jnp.concatenate(
        [
            hidden[(2 * dz + 1) * chunk_rows : (2 * dz + 2) * chunk_rows]
            for dz in range(len(refs) - 1)
        ],
        axis=0,
    )
    result = dot(far[:, :units], down_ref[...]) + dot(far[:, units:], share_ref[units:, :])
    for dz in range(len(refs) - 1):
        refs[dz][...] = result[dz * chunk_rows : (dz + 1) * chunk_rows].astype(jnp.bfloat16)


def down_kernel(hidden_ref, down_ref, share_ref, *out_refs):
    chunk_rows = out_refs[0].shape[0]
    units = down_ref.shape[0]
    hidden = hidden_ref[...]
    near = jnp.concatenate(
        [
            hidden[2 * dz * chunk_rows : (2 * dz + 1) * chunk_rows]
            for dz in range(len(out_refs))
        ],
        axis=0,
    )
    result = dot(near[:, :units], down_ref[...]) + dot(near[:, units:], share_ref[units:, :])
    for dz in range(len(out_refs)):
        out_refs[dz][...] = result[dz * chunk_rows : (dz + 1) * chunk_rows]


def add_kernel(near_ref, far_ref, out_ref):
    out_ref[...] = (near_ref[...] + far_ref[...].astype(jnp.float32)).astype(jnp.bfloat16)


def last_kernel(count, *refs):
    near_ref, far_ref = refs[0], refs[1]
    arrived = refs[2 : 2 + count]
    kept_ref, kept_other_ref, out_ref = refs[2 + count :]
    ci = place()[3]
    rows = out_ref.shape[0]
    half = kept_ref.shape[1]
    kept, other = kept_ref[...].astype(jnp.float32), kept_other_ref[...].astype(jnp.float32)
    total = near_ref[...] + far_ref[...].astype(jnp.float32)
    for ref in arrived:
        total = total + ref[...].astype(jnp.float32)
    low, high = jnp.where(ci == 0, kept, other), jnp.where(ci == 0, other, kept)
    out_ref[:, :half] = (low + total[:, :half])[:rows].astype(jnp.bfloat16)
    out_ref[:, half:] = (high + total[:, half:])[:rows].astype(jnp.bfloat16)


def body(
    queries,
    corpus,
    block_owner,
    slot_row,
    segment,
    query_weight,
    key_weight,
    value_weight,
    out_weight,
    gain_attn,
    gain_ffn,
    gate_weight,
    up_weight,
    down_weight,
):
    devices = lax.axis_size(AXIS)
    nz = devices // 4
    _, zi, yi, ci = place()
    z_order = [k for k in (2, 1) if k < nz] + list(range(3, nz))

    def along_z(value, k):
        return lax.ppermute(value, AXIS, [(i, i ^ (4 * k)) for i in range(devices)])

    def across_y(value):
        return lax.ppermute(value, AXIS, [(i, i ^ 2) for i in range(devices)])

    def across_core(value):
        return lax.ppermute(value, AXIS, [(i, i ^ 1) for i in range(devices)])

    def plane_gather(value, value_across=None, fence=None):
        near = {0: value}
        for k in z_order:
            near[k] = along_z(value, k)
        if fence is not None:
            for k in near:
                near[k], fence = lax.optimization_barrier((near[k], fence))
        if value_across is None:
            value_across = near[0]
        return near, {
            k: across_y(near[k] if k else value_across) for k in [0] + z_order
        }

    def paired(near, far):
        return [piece for k in range(nz) for piece in (near[k], far[k])]

    owners = block_owner[:, 0]
    features = queries.shape[1]
    half = features // 2
    query_rows = queries.shape[0]
    tokens = query_rows * devices + owners.shape[0] * BLK
    width = features // devices
    heads_rows = query_weight.shape[0]
    units = gate_weight.shape[0]
    rows_here = tokens // devices
    chunk_rows = -(-rows_here // 16) * 16
    bf16, f32 = jnp.bfloat16, jnp.float32
    shape = jax.ShapeDtypeStruct

    full, halved = piece_layout(query_rows + CAP * BLK)
    piece = kernel_call(
        fetch_kernel,
        shape((8, full * features + halved * half), bf16),
        [SMEM, SMEM, ANY, VMEM],
        [
            pltpu.VMEM((CAP, BLK, features), bf16),
            pltpu.VMEM((full * 8 + halved * 8, features), f32),
            pltpu.SemaphoreType.DMA((CAP,)),
        ],
        name="fetch",
        limit=60 * 1024 * 1024,
    )(owners, slot_row, corpus, queries)

    projections = [query_weight, key_weight, value_weight]
    plane_rows = 2 * nz * (full * 8 + halved * 4)
    wide = 256 + -(-width // 128) * 128
    *tied, _ = lax.optimization_barrier((*projections, piece))
    stacked = kernel_call(
        stack_kernel,
        shape((3 * heads_rows, features), bf16),
        [VMEM] * 3,
        name="stack",
        micros=20,
    )(*tied)
    piece_wide = piece.shape[1]
    value_across = kernel_call(
        across_kernel,
        shape((8, piece_wide + heads_rows // 8 * 2 * nz * width), bf16),
        [VMEM] * 2,
        name="across",
    )(piece, out_weight)
    near, far = plane_gather(piece, value_across, stacked)
    projections_other = across_core(stacked)
    own, away = kernel_call(
        functools.partial(projection_kernel, query_rows + CAP * BLK),
        (shape((plane_rows, wide), bf16), shape((plane_rows, wide), bf16)),
        [VMEM] * (2 * nz + 5),
        [pltpu.VMEM((plane_rows, features), bf16)],
        name="project",
        micros=10,
    )(*paired(near, far), gain_attn[None, :], *projections, projections_other)

    out_keep, out_send = kernel_call(
        functools.partial(pair_kernel, piece_wide),
        (shape((2 * heads_rows, nz * width), bf16),) * 2,
        [VMEM] * 2,
        name="pairs",
    )(out_weight, far[0])
    out_came = across_core(out_send)

    context, columns = kernel_call(
        functools.partial(attention_kernel, query_rows, width),
        (shape((tokens // 2, 2 * HDIM), bf16), shape((tokens, width), bf16)),
        [SMEM, SMEM, VMEM, VMEM],
        name="attend",
    )(owners, segment, own, across_core(away))
    share_gate, share_up, share_down, _ = lax.optimization_barrier(
        (gate_weight, up_weight, down_weight, context)
    )
    share = across_core(
        kernel_call(
            share_kernel, shape((2 * units, features), bf16), [VMEM] * 3, name="share"
        )(share_gate, share_up, share_down)
    )

    contexts = jnp.concatenate([context, across_y(context)], axis=0)
    attended, *parts = kernel_call(
        out_kernel,
        (shape((tokens, width), f32),) + (shape((tokens, width), bf16),) * (nz - 1),
        [VMEM] * 4,
        name="out",
    )(contexts, across_core(contexts), out_keep, out_came)
    middle = columns.astype(f32) + attended
    for d in z_order:
        middle = middle + along_z(parts[d - 1], d).astype(f32)
    middle = middle.astype(bf16)

    slots = 2 * nz * chunk_rows
    lanes = -(-(4 * units + 1) // 128) * 128
    keep, send, kept, kept_send = kernel_call(
        functools.partial(gate_kernel, rows_here, chunk_rows),
        (
            shape((slots, lanes), f32),
            shape((slots, lanes), f32),
            shape((chunk_rows, half), bf16),
            shape((chunk_rows, half), bf16),
        ),
        [VMEM] * (2 * nz + 4),
        [pltpu.VMEM((2 * slots, tokens), bf16), pltpu.VMEM((2 * slots, half), bf16)],
        name="gate_up",
    )(*paired(*plane_gather(middle)), gain_ffn[None, :], gate_weight, up_weight, share)
    came = across_core(send)
    kept_other = across_core(kept_send)

    chunk = shape((chunk_rows, features), bf16)
    *far, hidden = kernel_call(
        functools.partial(hidden_kernel, features),
        (chunk,) * nz + (shape((slots, 2 * units), bf16),),
        [VMEM] * 4,
        name="hidden",
    )(keep, came, down_weight, share)
    moved = {k: across_y(far[k]) for k in z_order + [0]}
    near = kernel_call(
        down_kernel,
        (shape((chunk_rows, features), f32),) * nz,
        [VMEM] * 3,
        name="down",
    )(hidden, down_weight, share)
    arrived = []
    for k in z_order:
        part = kernel_call(add_kernel, chunk, [VMEM, VMEM], name="add")(near[k], moved[k])
        arrived.append(along_z(part, k))
    return kernel_call(
        functools.partial(last_kernel, len(arrived)),
        shape((rows_here, features), bf16),
        [VMEM] * (len(arrived) + 4),
        name="last",
    )(near[0], moved[0], *arrived, kept, kept_other)


def solution(mesh):
    placed = (
        P(("groups", "tensor"), None),
        P(("groups", "tensor"), None, None),
        P("groups", None),
        P("groups"),
        P("groups"),
        P("tensor", None),
        P("tensor", None),
        P("tensor", None),
        P("tensor", None),
        P(),
        P(),
        P("tensor", None),
        P("tensor", None),
        P("tensor", None),
    )
    return jax.shard_map(
        body, mesh=mesh, in_specs=placed, out_specs=P(("groups", "tensor"), None), check_vma=False
    )
```

```python
import functools

import jax
import jax.numpy as jnp
from jax import lax
from jax.experimental import pallas as pl
from jax.experimental.pallas import tpu as pltpu
from jax.sharding import PartitionSpec as P

HDIM = 64
QLEN = 32
BLK = 4
CAP = 3
AXIS = "tensor"
VMEM_LIMIT = 28 * 1024 * 1024


def by_rows(left, weight):
    return lax.dot_general(
        left, weight, (((1,), (1,)), ((), ())), preferred_element_type=jnp.float32
    )


def dot(left, right):
    return jnp.dot(left, right, preferred_element_type=jnp.float32)


def place():
    me = lax.axis_index(AXIS)
    return me, me // 4, (me // 2) % 2, me % 2


def kernel_call(kernel, out_shape, in_specs, scratch=(), name=None, limit=VMEM_LIMIT, micros=1):
    return pl.pallas_call(
        kernel,
        out_shape=out_shape,
        cost_estimate=pl.CostEstimate(
            flops=micros * 1_000_000_000, bytes_accessed=micros * 3_000_000, transcendentals=0
        ),
        in_specs=in_specs,
        out_specs=jax.tree.map(lambda _: pl.BlockSpec(memory_space=pltpu.VMEM), out_shape),
        scratch_shapes=scratch,
        compiler_params=pltpu.CompilerParams(vmem_limit_bytes=limit),
        name=name,
    )


SMEM = pl.BlockSpec(memory_space=pltpu.SMEM)
VMEM = pl.BlockSpec(memory_space=pltpu.VMEM)
ANY = pl.BlockSpec(memory_space=pl.ANY)


def piece_layout(rows):
    full, rest = divmod(rows, 8)
    if 0 < rest <= 4:
        return full, True
    return full + (rest > 0), False


def fetch_kernel(owner_ref, row_ref, corpus_ref, query_ref, piece_ref, blocks, rows, sems):
    me = place()[0]
    features = query_ref.shape[1]
    query_rows = query_ref.shape[0]

    def look(b, carry):
        count, found = carry[0], carry[1:]
        mine = owner_ref[b] == me
        found = tuple(
            jnp.where(mine & (count == k), row_ref[b], found[k]) for k in range(CAP)
        )
        return (count + mine.astype(jnp.int32),) + found

    zero = jnp.int32(0)
    found = lax.fori_loop(0, owner_ref.shape[0], look, (zero,) * (CAP + 1))[1:]
    copies = [
        pltpu.make_async_copy(corpus_ref.at[found[k]], blocks.at[k], sems.at[k])
        for k in range(CAP)
    ]
    for copy in copies:
        copy.start()
    total = query_rows + CAP * BLK
    full, halved = piece_layout(total)
    rows[0:query_rows, :] = query_ref[...].astype(jnp.float32)
    for k in range(CAP):
        copies[k].wait()
        first = query_rows + k * BLK
        rows[first : first + BLK, :] = blocks[k].astype(jnp.float32)
    if not halved and total < full * 8:
        rows[total : full * 8, :] = jnp.zeros((full * 8 - total, features), jnp.float32)
    for i in range(full):
        piece_ref[:, i * features : (i + 1) * features] = rows[i * 8 : i * 8 + 8, :].astype(
            jnp.bfloat16
        )
    if halved:
        half = features // 2
        last = rows[full * 8 : full * 8 + 4, :]
        if total % 8 < 4:
            last = jnp.where(
                lax.broadcasted_iota(jnp.int32, last.shape, 0) < total % 8, last, 0.0
            )
        piece_ref[:, full * features :] = jnp.concatenate(
            [last[:, :half], last[:, half:]], axis=0
        ).astype(jnp.bfloat16)


def columns_at(ref, start, width):
    if width % 128 == 0:
        return ref[:, pl.ds(pl.multiple_of(start, 128), width)].astype(jnp.float32)
    base = pl.multiple_of(start // 128 * 128, 128)
    window = ref[:, pl.ds(base, 128)].astype(jnp.float32)
    return pltpu.roll(window, (128 - start % 128) % 128, 1)[:, :width]


def across_kernel(piece_ref, weight_ref, out_ref):
    _, zi, yi, _ = place()
    nz = lax.axis_size(AXIS) // 4
    rows, features = weight_ref.shape
    width = features // (4 * nz)
    first = piece_ref.shape[1]
    wide = 2 * nz * width
    out_ref[:, :first] = piece_ref[...]
    columns = jnp.concatenate(
        [
            columns_at(
                weight_ref, core * (features // 2) + (2 * (zi ^ d) + 1 - yi) * width, width
            )
            for d in range(nz)
            for core in range(2)
        ],
        axis=1,
    )
    for g in range(rows // 8):
        out_ref[:, first + g * wide : first + (g + 1) * wide] = columns[
            g * 8 : g * 8 + 8
        ].astype(jnp.bfloat16)


def pair_kernel(first, weight_ref, far_ref, keep_ref, send_ref):
    _, zi, yi, ci = place()
    rows, features = weight_ref.shape
    nz = lax.axis_size(AXIS) // 4
    width = features // (4 * nz)
    wide = 2 * nz * width
    for core, out_ref in ((ci, keep_ref), (1 - ci, send_ref)):
        own = [
            columns_at(
                weight_ref, core * (features // 2) + (2 * (zi ^ d) + yi) * width, width
            )
            for d in range(nz)
        ]
        out_ref[:rows, :] = jnp.concatenate(own, axis=1).astype(jnp.bfloat16)
        groups = []
        for g in range(rows // 8):
            parts = []
            for d in range(nz):
                start = first + g * wide + 2 * d * width
                both = far_ref[:, start : start + 2 * width].astype(jnp.float32)
                parts.append(jnp.where(core == 0, both[:, :width], both[:, width:]))
            groups.append(jnp.concatenate(parts, axis=1))
        out_ref[rows:, :] = jnp.concatenate(groups, axis=0).astype(jnp.bfloat16)


def stack_kernel(*refs):
    rows = refs[0].shape[0]
    for i, ref in enumerate(refs[:-1]):
        refs[-1][i * rows : (i + 1) * rows, :] = ref[...]


def share_kernel(gate_ref, up_ref, down_ref, out_ref):
    units, features = down_ref.shape
    half = features // 2
    other = pl.ds(pl.multiple_of((1 - place()[3]) * half, 128), half)
    out_ref[:units, :half] = gate_ref[:, other]
    out_ref[:units, half:] = up_ref[:, other]
    out_ref[units:, :] = down_ref[...]


def out_kernel(own_ref, other_ref, weight_ref, weight_other_ref, mine_ref, *send_refs):
    width = mine_ref.shape[1]
    half = own_ref.shape[0] // 2

    def heads(ref):
        near, far = ref[:half, :], ref[half:, :]
        return jnp.concatenate(
            [
                jnp.concatenate([near[:, :HDIM], far[:, :HDIM]], axis=1),
                jnp.concatenate([near[:, HDIM:], far[:, HDIM:]], axis=1),
            ],
            axis=0,
        )

    attended = dot(heads(own_ref), weight_ref[...]) + dot(heads(other_ref), weight_other_ref[...])
    mine_ref[...] = attended[:, :width]
    for d, ref in enumerate(send_refs, 1):
        ref[...] = attended[:, d * width : (d + 1) * width].astype(jnp.bfloat16)


def projection_kernel(piece_rows, *refs):
    count = len(refs) - 8
    pieces, rest = refs[:count], refs[count:]
    gain_ref, *mine, other_ref, out_ref, out_other_ref, normal = rest
    _, zi, yi, ci = place()
    features = gain_ref.shape[1]
    half = features // 2
    full, halved = piece_layout(piece_rows)
    width = features // lax.axis_size(AXIS)
    chip = 2 * zi + yi
    gain = gain_ref[...]
    spot = 256
    own_column = ci * half + chip * width
    other_column = (1 - ci) * half + chip * width

    def scaled(values, squares):
        return values * lax.rsqrt(squares / features + 1e-06)

    def put(row, groups):
        normal[row : row + 16, :] = jnp.concatenate(groups, axis=0).astype(jnp.bfloat16)

    chunks = [(p, i) for p in range(count) for i in range(full)]
    for first in range(0, len(chunks), 2):
        groups, own, away = [], [], []
        for p, i in chunks[first : first + 2]:
            values = pieces[p][:, i * features : (i + 1) * features].astype(jnp.float32)
            squares = jnp.sum(values * values, axis=-1, keepdims=True)
            groups.append(scaled(values, squares) * gain)
            own.append(columns_at(pieces[p], i * features + own_column, width))
            away.append(columns_at(pieces[p], i * features + other_column, width))
        row = first * 8
        put(row, groups)
        out_ref[row : row + 16, spot : spot + width] = jnp.concatenate(own, axis=0).astype(
            jnp.bfloat16
        )
        out_other_ref[row : row + 16, spot : spot + width] = jnp.concatenate(
            away, axis=0
        ).astype(jnp.bfloat16)
    if halved:
        for first in range(0, count, 4):
            groups, own, away = [], [], []
            for p in range(first, first + 4, 2):
                a, b = (
                    pieces[q][:, full * features : full * features + half].astype(jnp.float32)
                    for q in (p, p + 1)
                )
                low = jnp.concatenate([a[0:4], b[0:4]], axis=0)
                high = jnp.concatenate([a[4:8], b[4:8]], axis=0)
                squares = jnp.sum(low * low, axis=-1, keepdims=True) + jnp.sum(
                    high * high, axis=-1, keepdims=True
                )
                groups.append(
                    jnp.concatenate([scaled(low, squares), scaled(high, squares)], axis=1)
                    * gain
                )
                a, b = (
                    columns_at(pieces[q], full * features + chip * width, width)
                    for q in (p, p + 1)
                )
                low = jnp.concatenate([a[0:4], b[0:4]], axis=0)
                high = jnp.concatenate([a[4:8], b[4:8]], axis=0)
                own.append(jnp.where(ci == 0, low, high))
                away.append(jnp.where(ci == 0, high, low))
            row = len(chunks) * 8 + first * 4
            put(row, groups)
            out_ref[row : row + 16, spot : spot + width] = jnp.concatenate(
                own, axis=0
            ).astype(jnp.bfloat16)
            out_other_ref[row : row + 16, spot : spot + width] = jnp.concatenate(
                away, axis=0
            ).astype(jnp.bfloat16)
    rows = normal[...]
    for target, weights in ((out_other_ref, [other_ref]), (out_ref, mine)):
        value = jnp.concatenate([by_rows(rows, w[...]) for w in weights], axis=1)
        target[:, 0 : value.shape[1]] = value.astype(jnp.bfloat16)


def attention_kernel(query_rows, width, owner_ref, segment_ref, own_ref, away_ref, ctx_ref, col_ref):
    _, zi, yi, ci = place()
    nz = lax.axis_size(AXIS) // 4
    query_total = query_rows * 4 * nz
    blocks_total = owner_ref.shape[0]
    tokens = query_total + blocks_total * BLK
    piece_rows = query_rows + CAP * BLK
    full, halved = piece_layout(piece_rows)
    plane_rows = own_ref.shape[0]

    def lay(shape, axis):
        token = lax.broadcasted_iota(jnp.int32, shape, axis)
        block = (token - query_total) // BLK
        is_query = token < query_total
        owner = jnp.where(is_query, token // query_rows, 0)
        pair = jnp.where(is_query, token // QLEN, 0)

        def fill(b, carry):
            here = (block == b) & (token >= query_total)
            return (
                jnp.where(here, owner_ref[b], carry[0]),
                jnp.where(here, segment_ref[b], carry[1]),
            )

        owner, pair = lax.fori_loop(0, blocks_total, fill, (owner, pair))
        return token, block, owner, pair

    token, block, owner, pair = lay((tokens, 1), 0)
    token_row, block_row, owner_row, pair_row = lay((1, tokens), 1)
    ahead = (
        (owner == owner_row)
        & (block_row < block)
        & (token_row >= query_total)
        & (token >= query_total)
    )
    before = jnp.sum(ahead.astype(jnp.float32), axis=-1, keepdims=True).astype(jnp.int32)
    local = jnp.where(
        token < query_total,
        token % query_rows,
        query_rows + before + (token - query_total) % BLK,
    )
    source = (zi ^ (owner // 4)) * 2 + (((owner // 2) % 2) ^ yi)
    pieces = 2 * nz
    spot = source * (full * 8) + local
    if halved:
        spot = jnp.where(
            local < full * 8, spot, pieces * full * 8 + source * 4 + local - full * 8
        )
    spot = spot + ((owner % 2) ^ ci) * plane_rows
    lanes = lax.broadcasted_iota(jnp.int32, (tokens, plane_rows), 1)
    pick_own = (lanes == spot).astype(jnp.bfloat16)
    pick_away = (lanes == spot - plane_rows).astype(jnp.bfloat16)
    packed = dot(pick_own, own_ref[...]) + dot(pick_away, away_ref[...])
    col_ref[...] = packed[:, 256 : 256 + width].astype(jnp.bfloat16)
    query, key, value = (
        packed[:, i * HDIM : (i + 1) * HDIM].astype(jnp.bfloat16) for i in range(3)
    )
    scores = by_rows(query, key) * HDIM ** (-0.5)
    scores = jnp.where(pair == pair_row, scores, -1e30)
    weights = jnp.exp(scores - jnp.max(scores, axis=-1, keepdims=True))
    probability = (weights / jnp.sum(weights, axis=-1, keepdims=True)).astype(jnp.bfloat16)
    context = dot(probability, value)
    ctx_ref[...] = jnp.concatenate(
        [context[: tokens // 2], context[tokens // 2 :]], axis=1
    ).astype(jnp.bfloat16)


def gate_kernel(rows_here, chunk_rows, *refs):
    count = len(refs) - 10
    pieces = refs[:count]
    (
        gain_ref,
        gate_ref,
        up_ref,
        share_ref,
        keep_ref,
        send_ref,
        kept_ref,
        kept_send_ref,
        order_ref,
        rows_ref,
    ) = refs[count:]
    _, zi, yi, ci = place()
    nz = lax.axis_size(AXIS) // 4
    tokens, width = pieces[0].shape
    half = 2 * nz * width
    total = order_ref.shape[0]
    slots = total // 2
    row = lax.broadcasted_iota(jnp.int32, (total, 1), 0)
    core = jnp.where(row < slots, ci, 1 - ci)
    chunk = (row % slots) // chunk_rows
    device = (zi ^ (chunk // 2)) * 4 + ((chunk % 2) ^ yi) * 2 + core
    wanted = device * rows_here + jnp.minimum(row % chunk_rows, rows_here - 1)
    lanes = lax.broadcasted_iota(jnp.int32, (total, tokens), 1)
    order_ref[...] = (lanes == wanted).astype(jnp.bfloat16)
    squares = jnp.zeros((total, 1), jnp.float32)
    for dz in range(nz):
        near, far = pieces[2 * dz][...], pieces[2 * dz + 1][...]
        pair = jnp.where(
            yi == 0,
            jnp.concatenate([near, far], axis=1),
            jnp.concatenate([far, near], axis=1),
        )
        start = pl.multiple_of((zi ^ dz) * (2 * width), 128)
        values = dot(order_ref[...], pair)
        squares = squares + jnp.sum(values * values, axis=-1, keepdims=True)
        kept_ref[:, pl.ds(start, 2 * width)] = values[0:chunk_rows].astype(jnp.bfloat16)
        kept_send_ref[:, pl.ds(start, 2 * width)] = values[slots : slots + chunk_rows].astype(
            jnp.bfloat16
        )
        gain = gain_ref[:, pl.ds(pl.multiple_of(ci * half + start, 128), 2 * width)]
        rows_ref[:, pl.ds(start, 2 * width)] = (values * gain).astype(jnp.bfloat16)
    mine = pl.ds(pl.multiple_of(ci * half, 128), half)
    rows = rows_ref[...]
    units = gate_ref.shape[0]
    gate = by_rows(rows, gate_ref[:, mine])
    up = by_rows(rows, up_ref[:, mine])
    gate_other = by_rows(rows, share_ref[:units, :half])
    up_other = by_rows(rows, share_ref[:units, half:])
    wide = keep_ref.shape[1] - 4 * units
    spread = jnp.broadcast_to(squares, (total, wide))
    keep_ref[...] = jnp.concatenate(
        [gate[:slots], gate_other[:slots], up[:slots], up_other[:slots], spread[:slots]], axis=1
    )
    send_ref[...] = jnp.concatenate(
        [gate_other[slots:], gate[slots:], up_other[slots:], up[slots:], spread[slots:]], axis=1
    )


def packed(rows):
    count, features = rows.shape
    groups = [rows[i : i + 8] for i in range(0, count // 8 * 8, 8)]
    first = count // 8 * 8
    for size in (4, 2, 1):
        if (count - first) & size:
            step = features * size // 8
            groups.append(
                jnp.concatenate(
                    [
                        rows[first : first + size, j * step : (j + 1) * step]
                        for j in range(8 // size)
                    ],
                    axis=0,
                )
            )
            first += size
    return jnp.concatenate(groups, axis=1) if len(groups) > 1 else groups[0]


def unpack(value, target):
    count, features = target.shape
    for i in range(count // 8):
        target[i * 8 : i * 8 + 8, :] = value[:, i * features : (i + 1) * features]
    first, lane = count // 8 * 8, count // 8 * features
    for size in (4, 2, 1):
        if (count - first) & size:
            step = features * size // 8
            for j in range(8 // size):
                target[first : first + size, j * step : (j + 1) * step] = value[
                    j * size : (j + 1) * size, lane : lane + step
                ]
            first, lane = first + size, lane + step


def hidden_kernel(features, chunk_rows, rows_here, keep_ref, came_ref, down_ref, share_ref, *refs):
    hidden_ref = refs[-1]
    units = down_ref.shape[0]
    summed = keep_ref[...] + came_ref[...]
    scale = lax.rsqrt(summed[:, 4 * units : 4 * units + 1] / features + 1e-06)
    gate = summed[:, 0 : 2 * units] * scale
    up = summed[:, 2 * units : 4 * units] * scale
    hidden = (jax.nn.gelu(gate, approximate=True) * up).astype(jnp.bfloat16)
    hidden_ref[...] = hidden
    far = jnp.concatenate(
        [
            hidden[(2 * dz + 1) * chunk_rows : (2 * dz + 2) * chunk_rows]
            for dz in range(len(refs) - 1)
        ],
        axis=0,
    )
    result = dot(far[:, :units], down_ref[...]) + dot(far[:, units:], share_ref[units:, :])
    for dz in range(len(refs) - 1):
        first = dz * chunk_rows
        refs[dz][...] = packed(result[first : first + rows_here]).astype(jnp.bfloat16)


def down_kernel(chunk_rows, rows_here, hidden_ref, down_ref, share_ref, *out_refs):
    units = down_ref.shape[0]
    hidden = hidden_ref[...]
    near = jnp.concatenate(
        [
            hidden[2 * dz * chunk_rows : (2 * dz + 1) * chunk_rows]
            for dz in range(len(out_refs))
        ],
        axis=0,
    )
    result = dot(near[:, :units], down_ref[...]) + dot(near[:, units:], share_ref[units:, :])
    for dz in range(len(out_refs)):
        first = dz * chunk_rows
        out_refs[dz][...] = packed(result[first : first + rows_here])


def add_kernel(near_ref, far_ref, out_ref):
    out_ref[...] = (near_ref[...] + far_ref[...].astype(jnp.float32)).astype(jnp.bfloat16)


def last_kernel(count, *refs):
    near_ref, far_ref = refs[0], refs[1]
    arrived = refs[2 : 2 + count]
    kept_ref, kept_other_ref, out_ref, total_ref = refs[2 + count :]
    ci = place()[3]
    rows = out_ref.shape[0]
    half = kept_ref.shape[1]
    kept, other = kept_ref[...].astype(jnp.float32), kept_other_ref[...].astype(jnp.float32)
    total = near_ref[...] + far_ref[...].astype(jnp.float32)
    for ref in arrived:
        total = total + ref[...].astype(jnp.float32)
    low, high = jnp.where(ci == 0, kept, other), jnp.where(ci == 0, other, kept)
    unpack(total, total_ref)
    out_ref[:, :half] = (low[:rows] + total_ref[:, :half]).astype(jnp.bfloat16)
    out_ref[:, half:] = (high[:rows] + total_ref[:, half:]).astype(jnp.bfloat16)


def body(
    queries,
    corpus,
    block_owner,
    slot_row,
    segment,
    query_weight,
    key_weight,
    value_weight,
    out_weight,
    gain_attn,
    gain_ffn,
    gate_weight,
    up_weight,
    down_weight,
):
    devices = lax.axis_size(AXIS)
    nz = devices // 4
    _, zi, yi, ci = place()
    z_order = list(range(nz - 1, 0, -1))

    def along_z(value, k):
        return lax.ppermute(value, AXIS, [(i, i ^ (4 * k)) for i in range(devices)])

    def across_y(value):
        return lax.ppermute(value, AXIS, [(i, i ^ 2) for i in range(devices)])

    def across_core(value):
        return lax.ppermute(value, AXIS, [(i, i ^ 1) for i in range(devices)])

    def plane_gather(value, value_across=None, fence=None):
        near = {0: value}
        for k in z_order:
            near[k] = along_z(value, k)
        if fence is not None:
            for k in near:
                near[k], fence = lax.optimization_barrier((near[k], fence))
        if value_across is None:
            value_across = near[0]
        return near, {
            k: across_y(near[k] if k else value_across) for k in [0] + z_order
        }

    def paired(near, far):
        return [piece for k in range(nz) for piece in (near[k], far[k])]

    owners = block_owner[:, 0]
    features = queries.shape[1]
    half = features // 2
    query_rows = queries.shape[0]
    tokens = query_rows * devices + owners.shape[0] * BLK
    width = features // devices
    heads_rows = query_weight.shape[0]
    units = gate_weight.shape[0]
    rows_here = tokens // devices
    chunk_rows = -(-rows_here // 16) * 16
    bf16, f32 = jnp.bfloat16, jnp.float32
    shape = jax.ShapeDtypeStruct

    full, halved = piece_layout(query_rows + CAP * BLK)
    piece = kernel_call(
        fetch_kernel,
        shape((8, full * features + halved * half), bf16),
        [SMEM, SMEM, ANY, VMEM],
        [
            pltpu.VMEM((CAP, BLK, features), bf16),
            pltpu.VMEM((full * 8 + halved * 8, features), f32),
            pltpu.SemaphoreType.DMA((CAP,)),
        ],
        name="fetch",
        limit=60 * 1024 * 1024,
    )(owners, slot_row, corpus, queries)

    projections = [query_weight, key_weight, value_weight]
    plane_rows = 2 * nz * (full * 8 + halved * 4)
    wide = 256 + -(-width // 128) * 128
    *tied, _ = lax.optimization_barrier((*projections, piece))
    stacked = kernel_call(
        stack_kernel,
        shape((3 * heads_rows, features), bf16),
        [VMEM] * 3,
        name="stack",
        micros=20,
    )(*tied)
    piece_wide = piece.shape[1]
    value_across = kernel_call(
        across_kernel,
        shape((8, piece_wide + heads_rows // 8 * 2 * nz * width), bf16),
        [VMEM] * 2,
        name="across",
    )(piece, out_weight)
    near, far = plane_gather(piece, value_across, stacked)
    projections_other = across_core(stacked)
    own, away = kernel_call(
        functools.partial(projection_kernel, query_rows + CAP * BLK),
        (shape((plane_rows, wide), bf16), shape((plane_rows, wide), bf16)),
        [VMEM] * (2 * nz + 5),
        [pltpu.VMEM((plane_rows, features), bf16)],
        name="project",
        micros=10,
    )(*paired(near, far), gain_attn[None, :], *projections, projections_other)

    out_keep, out_send = kernel_call(
        functools.partial(pair_kernel, piece_wide),
        (shape((2 * heads_rows, nz * width), bf16),) * 2,
        [VMEM] * 2,
        name="pairs",
    )(out_weight, far[0])
    out_came = across_core(out_send)

    context, columns = kernel_call(
        functools.partial(attention_kernel, query_rows, width),
        (shape((tokens // 2, 2 * HDIM), bf16), shape((tokens, width), bf16)),
        [SMEM, SMEM, VMEM, VMEM],
        name="attend",
    )(owners, segment, own, across_core(away))
    share_gate, share_up, share_down, _ = lax.optimization_barrier(
        (gate_weight, up_weight, down_weight, context)
    )
    share = across_core(
        kernel_call(
            share_kernel, shape((2 * units, features), bf16), [VMEM] * 3, name="share"
        )(share_gate, share_up, share_down)
    )

    contexts = jnp.concatenate([context, across_y(context)], axis=0)
    attended, *parts = kernel_call(
        out_kernel,
        (shape((tokens, width), f32),) + (shape((tokens, width), bf16),) * (nz - 1),
        [VMEM] * 4,
        name="out",
    )(contexts, across_core(contexts), out_keep, out_came)
    middle = columns.astype(f32) + attended
    for d in z_order:
        middle = middle + along_z(parts[d - 1], d).astype(f32)
    middle = middle.astype(bf16)

    slots = 2 * nz * chunk_rows
    lanes = -(-(4 * units + 1) // 128) * 128
    keep, send, kept, kept_send = kernel_call(
        functools.partial(gate_kernel, rows_here, chunk_rows),
        (
            shape((slots, lanes), f32),
            shape((slots, lanes), f32),
            shape((chunk_rows, half), bf16),
            shape((chunk_rows, half), bf16),
        ),
        [VMEM] * (2 * nz + 4),
        [pltpu.VMEM((2 * slots, tokens), bf16), pltpu.VMEM((2 * slots, half), bf16)],
        name="gate_up",
    )(*paired(*plane_gather(middle)), gain_ffn[None, :], gate_weight, up_weight, share)
    came = across_core(send)
    kept_other = across_core(kept_send)

    chunk = shape((8, rows_here * features // 8), bf16)
    *far, hidden = kernel_call(
        functools.partial(hidden_kernel, features, chunk_rows, rows_here),
        (chunk,) * nz + (shape((slots, 2 * units), bf16),),
        [VMEM] * 4,
        name="hidden",
    )(keep, came, down_weight, share)
    moved = {k: across_y(far[k]) for k in [*range(1, nz), 0]}
    near = kernel_call(
        functools.partial(down_kernel, chunk_rows, rows_here),
        (shape(chunk.shape, f32),) * nz,
        [VMEM] * 3,
        name="down",
    )(hidden, down_weight, share)
    arrived = []
    for k in range(1, nz):
        part = kernel_call(add_kernel, chunk, [VMEM, VMEM], name="add")(near[k], moved[k])
        arrived.append(along_z(part, k))
    return kernel_call(
        functools.partial(last_kernel, len(arrived)),
        shape((rows_here, features), bf16),
        [VMEM] * (len(arrived) + 4),
        [pltpu.VMEM((rows_here, features), f32)],
        name="last",
    )(near[0], moved[0], *arrived, kept, kept_other)


def solution(mesh):
    placed = (
        P(("groups", "tensor"), None),
        P(("groups", "tensor"), None, None),
        P("groups", None),
        P("groups"),
        P("groups"),
        P("tensor", None),
        P("tensor", None),
        P("tensor", None),
        P("tensor", None),
        P(),
        P(),
        P("tensor", None),
        P("tensor", None),
        P("tensor", None),
    )
    return jax.shard_map(
        body, mesh=mesh, in_specs=placed, out_specs=P(("groups", "tensor"), None), check_vma=False
    )
```

```python
import functools

import jax
import jax.numpy as jnp
from jax import lax
from jax.experimental import pallas as pl
from jax.experimental.pallas import tpu as pltpu
from jax.sharding import PartitionSpec as P

HDIM = 64
QLEN = 32
BLK = 4
CAP = 3
AXIS = "tensor"
VMEM_LIMIT = 28 * 1024 * 1024


def by_rows(left, weight):
    return lax.dot_general(
        left, weight, (((1,), (1,)), ((), ())), preferred_element_type=jnp.float32
    )


def dot(left, right):
    return jnp.dot(left, right, preferred_element_type=jnp.float32)


def place():
    me = lax.axis_index(AXIS)
    return me, me // 4, (me // 2) % 2, me % 2


def kernel_call(kernel, out_shape, in_specs, scratch=(), name=None, limit=VMEM_LIMIT, micros=1):
    return pl.pallas_call(
        kernel,
        out_shape=out_shape,
        cost_estimate=pl.CostEstimate(
            flops=micros * 1_000_000_000, bytes_accessed=micros * 3_000_000, transcendentals=0
        ),
        in_specs=in_specs,
        out_specs=jax.tree.map(lambda _: pl.BlockSpec(memory_space=pltpu.VMEM), out_shape),
        scratch_shapes=scratch,
        compiler_params=pltpu.CompilerParams(vmem_limit_bytes=limit),
        name=name,
    )


SMEM = pl.BlockSpec(memory_space=pltpu.SMEM)
VMEM = pl.BlockSpec(memory_space=pltpu.VMEM)
ANY = pl.BlockSpec(memory_space=pl.ANY)


def piece_layout(rows):
    full, rest = divmod(rows, 8)
    if 0 < rest <= 4:
        return full, True
    return full + (rest > 0), False


def fetch_kernel(owner_ref, row_ref, corpus_ref, query_ref, piece_ref, blocks, rows, sems):
    me = place()[0]
    features = query_ref.shape[1]
    query_rows = query_ref.shape[0]

    def look(b, carry):
        count, found = carry[0], carry[1:]
        mine = owner_ref[b] == me
        found = tuple(
            jnp.where(mine & (count == k), row_ref[b], found[k]) for k in range(CAP)
        )
        return (count + mine.astype(jnp.int32),) + found

    zero = jnp.int32(0)
    found = lax.fori_loop(0, owner_ref.shape[0], look, (zero,) * (CAP + 1))[1:]
    copies = [
        pltpu.make_async_copy(corpus_ref.at[found[k]], blocks.at[k], sems.at[k])
        for k in range(CAP)
    ]
    for copy in copies:
        copy.start()
    total = query_rows + CAP * BLK
    full, halved = piece_layout(total)
    rows[0:query_rows, :] = query_ref[...].astype(jnp.float32)
    for k in range(CAP):
        copies[k].wait()
        first = query_rows + k * BLK
        rows[first : first + BLK, :] = blocks[k].astype(jnp.float32)
    if not halved and total < full * 8:
        rows[total : full * 8, :] = jnp.zeros((full * 8 - total, features), jnp.float32)
    for i in range(full):
        piece_ref[:, i * features : (i + 1) * features] = rows[i * 8 : i * 8 + 8, :].astype(
            jnp.bfloat16
        )
    if halved:
        half = features // 2
        last = rows[full * 8 : full * 8 + 4, :]
        if total % 8 < 4:
            last = jnp.where(
                lax.broadcasted_iota(jnp.int32, last.shape, 0) < total % 8, last, 0.0
            )
        piece_ref[:, full * features :] = jnp.concatenate(
            [last[:, :half], last[:, half:]], axis=0
        ).astype(jnp.bfloat16)


def columns_at(ref, start, width):
    if width % 128 == 0:
        return ref[:, pl.ds(pl.multiple_of(start, 128), width)].astype(jnp.float32)
    base = pl.multiple_of(start // 128 * 128, 128)
    window = ref[:, pl.ds(base, 128)].astype(jnp.float32)
    return pltpu.roll(window, (128 - start % 128) % 128, 1)[:, :width]


def across_kernel(piece_ref, weight_ref, out_ref):
    _, zi, yi, _ = place()
    nz = lax.axis_size(AXIS) // 4
    rows, features = weight_ref.shape
    width = features // (4 * nz)
    first = piece_ref.shape[1]
    wide = 2 * nz * width
    out_ref[:, :first] = piece_ref[...]
    columns = jnp.concatenate(
        [
            columns_at(
                weight_ref, core * (features // 2) + (2 * (zi ^ d) + 1 - yi) * width, width
            )
            for d in range(nz)
            for core in range(2)
        ],
        axis=1,
    )
    for g in range(rows // 8):
        out_ref[:, first + g * wide : first + (g + 1) * wide] = columns[
            g * 8 : g * 8 + 8
        ].astype(jnp.bfloat16)


def pair_kernel(first, weight_ref, far_ref, keep_ref, send_ref):
    _, zi, yi, ci = place()
    rows, features = weight_ref.shape
    nz = lax.axis_size(AXIS) // 4
    width = features // (4 * nz)
    wide = 2 * nz * width
    for core, out_ref in ((ci, keep_ref), (1 - ci, send_ref)):
        own = [
            columns_at(
                weight_ref, core * (features // 2) + (2 * (zi ^ d) + yi) * width, width
            )
            for d in range(nz)
        ]
        out_ref[:rows, :] = jnp.concatenate(own, axis=1).astype(jnp.bfloat16)
        groups = []
        for g in range(rows // 8):
            parts = []
            for d in range(nz):
                start = first + g * wide + 2 * d * width
                both = far_ref[:, start : start + 2 * width].astype(jnp.float32)
                parts.append(jnp.where(core == 0, both[:, :width], both[:, width:]))
            groups.append(jnp.concatenate(parts, axis=1))
        out_ref[rows:, :] = jnp.concatenate(groups, axis=0).astype(jnp.bfloat16)


def stack_kernel(*refs):
    rows = refs[0].shape[0]
    for i, ref in enumerate(refs[:-1]):
        refs[-1][i * rows : (i + 1) * rows, :] = ref[...]


def share_kernel(gate_ref, up_ref, down_ref, out_ref):
    units, features = down_ref.shape
    half = features // 2
    other = pl.ds(pl.multiple_of((1 - place()[3]) * half, 128), half)
    out_ref[:units, :half] = gate_ref[:, other]
    out_ref[:units, half:] = up_ref[:, other]
    out_ref[units:, :] = down_ref[...]


def out_kernel(*refs):
    near_ref, far_ref, other_ref, other_far_ref, weight_ref, weight_other_ref, mine_ref = refs[:7]
    send_refs = refs[7:]
    width = mine_ref.shape[1]

    def heads(near_ref, far_ref):
        near, far = near_ref[...], far_ref[...]
        return jnp.concatenate(
            [
                jnp.concatenate([near[:, :HDIM], far[:, :HDIM]], axis=1),
                jnp.concatenate([near[:, HDIM:], far[:, HDIM:]], axis=1),
            ],
            axis=0,
        )

    attended = dot(heads(near_ref, far_ref), weight_ref[...]) + dot(
        heads(other_ref, other_far_ref), weight_other_ref[...]
    )
    mine_ref[...] = attended[:, :width]
    for d, ref in enumerate(send_refs, 1):
        ref[...] = attended[:, d * width : (d + 1) * width].astype(jnp.bfloat16)


def projection_kernel(piece_rows, *refs):
    count = len(refs) - 8
    pieces, rest = refs[:count], refs[count:]
    gain_ref, *mine, other_ref, out_ref, out_other_ref, normal = rest
    _, zi, yi, ci = place()
    features = gain_ref.shape[1]
    half = features // 2
    full, halved = piece_layout(piece_rows)
    width = features // lax.axis_size(AXIS)
    chip = 2 * zi + yi
    gain = gain_ref[...]
    spot = 256
    own_column = ci * half + chip * width
    other_column = (1 - ci) * half + chip * width

    def scaled(values, squares):
        return values * lax.rsqrt(squares / features + 1e-06)

    def put(row, groups):
        normal[row : row + 16, :] = jnp.concatenate(groups, axis=0).astype(jnp.bfloat16)

    chunks = [(p, i) for p in range(count) for i in range(full)]
    for first in range(0, len(chunks), 2):
        groups, own, away = [], [], []
        for p, i in chunks[first : first + 2]:
            values = pieces[p][:, i * features : (i + 1) * features].astype(jnp.float32)
            squares = jnp.sum(values * values, axis=-1, keepdims=True)
            groups.append(scaled(values, squares) * gain)
            own.append(columns_at(pieces[p], i * features + own_column, width))
            away.append(columns_at(pieces[p], i * features + other_column, width))
        row = first * 8
        put(row, groups)
        out_ref[row : row + 16, spot : spot + width] = jnp.concatenate(own, axis=0).astype(
            jnp.bfloat16
        )
        out_other_ref[row : row + 16, spot : spot + width] = jnp.concatenate(
            away, axis=0
        ).astype(jnp.bfloat16)
    if halved:
        for first in range(0, count, 4):
            groups, own, away = [], [], []
            for p in range(first, first + 4, 2):
                a, b = (
                    pieces[q][:, full * features : full * features + half].astype(jnp.float32)
                    for q in (p, p + 1)
                )
                low = jnp.concatenate([a[0:4], b[0:4]], axis=0)
                high = jnp.concatenate([a[4:8], b[4:8]], axis=0)
                squares = jnp.sum(low * low, axis=-1, keepdims=True) + jnp.sum(
                    high * high, axis=-1, keepdims=True
                )
                groups.append(
                    jnp.concatenate([scaled(low, squares), scaled(high, squares)], axis=1)
                    * gain
                )
                a, b = (
                    columns_at(pieces[q], full * features + chip * width, width)
                    for q in (p, p + 1)
                )
                low = jnp.concatenate([a[0:4], b[0:4]], axis=0)
                high = jnp.concatenate([a[4:8], b[4:8]], axis=0)
                own.append(jnp.where(ci == 0, low, high))
                away.append(jnp.where(ci == 0, high, low))
            row = len(chunks) * 8 + first * 4
            put(row, groups)
            out_ref[row : row + 16, spot : spot + width] = jnp.concatenate(
                own, axis=0
            ).astype(jnp.bfloat16)
            out_other_ref[row : row + 16, spot : spot + width] = jnp.concatenate(
                away, axis=0
            ).astype(jnp.bfloat16)
    rows = normal[...]
    for target, weights in ((out_other_ref, [other_ref]), (out_ref, mine)):
        value = jnp.concatenate([by_rows(rows, w[...]) for w in weights], axis=1)
        target[:, 0 : value.shape[1]] = value.astype(jnp.bfloat16)


def plan_kernel(query_rows, owner_ref, segment_ref, own_ref, away_ref, mask_ref):
    _, zi, yi, ci = place()
    nz = lax.axis_size(AXIS) // 4
    query_total = query_rows * 4 * nz
    blocks_total = owner_ref.shape[0]
    tokens = query_total + blocks_total * BLK
    piece_rows = query_rows + CAP * BLK
    full, halved = piece_layout(piece_rows)
    plane_rows = own_ref.shape[1]

    def lay(shape, axis):
        token = lax.broadcasted_iota(jnp.int32, shape, axis)
        block = (token - query_total) // BLK
        is_query = token < query_total
        owner = jnp.where(is_query, token // query_rows, 0)
        pair = jnp.where(is_query, token // QLEN, 0)

        def fill(b, carry):
            here = (block == b) & (token >= query_total)
            return (
                jnp.where(here, owner_ref[b], carry[0]),
                jnp.where(here, segment_ref[b], carry[1]),
            )

        owner, pair = lax.fori_loop(0, blocks_total, fill, (owner, pair))
        return token, block, owner, pair

    token, block, owner, pair = lay((tokens, 1), 0)
    token_row, block_row, owner_row, pair_row = lay((1, tokens), 1)
    ahead = (
        (owner == owner_row)
        & (block_row < block)
        & (token_row >= query_total)
        & (token >= query_total)
    )
    before = jnp.sum(ahead.astype(jnp.float32), axis=-1, keepdims=True).astype(jnp.int32)
    local = jnp.where(
        token < query_total,
        token % query_rows,
        query_rows + before + (token - query_total) % BLK,
    )
    source = (zi ^ (owner // 4)) * 2 + (((owner // 2) % 2) ^ yi)
    pieces = 2 * nz
    spot = source * (full * 8) + local
    if halved:
        spot = jnp.where(
            local < full * 8, spot, pieces * full * 8 + source * 4 + local - full * 8
        )
    spot = spot + ((owner % 2) ^ ci) * plane_rows
    lanes = lax.broadcasted_iota(jnp.int32, (tokens, plane_rows), 1)
    own_ref[...] = (lanes == spot).astype(jnp.bfloat16)
    away_ref[...] = (lanes == spot - plane_rows).astype(jnp.bfloat16)
    mask_ref[...] = (pair == pair_row).astype(jnp.float32)


def attention_kernel(width, pick_ref, pick_away_ref, mask_ref, own_ref, away_ref, ctx_ref, col_ref):
    tokens = pick_ref.shape[0]
    packed = dot(pick_ref[...], own_ref[...]) + dot(pick_away_ref[...], away_ref[...])
    col_ref[...] = packed[:, 256 : 256 + width].astype(jnp.bfloat16)
    query, key, value = (
        packed[:, i * HDIM : (i + 1) * HDIM].astype(jnp.bfloat16) for i in range(3)
    )
    scores = by_rows(query, key) * HDIM ** (-0.5)
    scores = jnp.where(mask_ref[...] > 0.5, scores, -1e30)
    weights = jnp.exp(scores - jnp.max(scores, axis=-1, keepdims=True))
    probability = (weights / jnp.sum(weights, axis=-1, keepdims=True)).astype(jnp.bfloat16)
    context = dot(probability, value)
    ctx_ref[...] = jnp.concatenate(
        [context[: tokens // 2], context[tokens // 2 :]], axis=1
    ).astype(jnp.bfloat16)


def gate_kernel(rows_here, chunk_rows, own, *refs):
    count = len(refs) - 8
    pieces = refs[:count]
    (
        gain_ref,
        gate_ref,
        up_ref,
        share_ref,
        out_ref,
        kept_ref,
        order_ref,
        rows_ref,
    ) = refs[count:]
    _, zi, yi, ci = place()
    nz = lax.axis_size(AXIS) // 4
    tokens, width = pieces[0].shape
    half = 2 * nz * width
    total = order_ref.shape[0]
    row = lax.broadcasted_iota(jnp.int32, (total, 1), 0)
    core = ci if own else 1 - ci
    chunk = row // chunk_rows
    device = (zi ^ (chunk // 2)) * 4 + ((chunk % 2) ^ yi) * 2 + core
    wanted = device * rows_here + jnp.minimum(row % chunk_rows, rows_here - 1)
    lanes = lax.broadcasted_iota(jnp.int32, (total, tokens), 1)
    order_ref[...] = (lanes == wanted).astype(jnp.bfloat16)
    squares = jnp.zeros((total, 1), jnp.float32)
    for dz in range(nz):
        near, far = pieces[2 * dz][...], pieces[2 * dz + 1][...]
        pair = jnp.where(
            yi == 0,
            jnp.concatenate([near, far], axis=1),
            jnp.concatenate([far, near], axis=1),
        )
        start = pl.multiple_of((zi ^ dz) * (2 * width), 128)
        values = dot(order_ref[...], pair)
        squares = squares + jnp.sum(values * values, axis=-1, keepdims=True)
        kept_ref[:, pl.ds(start, 2 * width)] = values[0:chunk_rows].astype(jnp.bfloat16)
        gain = gain_ref[:, pl.ds(pl.multiple_of(ci * half + start, 128), 2 * width)]
        rows_ref[:, pl.ds(start, 2 * width)] = (values * gain).astype(jnp.bfloat16)
    mine = pl.ds(pl.multiple_of(ci * half, 128), half)
    rows = rows_ref[...]
    units = gate_ref.shape[0]
    gate = by_rows(rows, gate_ref[:, mine])
    up = by_rows(rows, up_ref[:, mine])
    gate_other = by_rows(rows, share_ref[:units, :half])
    up_other = by_rows(rows, share_ref[:units, half:])
    spread = jnp.broadcast_to(squares, (total, out_ref.shape[1] - 4 * units))
    parts = (gate, gate_other, up, up_other) if own else (gate_other, gate, up_other, up)
    out_ref[...] = jnp.concatenate([*parts, spread], axis=1)


def packed(rows):
    count, features = rows.shape
    groups = [rows[i : i + 8] for i in range(0, count // 8 * 8, 8)]
    first = count // 8 * 8
    for size in (4, 2, 1):
        if (count - first) & size:
            step = features * size // 8
            groups.append(
                jnp.concatenate(
                    [
                        rows[first : first + size, j * step : (j + 1) * step]
                        for j in range(8 // size)
                    ],
                    axis=0,
                )
            )
            first += size
    return jnp.concatenate(groups, axis=1) if len(groups) > 1 else groups[0]


def unpack(value, target):
    count, features = target.shape
    for i in range(count // 8):
        target[i * 8 : i * 8 + 8, :] = value[:, i * features : (i + 1) * features]
    first, lane = count // 8 * 8, count // 8 * features
    for size in (4, 2, 1):
        if (count - first) & size:
            step = features * size // 8
            for j in range(8 // size):
                target[first : first + size, j * step : (j + 1) * step] = value[
                    j * size : (j + 1) * size, lane : lane + step
                ]
            first, lane = first + size, lane + step


def hidden_kernel(features, chunk_rows, rows_here, keep_ref, came_ref, down_ref, share_ref, *refs):
    hidden_ref = refs[-1]
    units = down_ref.shape[0]
    summed = keep_ref[...] + came_ref[...]
    scale = lax.rsqrt(summed[:, 4 * units : 4 * units + 1] / features + 1e-06)
    gate = summed[:, 0 : 2 * units] * scale
    up = summed[:, 2 * units : 4 * units] * scale
    hidden = (jax.nn.gelu(gate, approximate=True) * up).astype(jnp.bfloat16)
    hidden_ref[...] = hidden
    far = jnp.concatenate(
        [
            hidden[(2 * dz + 1) * chunk_rows : (2 * dz + 2) * chunk_rows]
            for dz in range(len(refs) - 1)
        ],
        axis=0,
    )
    result = dot(far[:, :units], down_ref[...]) + dot(far[:, units:], share_ref[units:, :])
    for dz in range(len(refs) - 1):
        first = dz * chunk_rows
        refs[dz][...] = packed(result[first : first + rows_here]).astype(jnp.bfloat16)


def down_kernel(chunk_rows, rows_here, hidden_ref, down_ref, share_ref, *out_refs):
    units = down_ref.shape[0]
    hidden = hidden_ref[...]
    near = jnp.concatenate(
        [
            hidden[2 * dz * chunk_rows : (2 * dz + 1) * chunk_rows]
            for dz in range(len(out_refs))
        ],
        axis=0,
    )
    result = dot(near[:, :units], down_ref[...]) + dot(near[:, units:], share_ref[units:, :])
    for dz in range(len(out_refs)):
        first = dz * chunk_rows
        out_refs[dz][...] = packed(result[first : first + rows_here])


def add_kernel(near_ref, far_ref, out_ref):
    out_ref[...] = (near_ref[...] + far_ref[...].astype(jnp.float32)).astype(jnp.bfloat16)


def last_kernel(count, *refs):
    near_ref, far_ref = refs[0], refs[1]
    arrived = refs[2 : 2 + count]
    kept_ref, kept_other_ref, out_ref, total_ref = refs[2 + count :]
    ci = place()[3]
    rows = out_ref.shape[0]
    half = kept_ref.shape[1]
    kept, other = kept_ref[...].astype(jnp.float32), kept_other_ref[...].astype(jnp.float32)
    total = near_ref[...] + far_ref[...].astype(jnp.float32)
    for ref in arrived:
        total = total + ref[...].astype(jnp.float32)
    low, high = jnp.where(ci == 0, kept, other), jnp.where(ci == 0, other, kept)
    unpack(total, total_ref)
    out_ref[:, :half] = (low[:rows] + total_ref[:, :half]).astype(jnp.bfloat16)
    out_ref[:, half:] = (high[:rows] + total_ref[:, half:]).astype(jnp.bfloat16)


def body(
    queries,
    corpus,
    block_owner,
    slot_row,
    segment,
    query_weight,
    key_weight,
    value_weight,
    out_weight,
    gain_attn,
    gain_ffn,
    gate_weight,
    up_weight,
    down_weight,
):
    devices = lax.axis_size(AXIS)
    nz = devices // 4
    _, zi, yi, ci = place()
    z_order = list(range(nz - 1, 0, -1))

    def along_z(value, k):
        return lax.ppermute(value, AXIS, [(i, i ^ (4 * k)) for i in range(devices)])

    def across_y(value):
        return lax.ppermute(value, AXIS, [(i, i ^ 2) for i in range(devices)])

    def across_core(value):
        return lax.ppermute(value, AXIS, [(i, i ^ 1) for i in range(devices)])

    def plane_gather(value, value_across=None, fence=None):
        near = {0: value}
        for k in z_order:
            near[k] = along_z(value, k)
        if fence is not None:
            for k in near:
                near[k], fence = lax.optimization_barrier((near[k], fence))
        if value_across is None:
            value_across = near[0]
        return near, {
            k: across_y(near[k] if k else value_across) for k in [0] + z_order
        }

    def paired(near, far):
        return [piece for k in range(nz) for piece in (near[k], far[k])]

    owners = block_owner[:, 0]
    features = queries.shape[1]
    half = features // 2
    query_rows = queries.shape[0]
    tokens = query_rows * devices + owners.shape[0] * BLK
    width = features // devices
    heads_rows = query_weight.shape[0]
    units = gate_weight.shape[0]
    rows_here = tokens // devices
    chunk_rows = -(-rows_here // 16) * 16
    bf16, f32 = jnp.bfloat16, jnp.float32
    shape = jax.ShapeDtypeStruct

    full, halved = piece_layout(query_rows + CAP * BLK)
    piece = kernel_call(
        fetch_kernel,
        shape((8, full * features + halved * half), bf16),
        [SMEM, SMEM, ANY, VMEM],
        [
            pltpu.VMEM((CAP, BLK, features), bf16),
            pltpu.VMEM((full * 8 + halved * 8, features), f32),
            pltpu.SemaphoreType.DMA((CAP,)),
        ],
        name="fetch",
        limit=60 * 1024 * 1024,
    )(owners, slot_row, corpus, queries)

    projections = [query_weight, key_weight, value_weight]
    plane_rows = 2 * nz * (full * 8 + halved * 4)
    wide = 256 + -(-width // 128) * 128
    *tied, _ = lax.optimization_barrier((*projections, piece))
    stacked = kernel_call(
        stack_kernel,
        shape((3 * heads_rows, features), bf16),
        [VMEM] * 3,
        name="stack",
        micros=20,
    )(*tied)
    piece_wide = piece.shape[1]
    value_across = kernel_call(
        across_kernel,
        shape((8, piece_wide + heads_rows // 8 * 2 * nz * width), bf16),
        [VMEM] * 2,
        name="across",
    )(piece, out_weight)
    near, far = plane_gather(piece, value_across, stacked)
    projections_other = across_core(stacked)
    own, away = kernel_call(
        functools.partial(projection_kernel, query_rows + CAP * BLK),
        (shape((plane_rows, wide), bf16), shape((plane_rows, wide), bf16)),
        [VMEM] * (2 * nz + 5),
        [pltpu.VMEM((plane_rows, features), bf16)],
        name="project",
        micros=10,
    )(*paired(near, far), gain_attn[None, :], *projections, projections_other)

    out_keep, out_send = kernel_call(
        functools.partial(pair_kernel, piece_wide),
        (shape((2 * heads_rows, nz * width), bf16),) * 2,
        [VMEM] * 2,
        name="pairs",
    )(out_weight, far[0])
    out_came = across_core(out_send)
    own, out_came = lax.optimization_barrier((own, out_came))

    plan = kernel_call(
        functools.partial(plan_kernel, query_rows),
        (
            shape((tokens, plane_rows), bf16),
            shape((tokens, plane_rows), bf16),
            shape((tokens, tokens), f32),
        ),
        [SMEM, SMEM],
        name="plan",
    )(owners, segment)
    context, columns = kernel_call(
        functools.partial(attention_kernel, width),
        (shape((tokens // 2, 2 * HDIM), bf16), shape((tokens, width), bf16)),
        [VMEM] * 5,
        name="attend",
    )(*plan, own, across_core(away))
    contexts = [
        context,
        across_y(context),
        across_core(context),
        lax.ppermute(context, AXIS, [(i, i ^ 3) for i in range(devices)]),
    ]
    attended, *parts = kernel_call(
        out_kernel,
        (shape((tokens, width), f32),) + (shape((tokens, width), bf16),) * (nz - 1),
        [VMEM] * 6,
        name="out",
    )(*contexts, out_keep, out_came)
    middle = columns.astype(f32) + attended
    for d in z_order:
        middle = middle + along_z(parts[d - 1], d).astype(f32)
    middle = middle.astype(bf16)
    share_gate, share_up, share_down, _ = lax.optimization_barrier(
        (gate_weight, up_weight, down_weight, middle)
    )
    share = across_core(
        kernel_call(
            share_kernel, shape((2 * units, features), bf16), [VMEM] * 3, name="share"
        )(share_gate, share_up, share_down)
    )


    slots = 2 * nz * chunk_rows
    lanes = -(-(4 * units + 1) // 128) * 128
    blocks = paired(*plane_gather(middle))

    def gate_up(own, blocks):
        return kernel_call(
            functools.partial(gate_kernel, rows_here, chunk_rows, own),
            (shape((slots, lanes), f32), shape((chunk_rows, half), bf16)),
            [VMEM] * (2 * nz + 4),
            [pltpu.VMEM((slots, tokens), bf16), pltpu.VMEM((slots, half), bf16)],
            name="gate_up_own" if own else "gate_up",
        )(*blocks, gain_ffn[None, :], gate_weight, up_weight, share)

    send, kept_send = gate_up(False, blocks)
    first, _ = lax.optimization_barrier((blocks[0], send))
    keep, kept = gate_up(True, [first, *blocks[1:]])
    came = across_core(send)
    kept_other = across_core(kept_send)

    chunk = shape((8, rows_here * features // 8), bf16)
    *far, hidden = kernel_call(
        functools.partial(hidden_kernel, features, chunk_rows, rows_here),
        (chunk,) * nz + (shape((slots, 2 * units), bf16),),
        [VMEM] * 4,
        name="hidden",
    )(keep, came, down_weight, share)
    moved = {k: across_y(far[k]) for k in [*range(1, nz), 0]}
    near = kernel_call(
        functools.partial(down_kernel, chunk_rows, rows_here),
        (shape(chunk.shape, f32),) * nz,
        [VMEM] * 3,
        name="down",
    )(hidden, down_weight, share)
    arrived = []
    for k in range(1, nz):
        part = kernel_call(add_kernel, chunk, [VMEM, VMEM], name="add")(near[k], moved[k])
        arrived.append(along_z(part, k))
    return kernel_call(
        functools.partial(last_kernel, len(arrived)),
        shape((rows_here, features), bf16),
        [VMEM] * (len(arrived) + 4),
        [pltpu.VMEM((rows_here, features), f32)],
        name="last",
    )(near[0], moved[0], *arrived, kept, kept_other)


def solution(mesh):
    placed = (
        P(("groups", "tensor"), None),
        P(("groups", "tensor"), None, None),
        P("groups", None),
        P("groups"),
        P("groups"),
        P("tensor", None),
        P("tensor", None),
        P("tensor", None),
        P("tensor", None),
        P(),
        P(),
        P("tensor", None),
        P("tensor", None),
        P("tensor", None),
    )
    return jax.shard_map(
        body, mesh=mesh, in_specs=placed, out_specs=P(("groups", "tensor"), None), check_vma=False
    )
```

```python
import functools

import jax
import jax.numpy as jnp
from jax import lax
from jax.experimental import pallas as pl
from jax.experimental.pallas import tpu as pltpu
from jax.sharding import PartitionSpec as P

HDIM = 64
QLEN = 32
BLK = 4
CAP = 3
AXIS = "tensor"
VMEM_LIMIT = 28 * 1024 * 1024


def by_rows(left, weight):
    return lax.dot_general(
        left, weight, (((1,), (1,)), ((), ())), preferred_element_type=jnp.float32
    )


def dot(left, right):
    return jnp.dot(left, right, preferred_element_type=jnp.float32)


def place():
    me = lax.axis_index(AXIS)
    return me, me // 4, (me // 2) % 2, me % 2


def kernel_call(kernel, out_shape, in_specs, scratch=(), name=None, limit=VMEM_LIMIT, micros=1):
    return pl.pallas_call(
        kernel,
        out_shape=out_shape,
        cost_estimate=pl.CostEstimate(
            flops=micros * 1_000_000_000, bytes_accessed=micros * 3_000_000, transcendentals=0
        ),
        in_specs=in_specs,
        out_specs=jax.tree.map(lambda _: pl.BlockSpec(memory_space=pltpu.VMEM), out_shape),
        scratch_shapes=scratch,
        compiler_params=pltpu.CompilerParams(vmem_limit_bytes=limit),
        name=name,
    )


SMEM = pl.BlockSpec(memory_space=pltpu.SMEM)
VMEM = pl.BlockSpec(memory_space=pltpu.VMEM)
ANY = pl.BlockSpec(memory_space=pl.ANY)


def piece_layout(rows):
    full, rest = divmod(rows, 8)
    if 0 < rest <= 4:
        return full, True
    return full + (rest > 0), False


def fetch_kernel(owner_ref, row_ref, corpus_ref, query_ref, piece_ref, blocks, query, rows, sems):
    me = place()[0]
    query_copy = pltpu.make_async_copy(query_ref, query, sems.at[CAP])
    query_copy.start()
    features = query_ref.shape[1]
    query_rows = query_ref.shape[0]

    def look(b, carry):
        count, found = carry[0], carry[1:]
        mine = owner_ref[b] == me
        found = tuple(
            jnp.where(mine & (count == k), row_ref[b], found[k]) for k in range(CAP)
        )
        return (count + mine.astype(jnp.int32),) + found

    zero = jnp.int32(0)
    found = lax.fori_loop(0, owner_ref.shape[0], look, (zero,) * (CAP + 1))[1:]
    copies = [
        pltpu.make_async_copy(corpus_ref.at[found[k]], blocks.at[k], sems.at[k])
        for k in range(CAP)
    ]
    for copy in copies:
        copy.start()
    total = query_rows + CAP * BLK
    full, halved = piece_layout(total)
    query_copy.wait()
    rows[0:query_rows, :] = query[...].astype(jnp.float32)
    for k in range(CAP):
        copies[k].wait()
        first = query_rows + k * BLK
        rows[first : first + BLK, :] = blocks[k].astype(jnp.float32)
    if not halved and total < full * 8:
        rows[total : full * 8, :] = jnp.zeros((full * 8 - total, features), jnp.float32)
    for i in range(full):
        piece_ref[:, i * features : (i + 1) * features] = rows[i * 8 : i * 8 + 8, :].astype(
            jnp.bfloat16
        )
    if halved:
        half = features // 2
        last = rows[full * 8 : full * 8 + 4, :]
        if total % 8 < 4:
            last = jnp.where(
                lax.broadcasted_iota(jnp.int32, last.shape, 0) < total % 8, last, 0.0
            )
        piece_ref[:, full * features :] = jnp.concatenate(
            [last[:, :half], last[:, half:]], axis=0
        ).astype(jnp.bfloat16)


def columns_at(ref, start, width):
    if width % 128 == 0:
        return ref[:, pl.ds(pl.multiple_of(start, 128), width)].astype(jnp.float32)
    base = pl.multiple_of(start // 128 * 128, 128)
    window = ref[:, pl.ds(base, 128)].astype(jnp.float32)
    return pltpu.roll(window, (128 - start % 128) % 128, 1)[:, :width]


def across_kernel(piece_ref, weight_ref, out_ref):
    _, zi, yi, _ = place()
    nz = lax.axis_size(AXIS) // 4
    rows, features = weight_ref.shape
    width = features // (4 * nz)
    first = piece_ref.shape[1]
    wide = 2 * nz * width
    out_ref[:, :first] = piece_ref[...]
    columns = jnp.concatenate(
        [
            columns_at(
                weight_ref, core * (features // 2) + (2 * (zi ^ d) + 1 - yi) * width, width
            )
            for d in range(nz)
            for core in range(2)
        ],
        axis=1,
    )
    for g in range(rows // 8):
        out_ref[:, first + g * wide : first + (g + 1) * wide] = columns[
            g * 8 : g * 8 + 8
        ].astype(jnp.bfloat16)


def pair_kernel(first, weight_ref, far_ref, keep_ref, send_ref):
    _, zi, yi, ci = place()
    rows, features = weight_ref.shape
    nz = lax.axis_size(AXIS) // 4
    width = features // (4 * nz)
    wide = 2 * nz * width
    for core, out_ref in ((ci, keep_ref), (1 - ci, send_ref)):
        own = [
            columns_at(
                weight_ref, core * (features // 2) + (2 * (zi ^ d) + yi) * width, width
            )
            for d in range(nz)
        ]
        out_ref[:rows, :] = jnp.concatenate(own, axis=1).astype(jnp.bfloat16)
        groups = []
        for g in range(rows // 8):
            parts = []
            for d in range(nz):
                start = first + g * wide + 2 * d * width
                both = far_ref[:, start : start + 2 * width].astype(jnp.float32)
                parts.append(jnp.where(core == 0, both[:, :width], both[:, width:]))
            groups.append(jnp.concatenate(parts, axis=1))
        out_ref[rows:, :] = jnp.concatenate(groups, axis=0).astype(jnp.bfloat16)


def stack_kernel(*refs):
    rows = refs[0].shape[0]
    for i, ref in enumerate(refs[:-1]):
        refs[-1][i * rows : (i + 1) * rows, :] = ref[...]


def share_kernel(gate_ref, up_ref, down_ref, out_ref):
    units, features = down_ref.shape
    half = features // 2
    other = pl.ds(pl.multiple_of((1 - place()[3]) * half, 128), half)
    out_ref[:units, :half] = gate_ref[:, other]
    out_ref[:units, half:] = up_ref[:, other]
    out_ref[units:, :] = down_ref[...]


def out_kernel(*refs):
    near_ref, far_ref, other_ref, other_far_ref, weight_ref, weight_other_ref, mine_ref = refs[:7]
    send_refs = refs[7:]
    width = mine_ref.shape[1]

    def heads(near_ref, far_ref):
        near, far = near_ref[...], far_ref[...]
        return jnp.concatenate(
            [
                jnp.concatenate([near[:, :HDIM], far[:, :HDIM]], axis=1),
                jnp.concatenate([near[:, HDIM:], far[:, HDIM:]], axis=1),
            ],
            axis=0,
        )

    attended = dot(heads(near_ref, far_ref), weight_ref[...]) + dot(
        heads(other_ref, other_far_ref), weight_other_ref[...]
    )
    mine_ref[...] = attended[:, :width]
    for d, ref in enumerate(send_refs, 1):
        ref[...] = attended[:, d * width : (d + 1) * width].astype(jnp.bfloat16)


def projection_kernel(piece_rows, *refs):
    count = len(refs) - 8
    pieces, rest = refs[:count], refs[count:]
    gain_ref, *mine, other_ref, out_ref, out_other_ref, normal = rest
    _, zi, yi, ci = place()
    features = gain_ref.shape[1]
    half = features // 2
    full, halved = piece_layout(piece_rows)
    width = features // lax.axis_size(AXIS)
    chip = 2 * zi + yi
    gain = gain_ref[...]
    spot = 256
    own_column = ci * half + chip * width
    other_column = (1 - ci) * half + chip * width

    def scaled(values, squares):
        return values * lax.rsqrt(squares / features + 1e-06)

    def put(row, groups):
        normal[row : row + 16, :] = jnp.concatenate(groups, axis=0).astype(jnp.bfloat16)

    chunks = [(p, i) for p in range(count) for i in range(full)]
    for first in range(0, len(chunks), 2):
        groups, own, away = [], [], []
        for p, i in chunks[first : first + 2]:
            values = pieces[p][:, i * features : (i + 1) * features].astype(jnp.float32)
            squares = jnp.sum(values * values, axis=-1, keepdims=True)
            groups.append(scaled(values, squares) * gain)
            own.append(columns_at(pieces[p], i * features + own_column, width))
            away.append(columns_at(pieces[p], i * features + other_column, width))
        row = first * 8
        put(row, groups)
        out_ref[row : row + 16, spot : spot + width] = jnp.concatenate(own, axis=0).astype(
            jnp.bfloat16
        )
        out_other_ref[row : row + 16, spot : spot + width] = jnp.concatenate(
            away, axis=0
        ).astype(jnp.bfloat16)
    if halved:
        for first in range(0, count, 4):
            groups, own, away = [], [], []
            for p in range(first, first + 4, 2):
                a, b = (
                    pieces[q][:, full * features : full * features + half].astype(jnp.float32)
                    for q in (p, p + 1)
                )
                low = jnp.concatenate([a[0:4], b[0:4]], axis=0)
                high = jnp.concatenate([a[4:8], b[4:8]], axis=0)
                squares = jnp.sum(low * low, axis=-1, keepdims=True) + jnp.sum(
                    high * high, axis=-1, keepdims=True
                )
                groups.append(
                    jnp.concatenate([scaled(low, squares), scaled(high, squares)], axis=1)
                    * gain
                )
                a, b = (
                    columns_at(pieces[q], full * features + chip * width, width)
                    for q in (p, p + 1)
                )
                low = jnp.concatenate([a[0:4], b[0:4]], axis=0)
                high = jnp.concatenate([a[4:8], b[4:8]], axis=0)
                own.append(jnp.where(ci == 0, low, high))
                away.append(jnp.where(ci == 0, high, low))
            row = len(chunks) * 8 + first * 4
            put(row, groups)
            out_ref[row : row + 16, spot : spot + width] = jnp.concatenate(
                own, axis=0
            ).astype(jnp.bfloat16)
            out_other_ref[row : row + 16, spot : spot + width] = jnp.concatenate(
                away, axis=0
            ).astype(jnp.bfloat16)
    rows = normal[...]
    for target, weights in ((out_other_ref, [other_ref]), (out_ref, mine)):
        value = jnp.concatenate([by_rows(rows, w[...]) for w in weights], axis=1)
        target[:, 0 : value.shape[1]] = value.astype(jnp.bfloat16)


def plan_kernel(query_rows, owner_ref, segment_ref, own_ref, away_ref, mask_ref):
    _, zi, yi, ci = place()
    nz = lax.axis_size(AXIS) // 4
    query_total = query_rows * 4 * nz
    blocks_total = owner_ref.shape[0]
    tokens = query_total + blocks_total * BLK
    piece_rows = query_rows + CAP * BLK
    full, halved = piece_layout(piece_rows)
    plane_rows = own_ref.shape[1]

    def lay(shape, axis):
        token = lax.broadcasted_iota(jnp.int32, shape, axis)
        block = (token - query_total) // BLK
        is_query = token < query_total
        owner = jnp.where(is_query, token // query_rows, 0)
        pair = jnp.where(is_query, token // QLEN, 0)

        def fill(b, carry):
            here = (block == b) & (token >= query_total)
            return (
                jnp.where(here, owner_ref[b], carry[0]),
                jnp.where(here, segment_ref[b], carry[1]),
            )

        owner, pair = lax.fori_loop(0, blocks_total, fill, (owner, pair))
        return token, block, owner, pair

    token, block, owner, pair = lay((tokens, 1), 0)
    token_row, block_row, owner_row, pair_row = lay((1, tokens), 1)
    ahead = (
        (owner == owner_row)
        & (block_row < block)
        & (token_row >= query_total)
        & (token >= query_total)
    )
    before = jnp.sum(ahead.astype(jnp.float32), axis=-1, keepdims=True).astype(jnp.int32)
    local = jnp.where(
        token < query_total,
        token % query_rows,
        query_rows + before + (token - query_total) % BLK,
    )
    source = (zi ^ (owner // 4)) * 2 + (((owner // 2) % 2) ^ yi)
    pieces = 2 * nz
    spot = source * (full * 8) + local
    if halved:
        spot = jnp.where(
            local < full * 8, spot, pieces * full * 8 + source * 4 + local - full * 8
        )
    spot = spot + ((owner % 2) ^ ci) * plane_rows
    lanes = lax.broadcasted_iota(jnp.int32, (tokens, plane_rows), 1)
    own_ref[...] = (lanes == spot).astype(jnp.bfloat16)
    away_ref[...] = (lanes == spot - plane_rows).astype(jnp.bfloat16)
    mask_ref[...] = (pair == pair_row).astype(jnp.float32)


def attention_kernel(width, pick_ref, pick_away_ref, mask_ref, own_ref, away_ref, ctx_ref, col_ref):
    tokens = pick_ref.shape[0]
    packed = dot(pick_ref[...], own_ref[...]) + dot(pick_away_ref[...], away_ref[...])
    col_ref[...] = packed[:, 256 : 256 + width].astype(jnp.bfloat16)
    query, key, value = (
        packed[:, i * HDIM : (i + 1) * HDIM].astype(jnp.bfloat16) for i in range(3)
    )
    scores = by_rows(query, key) * HDIM ** (-0.5)
    scores = jnp.where(mask_ref[...] > 0.5, scores, -1e30)
    weights = jnp.exp(scores - jnp.max(scores, axis=-1, keepdims=True))
    probability = (weights / jnp.sum(weights, axis=-1, keepdims=True)).astype(jnp.bfloat16)
    context = dot(probability, value)
    ctx_ref[...] = jnp.concatenate(
        [context[: tokens // 2], context[tokens // 2 :]], axis=1
    ).astype(jnp.bfloat16)


def gate_kernel(rows_here, chunk_rows, own, *refs):
    count = len(refs) - 8
    pieces = refs[:count]
    (
        gain_ref,
        gate_ref,
        up_ref,
        share_ref,
        out_ref,
        kept_ref,
        order_ref,
        rows_ref,
    ) = refs[count:]
    _, zi, yi, ci = place()
    nz = lax.axis_size(AXIS) // 4
    tokens, width = pieces[0].shape
    half = 2 * nz * width
    total = order_ref.shape[0]
    row = lax.broadcasted_iota(jnp.int32, (total, 1), 0)
    core = ci if own else 1 - ci
    chunk = row // chunk_rows
    device = (zi ^ (chunk // 2)) * 4 + ((chunk % 2) ^ yi) * 2 + core
    wanted = device * rows_here + jnp.minimum(row % chunk_rows, rows_here - 1)
    lanes = lax.broadcasted_iota(jnp.int32, (total, tokens), 1)
    order_ref[...] = (lanes == wanted).astype(jnp.bfloat16)
    squares = jnp.zeros((total, 1), jnp.float32)
    for dz in range(nz):
        near, far = pieces[2 * dz][...], pieces[2 * dz + 1][...]
        pair = jnp.where(
            yi == 0,
            jnp.concatenate([near, far], axis=1),
            jnp.concatenate([far, near], axis=1),
        )
        start = pl.multiple_of((zi ^ dz) * (2 * width), 128)
        values = dot(order_ref[...], pair)
        squares = squares + jnp.sum(values * values, axis=-1, keepdims=True)
        kept_ref[:, pl.ds(start, 2 * width)] = values[0:chunk_rows].astype(jnp.bfloat16)
        gain = gain_ref[:, pl.ds(pl.multiple_of(ci * half + start, 128), 2 * width)]
        rows_ref[:, pl.ds(start, 2 * width)] = (values * gain).astype(jnp.bfloat16)
    mine = pl.ds(pl.multiple_of(ci * half, 128), half)
    rows = rows_ref[...]
    units = gate_ref.shape[0]
    gate = by_rows(rows, gate_ref[:, mine])
    up = by_rows(rows, up_ref[:, mine])
    gate_other = by_rows(rows, share_ref[:units, :half])
    up_other = by_rows(rows, share_ref[:units, half:])
    spread = jnp.broadcast_to(squares, (total, out_ref.shape[1] - 4 * units))
    parts = (gate, gate_other, up, up_other) if own else (gate_other, gate, up_other, up)
    out_ref[...] = jnp.concatenate([*parts, spread], axis=1)


def packed(rows):
    count, features = rows.shape
    groups = [rows[i : i + 8] for i in range(0, count // 8 * 8, 8)]
    first = count // 8 * 8
    for size in (4, 2, 1):
        if (count - first) & size:
            step = features * size // 8
            groups.append(
                jnp.concatenate(
                    [
                        rows[first : first + size, j * step : (j + 1) * step]
                        for j in range(8 // size)
                    ],
                    axis=0,
                )
            )
            first += size
    return jnp.concatenate(groups, axis=1) if len(groups) > 1 else groups[0]


def unpack(value, target):
    count, features = target.shape
    for i in range(count // 8):
        target[i * 8 : i * 8 + 8, :] = value[:, i * features : (i + 1) * features]
    first, lane = count // 8 * 8, count // 8 * features
    for size in (4, 2, 1):
        if (count - first) & size:
            step = features * size // 8
            for j in range(8 // size):
                target[first : first + size, j * step : (j + 1) * step] = value[
                    j * size : (j + 1) * size, lane : lane + step
                ]
            first, lane = first + size, lane + step


def hidden_kernel(features, chunk_rows, rows_here, keep_ref, came_ref, down_ref, share_ref, *refs):
    hidden_ref = refs[-1]
    units = down_ref.shape[0]
    summed = keep_ref[...] + came_ref[...]
    scale = lax.rsqrt(summed[:, 4 * units : 4 * units + 1] / features + 1e-06)
    gate = summed[:, 0 : 2 * units] * scale
    up = summed[:, 2 * units : 4 * units] * scale
    hidden = (jax.nn.gelu(gate, approximate=True) * up).astype(jnp.bfloat16)
    hidden_ref[...] = hidden
    far = jnp.concatenate(
        [
            hidden[(2 * dz + 1) * chunk_rows : (2 * dz + 2) * chunk_rows]
            for dz in range(len(refs) - 1)
        ],
        axis=0,
    )
    result = dot(far[:, :units], down_ref[...]) + dot(far[:, units:], share_ref[units:, :])
    for dz in range(len(refs) - 1):
        first = dz * chunk_rows
        refs[dz][...] = packed(result[first : first + rows_here]).astype(jnp.bfloat16)


def down_kernel(chunk_rows, rows_here, hidden_ref, down_ref, share_ref, *out_refs):
    units = down_ref.shape[0]
    hidden = hidden_ref[...]
    near = jnp.concatenate(
        [
            hidden[2 * dz * chunk_rows : (2 * dz + 1) * chunk_rows]
            for dz in range(len(out_refs))
        ],
        axis=0,
    )
    result = dot(near[:, :units], down_ref[...]) + dot(near[:, units:], share_ref[units:, :])
    for dz in range(len(out_refs)):
        first = dz * chunk_rows
        out_refs[dz][...] = packed(result[first : first + rows_here])


def add_kernel(near_ref, far_ref, out_ref):
    out_ref[...] = (near_ref[...] + far_ref[...].astype(jnp.float32)).astype(jnp.bfloat16)


def last_kernel(count, *refs):
    near_ref, far_ref = refs[0], refs[1]
    arrived = refs[2 : 2 + count]
    kept_ref, kept_other_ref, out_ref, total_ref = refs[2 + count :]
    ci = place()[3]
    rows = out_ref.shape[0]
    half = kept_ref.shape[1]
    kept, other = kept_ref[...].astype(jnp.float32), kept_other_ref[...].astype(jnp.float32)
    total = near_ref[...] + far_ref[...].astype(jnp.float32)
    for ref in arrived:
        total = total + ref[...].astype(jnp.float32)
    low, high = jnp.where(ci == 0, kept, other), jnp.where(ci == 0, other, kept)
    unpack(total, total_ref)
    out_ref[:, :half] = (low[:rows] + total_ref[:, :half]).astype(jnp.bfloat16)
    out_ref[:, half:] = (high[:rows] + total_ref[:, half:]).astype(jnp.bfloat16)


def body(
    queries,
    corpus,
    block_owner,
    slot_row,
    segment,
    query_weight,
    key_weight,
    value_weight,
    out_weight,
    gain_attn,
    gain_ffn,
    gate_weight,
    up_weight,
    down_weight,
):
    devices = lax.axis_size(AXIS)
    nz = devices // 4
    _, zi, yi, ci = place()
    z_order = list(range(nz - 1, 0, -1))

    def along_z(value, k):
        return lax.ppermute(value, AXIS, [(i, i ^ (4 * k)) for i in range(devices)])

    def across_y(value):
        return lax.ppermute(value, AXIS, [(i, i ^ 2) for i in range(devices)])

    def across_core(value):
        return lax.ppermute(value, AXIS, [(i, i ^ 1) for i in range(devices)])

    def plane_gather(value, value_across=None, fence=None):
        near = {0: value}
        for k in z_order:
            near[k] = along_z(value, k)
        if fence is not None:
            for k in near:
                near[k], fence = lax.optimization_barrier((near[k], fence))
        if value_across is None:
            value_across = near[0]
        return near, {
            k: across_y(near[k] if k else value_across) for k in [0] + z_order
        }

    def paired(near, far):
        return [piece for k in range(nz) for piece in (near[k], far[k])]

    owners = block_owner[:, 0]
    features = queries.shape[1]
    half = features // 2
    query_rows = queries.shape[0]
    tokens = query_rows * devices + owners.shape[0] * BLK
    width = features // devices
    heads_rows = query_weight.shape[0]
    units = gate_weight.shape[0]
    rows_here = tokens // devices
    chunk_rows = -(-rows_here // 16) * 16
    bf16, f32 = jnp.bfloat16, jnp.float32
    shape = jax.ShapeDtypeStruct

    full, halved = piece_layout(query_rows + CAP * BLK)
    piece = kernel_call(
        fetch_kernel,
        shape((8, full * features + halved * half), bf16),
        [SMEM, SMEM, ANY, ANY],
        [
            pltpu.VMEM((CAP, BLK, features), bf16),
            pltpu.VMEM((query_rows, features), bf16),
            pltpu.VMEM((full * 8 + halved * 8, features), f32),
            pltpu.SemaphoreType.DMA((CAP + 1,)),
        ],
        name="fetch",
        limit=60 * 1024 * 1024,
    )(owners, slot_row, corpus, queries)

    projections = [query_weight, key_weight, value_weight]
    plane_rows = 2 * nz * (full * 8 + halved * 4)
    wide = 256 + -(-width // 128) * 128
    *tied, _ = lax.optimization_barrier((*projections, piece))
    stacked = kernel_call(
        stack_kernel,
        shape((3 * heads_rows, features), bf16),
        [VMEM] * 3,
        name="stack",
        micros=20,
    )(*tied)
    piece_wide = piece.shape[1]
    value_across = kernel_call(
        across_kernel,
        shape((8, piece_wide + heads_rows // 8 * 2 * nz * width), bf16),
        [VMEM] * 2,
        name="across",
    )(piece, out_weight)
    near, far = plane_gather(piece, value_across, stacked)
    projections_other = across_core(stacked)
    own, away = kernel_call(
        functools.partial(projection_kernel, query_rows + CAP * BLK),
        (shape((plane_rows, wide), bf16), shape((plane_rows, wide), bf16)),
        [VMEM] * (2 * nz + 5),
        [pltpu.VMEM((plane_rows, features), bf16)],
        name="project",
        micros=10,
    )(*paired(near, far), gain_attn[None, :], *projections, projections_other)

    out_keep, out_send = kernel_call(
        functools.partial(pair_kernel, piece_wide),
        (shape((2 * heads_rows, nz * width), bf16),) * 2,
        [VMEM] * 2,
        name="pairs",
    )(out_weight, far[0])
    out_came = across_core(out_send)
    own, out_came = lax.optimization_barrier((own, out_came))

    plan = kernel_call(
        functools.partial(plan_kernel, query_rows),
        (
            shape((tokens, plane_rows), bf16),
            shape((tokens, plane_rows), bf16),
            shape((tokens, tokens), f32),
        ),
        [SMEM, SMEM],
        name="plan",
    )(owners, segment)
    context, columns = kernel_call(
        functools.partial(attention_kernel, width),
        (shape((tokens // 2, 2 * HDIM), bf16), shape((tokens, width), bf16)),
        [VMEM] * 5,
        name="attend",
    )(*plan, own, across_core(away))
    contexts = [
        context,
        across_y(context),
        across_core(context),
        lax.ppermute(context, AXIS, [(i, i ^ 3) for i in range(devices)]),
    ]
    attended, *parts = kernel_call(
        out_kernel,
        (shape((tokens, width), f32),) + (shape((tokens, width), bf16),) * (nz - 1),
        [VMEM] * 6,
        name="out",
    )(*contexts, out_keep, out_came)
    middle = columns.astype(f32) + attended
    for d in z_order:
        middle = middle + along_z(parts[d - 1], d).astype(f32)
    middle = middle.astype(bf16)
    share_gate, share_up, share_down, _ = lax.optimization_barrier(
        (gate_weight, up_weight, down_weight, middle)
    )
    share = across_core(
        kernel_call(
            share_kernel, shape((2 * units, features), bf16), [VMEM] * 3, name="share"
        )(share_gate, share_up, share_down)
    )


    slots = 2 * nz * chunk_rows
    lanes = -(-(4 * units + 1) // 128) * 128
    blocks = paired(*plane_gather(middle))

    def gate_up(own, blocks):
        return kernel_call(
            functools.partial(gate_kernel, rows_here, chunk_rows, own),
            (shape((slots, lanes), f32), shape((chunk_rows, half), bf16)),
            [VMEM] * (2 * nz + 4),
            [pltpu.VMEM((slots, tokens), bf16), pltpu.VMEM((slots, half), bf16)],
            name="gate_up_own" if own else "gate_up",
        )(*blocks, gain_ffn[None, :], gate_weight, up_weight, share)

    send, kept_send = gate_up(False, blocks)
    first, _ = lax.optimization_barrier((blocks[0], send))
    keep, kept = gate_up(True, [first, *blocks[1:]])
    came = across_core(send)
    kept_other = across_core(kept_send)

    chunk = shape((8, rows_here * features // 8), bf16)
    *far, hidden = kernel_call(
        functools.partial(hidden_kernel, features, chunk_rows, rows_here),
        (chunk,) * nz + (shape((slots, 2 * units), bf16),),
        [VMEM] * 4,
        name="hidden",
    )(keep, came, down_weight, share)
    moved = {k: across_y(far[k]) for k in [*range(1, nz), 0]}
    near = kernel_call(
        functools.partial(down_kernel, chunk_rows, rows_here),
        (shape(chunk.shape, f32),) * nz,
        [VMEM] * 3,
        name="down",
    )(hidden, down_weight, share)
    arrived = []
    for k in range(1, nz):
        part = kernel_call(add_kernel, chunk, [VMEM, VMEM], name="add")(near[k], moved[k])
        arrived.append(along_z(part, k))
    return kernel_call(
        functools.partial(last_kernel, len(arrived)),
        shape((rows_here, features), bf16),
        [VMEM] * (len(arrived) + 4),
        [pltpu.VMEM((rows_here, features), f32)],
        name="last",
    )(near[0], moved[0], *arrived, kept, kept_other)


def solution(mesh):
    placed = (
        P(("groups", "tensor"), None),
        P(("groups", "tensor"), None, None),
        P("groups", None),
        P("groups"),
        P("groups"),
        P("tensor", None),
        P("tensor", None),
        P("tensor", None),
        P("tensor", None),
        P(),
        P(),
        P("tensor", None),
        P("tensor", None),
        P("tensor", None),
    )
    return jax.shard_map(
        body, mesh=mesh, in_specs=placed, out_specs=P(("groups", "tensor"), None), check_vma=False
    )
```

```python
import functools

import jax
import jax.numpy as jnp
from jax import lax
from jax.experimental import pallas as pl
from jax.experimental.pallas import tpu as pltpu
from jax.sharding import PartitionSpec as P

HDIM = 64
QLEN = 32
BLK = 4
CAP = 3
AXIS = "tensor"
VMEM_LIMIT = 28 * 1024 * 1024


def by_rows(left, weight):
    return lax.dot_general(
        left, weight, (((1,), (1,)), ((), ())), preferred_element_type=jnp.float32
    )


def dot(left, right):
    return jnp.dot(left, right, preferred_element_type=jnp.float32)


def place():
    me = lax.axis_index(AXIS)
    return me, me // 4, (me // 2) % 2, me % 2


def kernel_call(kernel, out_shape, in_specs, scratch=(), name=None, limit=VMEM_LIMIT, micros=1):
    return pl.pallas_call(
        kernel,
        out_shape=out_shape,
        cost_estimate=pl.CostEstimate(
            flops=micros * 1_000_000_000, bytes_accessed=micros * 3_000_000, transcendentals=0
        ),
        in_specs=in_specs,
        out_specs=jax.tree.map(lambda _: pl.BlockSpec(memory_space=pltpu.VMEM), out_shape),
        scratch_shapes=scratch,
        compiler_params=pltpu.CompilerParams(vmem_limit_bytes=limit),
        name=name,
    )


SMEM = pl.BlockSpec(memory_space=pltpu.SMEM)
VMEM = pl.BlockSpec(memory_space=pltpu.VMEM)
ANY = pl.BlockSpec(memory_space=pl.ANY)


def piece_layout(rows):
    full, rest = divmod(rows, 8)
    if 0 < rest <= 4:
        return full, True
    return full + (rest > 0), False


def fetch_kernel(owner_ref, row_ref, corpus_ref, query_ref, piece_ref, blocks, query, rows, sems):
    me = place()[0]
    query_copy = pltpu.make_async_copy(query_ref, query, sems.at[CAP])
    query_copy.start()
    features = query_ref.shape[1]
    query_rows = query_ref.shape[0]

    def look(b, carry):
        count, found = carry[0], carry[1:]
        mine = owner_ref[b] == me
        found = tuple(
            jnp.where(mine & (count == k), row_ref[b], found[k]) for k in range(CAP)
        )
        return (count + mine.astype(jnp.int32),) + found

    zero = jnp.int32(0)
    found = lax.fori_loop(0, owner_ref.shape[0], look, (zero,) * (CAP + 1))[1:]
    copies = [
        pltpu.make_async_copy(corpus_ref.at[found[k]], blocks.at[k], sems.at[k])
        for k in range(CAP)
    ]
    for copy in copies:
        copy.start()
    total = query_rows + CAP * BLK
    full, halved = piece_layout(total)
    query_copy.wait()
    rows[0:query_rows, :] = query[...].astype(jnp.float32)
    for k in range(CAP):
        copies[k].wait()
        first = query_rows + k * BLK
        rows[first : first + BLK, :] = blocks[k].astype(jnp.float32)
    if not halved and total < full * 8:
        rows[total : full * 8, :] = jnp.zeros((full * 8 - total, features), jnp.float32)
    for i in range(full):
        piece_ref[:, i * features : (i + 1) * features] = rows[i * 8 : i * 8 + 8, :].astype(
            jnp.bfloat16
        )
    if halved:
        half = features // 2
        last = rows[full * 8 : full * 8 + 4, :]
        if total % 8 < 4:
            last = jnp.where(
                lax.broadcasted_iota(jnp.int32, last.shape, 0) < total % 8, last, 0.0
            )
        piece_ref[:, full * features :] = jnp.concatenate(
            [last[:, :half], last[:, half:]], axis=0
        ).astype(jnp.bfloat16)


def columns_at(ref, start, width):
    if width % 128 == 0:
        return ref[:, pl.ds(pl.multiple_of(start, 128), width)].astype(jnp.float32)
    base = pl.multiple_of(start // 128 * 128, 128)
    window = ref[:, pl.ds(base, 128)].astype(jnp.float32)
    return pltpu.roll(window, (128 - start % 128) % 128, 1)[:, :width]


def across_kernel(piece_ref, weight_ref, out_ref):
    _, zi, yi, _ = place()
    nz = lax.axis_size(AXIS) // 4
    rows, features = weight_ref.shape
    width = features // (4 * nz)
    first = piece_ref.shape[1]
    wide = 2 * nz * width
    out_ref[:, :first] = piece_ref[...]
    columns = jnp.concatenate(
        [
            columns_at(
                weight_ref, core * (features // 2) + (2 * (zi ^ d) + 1 - yi) * width, width
            )
            for d in range(nz)
            for core in range(2)
        ],
        axis=1,
    )
    for g in range(rows // 8):
        out_ref[:, first + g * wide : first + (g + 1) * wide] = columns[
            g * 8 : g * 8 + 8
        ].astype(jnp.bfloat16)


def pair_kernel(first, weight_ref, far_ref, keep_ref, send_ref):
    _, zi, yi, ci = place()
    rows, features = weight_ref.shape
    nz = lax.axis_size(AXIS) // 4
    width = features // (4 * nz)
    wide = 2 * nz * width
    for core, out_ref in ((ci, keep_ref), (1 - ci, send_ref)):
        own = [
            columns_at(
                weight_ref, core * (features // 2) + (2 * (zi ^ d) + yi) * width, width
            )
            for d in range(nz)
        ]
        out_ref[:rows, :] = jnp.concatenate(own, axis=1).astype(jnp.bfloat16)
        groups = []
        for g in range(rows // 8):
            parts = []
            for d in range(nz):
                start = first + g * wide + 2 * d * width
                both = far_ref[:, start : start + 2 * width].astype(jnp.float32)
                parts.append(jnp.where(core == 0, both[:, :width], both[:, width:]))
            groups.append(jnp.concatenate(parts, axis=1))
        out_ref[rows:, :] = jnp.concatenate(groups, axis=0).astype(jnp.bfloat16)


def stack_kernel(*refs):
    rows = refs[0].shape[0]
    for i, ref in enumerate(refs[:-1]):
        refs[-1][i * rows : (i + 1) * rows, :] = ref[...]


def share_kernel(gate_ref, up_ref, down_ref, out_ref):
    units, features = down_ref.shape
    half = features // 2
    other = pl.ds(pl.multiple_of((1 - place()[3]) * half, 128), half)
    out_ref[:units, :half] = gate_ref[:, other]
    out_ref[:units, half:] = up_ref[:, other]
    out_ref[units:, :] = down_ref[...]


def out_kernel(*refs):
    near_ref, far_ref, other_ref, other_far_ref, weight_ref, weight_other_ref, mine_ref = refs[:7]
    send_refs = refs[7:]
    width = mine_ref.shape[1]

    def heads(near_ref, far_ref):
        near, far = near_ref[...], far_ref[...]
        return jnp.concatenate(
            [
                jnp.concatenate([near[:, :HDIM], far[:, :HDIM]], axis=1),
                jnp.concatenate([near[:, HDIM:], far[:, HDIM:]], axis=1),
            ],
            axis=0,
        )

    attended = dot(heads(near_ref, far_ref), weight_ref[...]) + dot(
        heads(other_ref, other_far_ref), weight_other_ref[...]
    )
    mine_ref[...] = attended[:, :width]
    for d, ref in enumerate(send_refs, 1):
        ref[...] = attended[:, d * width : (d + 1) * width].astype(jnp.bfloat16)


def projection_kernel(piece_rows, *refs):
    count = len(refs) - 8
    pieces, rest = refs[:count], refs[count:]
    gain_ref, *mine, other_ref, out_ref, out_other_ref, normal = rest
    _, zi, yi, ci = place()
    features = gain_ref.shape[1]
    half = features // 2
    full, halved = piece_layout(piece_rows)
    width = features // lax.axis_size(AXIS)
    chip = 2 * zi + yi
    gain = gain_ref[...]
    spot = 256
    own_column = ci * half + chip * width
    other_column = (1 - ci) * half + chip * width

    def scaled(values, squares):
        return values * lax.rsqrt(squares / features + 1e-06)

    def put(row, groups):
        normal[row : row + 16, :] = jnp.concatenate(groups, axis=0).astype(jnp.bfloat16)

    chunks = [(p, i) for p in range(count) for i in range(full)]
    for first in range(0, len(chunks), 2):
        groups, own, away = [], [], []
        for p, i in chunks[first : first + 2]:
            values = pieces[p][:, i * features : (i + 1) * features].astype(jnp.float32)
            squares = jnp.sum(values * values, axis=-1, keepdims=True)
            groups.append(scaled(values, squares) * gain)
            own.append(columns_at(pieces[p], i * features + own_column, width))
            away.append(columns_at(pieces[p], i * features + other_column, width))
        row = first * 8
        put(row, groups)
        out_ref[row : row + 16, spot : spot + width] = jnp.concatenate(own, axis=0).astype(
            jnp.bfloat16
        )
        out_other_ref[row : row + 16, spot : spot + width] = jnp.concatenate(
            away, axis=0
        ).astype(jnp.bfloat16)
    if halved:
        for first in range(0, count, 4):
            groups, own, away = [], [], []
            for p in range(first, first + 4, 2):
                a, b = (
                    pieces[q][:, full * features : full * features + half].astype(jnp.float32)
                    for q in (p, p + 1)
                )
                low = jnp.concatenate([a[0:4], b[0:4]], axis=0)
                high = jnp.concatenate([a[4:8], b[4:8]], axis=0)
                squares = jnp.sum(low * low, axis=-1, keepdims=True) + jnp.sum(
                    high * high, axis=-1, keepdims=True
                )
                groups.append(
                    jnp.concatenate([scaled(low, squares), scaled(high, squares)], axis=1)
                    * gain
                )
                a, b = (
                    columns_at(pieces[q], full * features + chip * width, width)
                    for q in (p, p + 1)
                )
                low = jnp.concatenate([a[0:4], b[0:4]], axis=0)
                high = jnp.concatenate([a[4:8], b[4:8]], axis=0)
                own.append(jnp.where(ci == 0, low, high))
                away.append(jnp.where(ci == 0, high, low))
            row = len(chunks) * 8 + first * 4
            put(row, groups)
            out_ref[row : row + 16, spot : spot + width] = jnp.concatenate(
                own, axis=0
            ).astype(jnp.bfloat16)
            out_other_ref[row : row + 16, spot : spot + width] = jnp.concatenate(
                away, axis=0
            ).astype(jnp.bfloat16)
    rows = normal[...]
    for target, weights in ((out_other_ref, [other_ref]), (out_ref, mine)):
        value = jnp.concatenate([by_rows(rows, w[...]) for w in weights], axis=1)
        target[:, 0 : value.shape[1]] = value.astype(jnp.bfloat16)


def plan_kernel(query_rows, owner_ref, segment_ref, own_ref, away_ref, mask_ref):
    _, zi, yi, ci = place()
    nz = lax.axis_size(AXIS) // 4
    query_total = query_rows * 4 * nz
    blocks_total = owner_ref.shape[0]
    tokens = query_total + blocks_total * BLK
    piece_rows = query_rows + CAP * BLK
    full, halved = piece_layout(piece_rows)
    plane_rows = own_ref.shape[1]

    def lay(shape, axis):
        token = lax.broadcasted_iota(jnp.int32, shape, axis)
        block = (token - query_total) // BLK
        is_query = token < query_total
        owner = jnp.where(is_query, token // query_rows, 0)
        pair = jnp.where(is_query, token // QLEN, 0)

        def fill(b, carry):
            here = (block == b) & (token >= query_total)
            return (
                jnp.where(here, owner_ref[b], carry[0]),
                jnp.where(here, segment_ref[b], carry[1]),
            )

        owner, pair = lax.fori_loop(0, blocks_total, fill, (owner, pair))
        return token, block, owner, pair

    token, block, owner, pair = lay((tokens, 1), 0)
    token_row, block_row, owner_row, pair_row = lay((1, tokens), 1)
    ahead = (
        (owner == owner_row)
        & (block_row < block)
        & (token_row >= query_total)
        & (token >= query_total)
    )
    before = jnp.sum(ahead.astype(jnp.float32), axis=-1, keepdims=True).astype(jnp.int32)
    local = jnp.where(
        token < query_total,
        token % query_rows,
        query_rows + before + (token - query_total) % BLK,
    )
    source = (zi ^ (owner // 4)) * 2 + (((owner // 2) % 2) ^ yi)
    pieces = 2 * nz
    spot = source * (full * 8) + local
    if halved:
        spot = jnp.where(
            local < full * 8, spot, pieces * full * 8 + source * 4 + local - full * 8
        )
    spot = spot + ((owner % 2) ^ ci) * plane_rows
    lanes = lax.broadcasted_iota(jnp.int32, (tokens, plane_rows), 1)
    own_ref[...] = (lanes == spot).astype(jnp.bfloat16)
    away_ref[...] = (lanes == spot - plane_rows).astype(jnp.bfloat16)
    mask_ref[...] = (pair == pair_row).astype(jnp.float32)


def attention_kernel(width, pick_ref, pick_away_ref, mask_ref, own_ref, away_ref, ctx_ref, col_ref):
    tokens = pick_ref.shape[0]
    packed = dot(pick_ref[...], own_ref[...]) + dot(pick_away_ref[...], away_ref[...])
    col_ref[...] = packed[:, 256 : 256 + width].astype(jnp.bfloat16)
    query, key, value = (
        packed[:, i * HDIM : (i + 1) * HDIM].astype(jnp.bfloat16) for i in range(3)
    )
    scores = by_rows(query, key) * HDIM ** (-0.5)
    scores = jnp.where(mask_ref[...] > 0.5, scores, -1e30)
    weights = jnp.exp(scores - jnp.max(scores, axis=-1, keepdims=True))
    probability = (weights / jnp.sum(weights, axis=-1, keepdims=True)).astype(jnp.bfloat16)
    context = dot(probability, value)
    ctx_ref[...] = jnp.concatenate(
        [context[: tokens // 2], context[tokens // 2 :]], axis=1
    ).astype(jnp.bfloat16)


def gate_kernel(rows_here, chunk_rows, own, *refs):
    count = len(refs) - 8
    pieces = refs[:count]
    (
        gain_ref,
        gate_ref,
        up_ref,
        share_ref,
        out_ref,
        kept_ref,
        order_ref,
        rows_ref,
    ) = refs[count:]
    _, zi, yi, ci = place()
    nz = lax.axis_size(AXIS) // 4
    tokens, width = pieces[0].shape
    half = 2 * nz * width
    total = order_ref.shape[0]
    row = lax.broadcasted_iota(jnp.int32, (total, 1), 0)
    core = ci if own else 1 - ci
    chunk = row // chunk_rows
    device = (zi ^ (chunk // 2)) * 4 + ((chunk % 2) ^ yi) * 2 + core
    wanted = device * rows_here + jnp.minimum(row % chunk_rows, rows_here - 1)
    lanes = lax.broadcasted_iota(jnp.int32, (total, tokens), 1)
    order_ref[...] = (lanes == wanted).astype(jnp.bfloat16)
    squares = jnp.zeros((total, 1), jnp.float32)
    for dz in range(nz):
        near, far = pieces[2 * dz][...], pieces[2 * dz + 1][...]
        pair = jnp.where(
            yi == 0,
            jnp.concatenate([near, far], axis=1),
            jnp.concatenate([far, near], axis=1),
        )
        start = pl.multiple_of((zi ^ dz) * (2 * width), 128)
        values = dot(order_ref[...], pair)
        squares = squares + jnp.sum(values * values, axis=-1, keepdims=True)
        kept_ref[:, pl.ds(start, 2 * width)] = values[0:chunk_rows].astype(jnp.bfloat16)
        gain = gain_ref[:, pl.ds(pl.multiple_of(ci * half + start, 128), 2 * width)]
        rows_ref[:, pl.ds(start, 2 * width)] = (values * gain).astype(jnp.bfloat16)
    mine = pl.ds(pl.multiple_of(ci * half, 128), half)
    rows = rows_ref[...]
    units = gate_ref.shape[0]
    gate = by_rows(rows, gate_ref[:, mine])
    up = by_rows(rows, up_ref[:, mine])
    gate_other = by_rows(rows, share_ref[:units, :half])
    up_other = by_rows(rows, share_ref[:units, half:])
    spread = jnp.broadcast_to(squares, (total, out_ref.shape[1] - 4 * units))
    parts = (gate, gate_other, up, up_other) if own else (gate_other, gate, up_other, up)
    out_ref[...] = jnp.concatenate([*parts, spread], axis=1)


def packed(rows):
    count, features = rows.shape
    groups = [rows[i : i + 8] for i in range(0, count // 8 * 8, 8)]
    first = count // 8 * 8
    for size in (4, 2, 1):
        if (count - first) & size:
            step = features * size // 8
            groups.append(
                jnp.concatenate(
                    [
                        rows[first : first + size, j * step : (j + 1) * step]
                        for j in range(8 // size)
                    ],
                    axis=0,
                )
            )
            first += size
    return jnp.concatenate(groups, axis=1) if len(groups) > 1 else groups[0]


def unpack(value, target):
    count, features = target.shape
    for i in range(count // 8):
        target[i * 8 : i * 8 + 8, :] = value[:, i * features : (i + 1) * features]
    first, lane = count // 8 * 8, count // 8 * features
    for size in (4, 2, 1):
        if (count - first) & size:
            step = features * size // 8
            for j in range(8 // size):
                target[first : first + size, j * step : (j + 1) * step] = value[
                    j * size : (j + 1) * size, lane : lane + step
                ]
            first, lane = first + size, lane + step


def hidden_kernel(features, chunk_rows, rows_here, keep_ref, came_ref, down_ref, share_ref, *refs):
    hidden_ref = refs[-1]
    units = down_ref.shape[0]
    summed = keep_ref[...] + came_ref[...]
    scale = lax.rsqrt(summed[:, 4 * units : 4 * units + 1] / features + 1e-06)
    gate = summed[:, 0 : 2 * units] * scale
    up = summed[:, 2 * units : 4 * units] * scale
    hidden = (jax.nn.gelu(gate, approximate=True) * up).astype(jnp.bfloat16)
    hidden_ref[...] = hidden
    far = jnp.concatenate(
        [
            hidden[(2 * dz + 1) * chunk_rows : (2 * dz + 2) * chunk_rows]
            for dz in range(len(refs) - 1)
        ],
        axis=0,
    )
    result = dot(far[:, :units], down_ref[...]) + dot(far[:, units:], share_ref[units:, :])
    for dz in range(len(refs) - 1):
        first = dz * chunk_rows
        refs[dz][...] = packed(result[first : first + rows_here]).astype(jnp.bfloat16)


def down_kernel(chunk_rows, rows_here, hidden_ref, down_ref, share_ref, *out_refs):
    units = down_ref.shape[0]
    hidden = hidden_ref[...]
    near = jnp.concatenate(
        [
            hidden[2 * dz * chunk_rows : (2 * dz + 1) * chunk_rows]
            for dz in range(len(out_refs))
        ],
        axis=0,
    )
    result = dot(near[:, :units], down_ref[...]) + dot(near[:, units:], share_ref[units:, :])
    for dz in range(len(out_refs)):
        first = dz * chunk_rows
        out_refs[dz][...] = packed(result[first : first + rows_here])


def add_kernel(near_ref, far_ref, out_ref):
    out_ref[...] = (near_ref[...] + far_ref[...].astype(jnp.float32)).astype(jnp.bfloat16)


def base_kernel(near_ref, far_ref, kept_ref, kept_other_ref, out_ref):
    ci = place()[3]
    rows = out_ref.shape[0]
    half = kept_ref.shape[1]
    kept, other = kept_ref[...].astype(jnp.float32), kept_other_ref[...].astype(jnp.float32)
    low, high = jnp.where(ci == 0, kept, other), jnp.where(ci == 0, other, kept)
    unpack(near_ref[...] + far_ref[...].astype(jnp.float32), out_ref)
    out_ref[:, :half] = low[:rows] + out_ref[:, :half]
    out_ref[:, half:] = high[:rows] + out_ref[:, half:]


def last_kernel(base_ref, *refs):
    arrived, (out_ref, total_ref) = refs[:-2], refs[-2:]
    total = arrived[0][...].astype(jnp.float32)
    for ref in arrived[1:]:
        total = total + ref[...].astype(jnp.float32)
    unpack(total, total_ref)
    out_ref[...] = (base_ref[...] + total_ref[...]).astype(jnp.bfloat16)


def body(
    queries,
    corpus,
    block_owner,
    slot_row,
    segment,
    query_weight,
    key_weight,
    value_weight,
    out_weight,
    gain_attn,
    gain_ffn,
    gate_weight,
    up_weight,
    down_weight,
):
    devices = lax.axis_size(AXIS)
    nz = devices // 4
    _, zi, yi, ci = place()
    z_order = list(range(nz - 1, 0, -1))

    def along_z(value, k):
        return lax.ppermute(value, AXIS, [(i, i ^ (4 * k)) for i in range(devices)])

    def across_y(value):
        return lax.ppermute(value, AXIS, [(i, i ^ 2) for i in range(devices)])

    def across_core(value):
        return lax.ppermute(value, AXIS, [(i, i ^ 1) for i in range(devices)])

    def plane_gather(value, value_across=None, fence=None):
        near = {0: value}
        for k in z_order:
            near[k] = along_z(value, k)
        if fence is not None:
            for k in near:
                near[k], fence = lax.optimization_barrier((near[k], fence))
        if value_across is None:
            value_across = near[0]
        return near, {
            k: across_y(near[k] if k else value_across) for k in [0] + z_order
        }

    def paired(near, far):
        return [piece for k in range(nz) for piece in (near[k], far[k])]

    owners = block_owner[:, 0]
    features = queries.shape[1]
    half = features // 2
    query_rows = queries.shape[0]
    tokens = query_rows * devices + owners.shape[0] * BLK
    width = features // devices
    heads_rows = query_weight.shape[0]
    units = gate_weight.shape[0]
    rows_here = tokens // devices
    chunk_rows = -(-rows_here // 16) * 16
    bf16, f32 = jnp.bfloat16, jnp.float32
    shape = jax.ShapeDtypeStruct

    full, halved = piece_layout(query_rows + CAP * BLK)
    piece = kernel_call(
        fetch_kernel,
        shape((8, full * features + halved * half), bf16),
        [SMEM, SMEM, ANY, ANY],
        [
            pltpu.VMEM((CAP, BLK, features), bf16),
            pltpu.VMEM((query_rows, features), bf16),
            pltpu.VMEM((full * 8 + halved * 8, features), f32),
            pltpu.SemaphoreType.DMA((CAP + 1,)),
        ],
        name="fetch",
        limit=60 * 1024 * 1024,
    )(owners, slot_row, corpus, queries)

    projections = [query_weight, key_weight, value_weight]
    plane_rows = 2 * nz * (full * 8 + halved * 4)
    wide = 256 + -(-width // 128) * 128
    *tied, _ = lax.optimization_barrier((*projections, piece))
    stacked = kernel_call(
        stack_kernel,
        shape((3 * heads_rows, features), bf16),
        [VMEM] * 3,
        name="stack",
        micros=20,
    )(*tied)
    piece_wide = piece.shape[1]
    value_across = kernel_call(
        across_kernel,
        shape((8, piece_wide + heads_rows // 8 * 2 * nz * width), bf16),
        [VMEM] * 2,
        name="across",
    )(piece, out_weight)
    near, far = plane_gather(piece, value_across, stacked)
    projections_other = across_core(stacked)
    own, away = kernel_call(
        functools.partial(projection_kernel, query_rows + CAP * BLK),
        (shape((plane_rows, wide), bf16), shape((plane_rows, wide), bf16)),
        [VMEM] * (2 * nz + 5),
        [pltpu.VMEM((plane_rows, features), bf16)],
        name="project",
        micros=10,
    )(*paired(near, far), gain_attn[None, :], *projections, projections_other)

    out_keep, out_send = kernel_call(
        functools.partial(pair_kernel, piece_wide),
        (shape((2 * heads_rows, nz * width), bf16),) * 2,
        [VMEM] * 2,
        name="pairs",
    )(out_weight, far[0])
    out_came = across_core(out_send)
    own, out_came = lax.optimization_barrier((own, out_came))

    plan = kernel_call(
        functools.partial(plan_kernel, query_rows),
        (
            shape((tokens, plane_rows), bf16),
            shape((tokens, plane_rows), bf16),
            shape((tokens, tokens), f32),
        ),
        [SMEM, SMEM],
        name="plan",
    )(owners, segment)
    context, columns = kernel_call(
        functools.partial(attention_kernel, width),
        (shape((tokens // 2, 2 * HDIM), bf16), shape((tokens, width), bf16)),
        [VMEM] * 5,
        name="attend",
    )(*plan, own, across_core(away))
    contexts = [
        context,
        across_y(context),
        across_core(context),
        lax.ppermute(context, AXIS, [(i, i ^ 3) for i in range(devices)]),
    ]
    attended, *parts = kernel_call(
        out_kernel,
        (shape((tokens, width), f32),) + (shape((tokens, width), bf16),) * (nz - 1),
        [VMEM] * 6,
        name="out",
    )(*contexts, out_keep, out_came)
    middle = columns.astype(f32) + attended
    for d in z_order:
        middle = middle + along_z(parts[d - 1], d).astype(f32)
    middle = middle.astype(bf16)
    share_gate, share_up, share_down, _ = lax.optimization_barrier(
        (gate_weight, up_weight, down_weight, middle)
    )
    share = across_core(
        kernel_call(
            share_kernel, shape((2 * units, features), bf16), [VMEM] * 3, name="share"
        )(share_gate, share_up, share_down)
    )


    slots = 2 * nz * chunk_rows
    lanes = -(-(4 * units + 1) // 128) * 128
    blocks = paired(*plane_gather(middle))

    def gate_up(own, blocks):
        return kernel_call(
            functools.partial(gate_kernel, rows_here, chunk_rows, own),
            (shape((slots, lanes), f32), shape((chunk_rows, half), bf16)),
            [VMEM] * (2 * nz + 4),
            [pltpu.VMEM((slots, tokens), bf16), pltpu.VMEM((slots, half), bf16)],
            name="gate_up_own" if own else "gate_up",
        )(*blocks, gain_ffn[None, :], gate_weight, up_weight, share)

    send, kept_send = gate_up(False, blocks)
    first, _ = lax.optimization_barrier((blocks[0], send))
    keep, kept = gate_up(True, [first, *blocks[1:]])
    came = across_core(send)
    kept_other = across_core(kept_send)

    chunk = shape((8, rows_here * features // 8), bf16)
    *far, hidden = kernel_call(
        functools.partial(hidden_kernel, features, chunk_rows, rows_here),
        (chunk,) * nz + (shape((slots, 2 * units), bf16),),
        [VMEM] * 4,
        name="hidden",
    )(keep, came, down_weight, share)
    moved = {k: across_y(far[k]) for k in [*range(1, nz), 0]}
    near = kernel_call(
        functools.partial(down_kernel, chunk_rows, rows_here),
        (shape(chunk.shape, f32),) * nz,
        [VMEM] * 3,
        name="down",
    )(hidden, down_weight, share)
    arrived = []
    for k in range(1, nz):
        part = kernel_call(add_kernel, chunk, [VMEM, VMEM], name="add")(near[k], moved[k])
        arrived.append(along_z(part, k))
    base = kernel_call(
        base_kernel, shape((rows_here, features), f32), [VMEM] * 4, name="base"
    )(near[0], moved[0], kept, kept_other)
    return kernel_call(
        last_kernel,
        shape((rows_here, features), bf16),
        [VMEM] * (len(arrived) + 1),
        [pltpu.VMEM((rows_here, features), f32)],
        name="last",
    )(base, *arrived)


def solution(mesh):
    placed = (
        P(("groups", "tensor"), None),
        P(("groups", "tensor"), None, None),
        P("groups", None),
        P("groups"),
        P("groups"),
        P("tensor", None),
        P("tensor", None),
        P("tensor", None),
        P("tensor", None),
        P(),
        P(),
        P("tensor", None),
        P("tensor", None),
        P("tensor", None),
    )
    return jax.shard_map(
        body, mesh=mesh, in_specs=placed, out_specs=P(("groups", "tensor"), None), check_vma=False
    )
```

```python
import functools

import jax
import jax.numpy as jnp
from jax import lax
from jax.experimental import pallas as pl
from jax.experimental.pallas import tpu as pltpu
from jax.sharding import PartitionSpec as P

HDIM = 64
QLEN = 32
BLK = 4
CAP = 3
AXIS = "tensor"
VMEM_LIMIT = 28 * 1024 * 1024


def by_rows(left, weight):
    return lax.dot_general(
        left, weight, (((1,), (1,)), ((), ())), preferred_element_type=jnp.float32
    )


def dot(left, right):
    return jnp.dot(left, right, preferred_element_type=jnp.float32)


def place():
    me = lax.axis_index(AXIS)
    return me, me // 4, (me // 2) % 2, me % 2


def kernel_call(kernel, out_shape, in_specs, scratch=(), name=None, limit=VMEM_LIMIT, micros=1):
    return pl.pallas_call(
        kernel,
        out_shape=out_shape,
        cost_estimate=pl.CostEstimate(
            flops=micros * 1_000_000_000, bytes_accessed=micros * 3_000_000, transcendentals=0
        ),
        in_specs=in_specs,
        out_specs=jax.tree.map(lambda _: pl.BlockSpec(memory_space=pltpu.VMEM), out_shape),
        scratch_shapes=scratch,
        compiler_params=pltpu.CompilerParams(vmem_limit_bytes=limit),
        name=name,
    )


SMEM = pl.BlockSpec(memory_space=pltpu.SMEM)
VMEM = pl.BlockSpec(memory_space=pltpu.VMEM)
ANY = pl.BlockSpec(memory_space=pl.ANY)


def piece_layout(rows):
    full, rest = divmod(rows, 8)
    if 0 < rest <= 4:
        return full, True
    return full + (rest > 0), False


def fetch_kernel(owner_ref, row_ref, corpus_ref, query_ref, piece_ref, blocks, query, rows, sems):
    me = place()[0]
    query_copy = pltpu.make_async_copy(query_ref, query, sems.at[CAP])
    query_copy.start()
    features = query_ref.shape[1]
    query_rows = query_ref.shape[0]

    def look(b, carry):
        count, found = carry[0], carry[1:]
        mine = owner_ref[b] == me
        found = tuple(
            jnp.where(mine & (count == k), row_ref[b], found[k]) for k in range(CAP)
        )
        return (count + mine.astype(jnp.int32),) + found

    zero = jnp.int32(0)
    found = lax.fori_loop(0, owner_ref.shape[0], look, (zero,) * (CAP + 1))[1:]
    copies = [
        pltpu.make_async_copy(corpus_ref.at[found[k]], blocks.at[k], sems.at[k])
        for k in range(CAP)
    ]
    for copy in copies:
        copy.start()
    total = query_rows + CAP * BLK
    full, halved = piece_layout(total)
    query_copy.wait()
    rows[0:query_rows, :] = query[...].astype(jnp.float32)
    for k in range(CAP):
        copies[k].wait()
        first = query_rows + k * BLK
        rows[first : first + BLK, :] = blocks[k].astype(jnp.float32)
    if not halved and total < full * 8:
        rows[total : full * 8, :] = jnp.zeros((full * 8 - total, features), jnp.float32)
    for i in range(full):
        piece_ref[:, i * features : (i + 1) * features] = rows[i * 8 : i * 8 + 8, :].astype(
            jnp.bfloat16
        )
    if halved:
        half = features // 2
        last = rows[full * 8 : full * 8 + 4, :]
        if total % 8 < 4:
            last = jnp.where(
                lax.broadcasted_iota(jnp.int32, last.shape, 0) < total % 8, last, 0.0
            )
        piece_ref[:, full * features :] = jnp.concatenate(
            [last[:, :half], last[:, half:]], axis=0
        ).astype(jnp.bfloat16)


def columns_at(ref, start, width):
    if width % 128 == 0:
        return ref[:, pl.ds(pl.multiple_of(start, 128), width)].astype(jnp.float32)
    base = pl.multiple_of(start // 128 * 128, 128)
    window = ref[:, pl.ds(base, 128)].astype(jnp.float32)
    return pltpu.roll(window, (128 - start % 128) % 128, 1)[:, :width]


def across_kernel(piece_ref, weight_ref, out_ref):
    _, zi, yi, _ = place()
    nz = lax.axis_size(AXIS) // 4
    rows, features = weight_ref.shape
    width = features // (4 * nz)
    first = piece_ref.shape[1]
    wide = 2 * nz * width
    out_ref[:, :first] = piece_ref[...]
    columns = jnp.concatenate(
        [
            columns_at(
                weight_ref, core * (features // 2) + (2 * (zi ^ d) + 1 - yi) * width, width
            )
            for d in range(nz)
            for core in range(2)
        ],
        axis=1,
    )
    for g in range(rows // 8):
        out_ref[:, first + g * wide : first + (g + 1) * wide] = columns[
            g * 8 : g * 8 + 8
        ].astype(jnp.bfloat16)


def pair_kernel(first, weight_ref, far_ref, keep_ref, send_ref):
    _, zi, yi, ci = place()
    rows, features = weight_ref.shape
    nz = lax.axis_size(AXIS) // 4
    width = features // (4 * nz)
    wide = 2 * nz * width
    for core, out_ref in ((ci, keep_ref), (1 - ci, send_ref)):
        own = [
            columns_at(
                weight_ref, core * (features // 2) + (2 * (zi ^ d) + yi) * width, width
            )
            for d in range(nz)
        ]
        out_ref[:rows, :] = jnp.concatenate(own, axis=1).astype(jnp.bfloat16)
        groups = []
        for g in range(rows // 8):
            parts = []
            for d in range(nz):
                start = first + g * wide + 2 * d * width
                both = far_ref[:, start : start + 2 * width].astype(jnp.float32)
                parts.append(jnp.where(core == 0, both[:, :width], both[:, width:]))
            groups.append(jnp.concatenate(parts, axis=1))
        out_ref[rows:, :] = jnp.concatenate(groups, axis=0).astype(jnp.bfloat16)


def stack_kernel(*refs):
    rows = refs[0].shape[0]
    for i, ref in enumerate(refs[:-1]):
        refs[-1][i * rows : (i + 1) * rows, :] = ref[...]


def share_kernel(gate_ref, up_ref, down_ref, out_ref):
    units, features = down_ref.shape
    half = features // 2
    other = pl.ds(pl.multiple_of((1 - place()[3]) * half, 128), half)
    out_ref[:units, :half] = gate_ref[:, other]
    out_ref[:units, half:] = up_ref[:, other]
    out_ref[units:, :] = down_ref[...]


def out_kernel(*refs):
    near_ref, far_ref, other_ref, other_far_ref, weight_ref, weight_other_ref, mine_ref = refs[:7]
    send_refs = refs[7:]
    width = mine_ref.shape[1]

    def heads(near_ref, far_ref):
        near, far = near_ref[...], far_ref[...]
        return jnp.concatenate(
            [
                jnp.concatenate([near[:, :HDIM], far[:, :HDIM]], axis=1),
                jnp.concatenate([near[:, HDIM:], far[:, HDIM:]], axis=1),
            ],
            axis=0,
        )

    attended = dot(heads(near_ref, far_ref), weight_ref[...]) + dot(
        heads(other_ref, other_far_ref), weight_other_ref[...]
    )
    mine_ref[...] = attended[:, :width]
    for d, ref in enumerate(send_refs, 1):
        ref[...] = attended[:, d * width : (d + 1) * width].astype(jnp.bfloat16)


def projection_kernel(piece_rows, *refs):
    count = len(refs) - 8
    pieces, rest = refs[:count], refs[count:]
    gain_ref, *mine, other_ref, out_ref, out_other_ref, normal = rest
    _, zi, yi, ci = place()
    features = gain_ref.shape[1]
    half = features // 2
    full, halved = piece_layout(piece_rows)
    width = features // lax.axis_size(AXIS)
    chip = 2 * zi + yi
    gain = gain_ref[...]
    spot = 256
    own_column = ci * half + chip * width
    other_column = (1 - ci) * half + chip * width

    def scaled(values, squares):
        return values * lax.rsqrt(squares / features + 1e-06)

    def put(row, groups):
        normal[row : row + 16, :] = jnp.concatenate(groups, axis=0).astype(jnp.bfloat16)

    chunks = [(p, i) for p in range(count) for i in range(full)]
    for first in range(0, len(chunks), 2):
        groups, own, away = [], [], []
        for p, i in chunks[first : first + 2]:
            values = pieces[p][:, i * features : (i + 1) * features].astype(jnp.float32)
            squares = jnp.sum(values * values, axis=-1, keepdims=True)
            groups.append(scaled(values, squares) * gain)
            own.append(columns_at(pieces[p], i * features + own_column, width))
            away.append(columns_at(pieces[p], i * features + other_column, width))
        row = first * 8
        put(row, groups)
        out_ref[row : row + 16, spot : spot + width] = jnp.concatenate(own, axis=0).astype(
            jnp.bfloat16
        )
        out_other_ref[row : row + 16, spot : spot + width] = jnp.concatenate(
            away, axis=0
        ).astype(jnp.bfloat16)
    if halved:
        for first in range(0, count, 4):
            groups, own, away = [], [], []
            for p in range(first, first + 4, 2):
                a, b = (
                    pieces[q][:, full * features : full * features + half].astype(jnp.float32)
                    for q in (p, p + 1)
                )
                low = jnp.concatenate([a[0:4], b[0:4]], axis=0)
                high = jnp.concatenate([a[4:8], b[4:8]], axis=0)
                squares = jnp.sum(low * low, axis=-1, keepdims=True) + jnp.sum(
                    high * high, axis=-1, keepdims=True
                )
                groups.append(
                    jnp.concatenate([scaled(low, squares), scaled(high, squares)], axis=1)
                    * gain
                )
                a, b = (
                    columns_at(pieces[q], full * features + chip * width, width)
                    for q in (p, p + 1)
                )
                low = jnp.concatenate([a[0:4], b[0:4]], axis=0)
                high = jnp.concatenate([a[4:8], b[4:8]], axis=0)
                own.append(jnp.where(ci == 0, low, high))
                away.append(jnp.where(ci == 0, high, low))
            row = len(chunks) * 8 + first * 4
            put(row, groups)
            out_ref[row : row + 16, spot : spot + width] = jnp.concatenate(
                own, axis=0
            ).astype(jnp.bfloat16)
            out_other_ref[row : row + 16, spot : spot + width] = jnp.concatenate(
                away, axis=0
            ).astype(jnp.bfloat16)
    rows = normal[...]
    for target, weights in ((out_other_ref, [other_ref]), (out_ref, mine)):
        value = jnp.concatenate([by_rows(rows, w[...]) for w in weights], axis=1)
        target[:, 0 : value.shape[1]] = value.astype(jnp.bfloat16)


def plan_kernel(query_rows, owner_ref, segment_ref, own_ref, away_ref, mask_ref):
    _, zi, yi, ci = place()
    nz = lax.axis_size(AXIS) // 4
    query_total = query_rows * 4 * nz
    blocks_total = owner_ref.shape[0]
    tokens = query_total + blocks_total * BLK
    piece_rows = query_rows + CAP * BLK
    full, halved = piece_layout(piece_rows)
    plane_rows = own_ref.shape[1]

    def lay(shape, axis):
        token = lax.broadcasted_iota(jnp.int32, shape, axis)
        block = (token - query_total) // BLK
        is_query = token < query_total
        owner = jnp.where(is_query, token // query_rows, 0)
        pair = jnp.where(is_query, token // QLEN, 0)

        def fill(b, carry):
            here = (block == b) & (token >= query_total)
            return (
                jnp.where(here, owner_ref[b], carry[0]),
                jnp.where(here, segment_ref[b], carry[1]),
            )

        owner, pair = lax.fori_loop(0, blocks_total, fill, (owner, pair))
        return token, block, owner, pair

    token, block, owner, pair = lay((tokens, 1), 0)
    token_row, block_row, owner_row, pair_row = lay((1, tokens), 1)
    ahead = (
        (owner == owner_row)
        & (block_row < block)
        & (token_row >= query_total)
        & (token >= query_total)
    )
    before = jnp.sum(ahead.astype(jnp.float32), axis=-1, keepdims=True).astype(jnp.int32)
    local = jnp.where(
        token < query_total,
        token % query_rows,
        query_rows + before + (token - query_total) % BLK,
    )
    source = (zi ^ (owner // 4)) * 2 + (((owner // 2) % 2) ^ yi)
    pieces = 2 * nz
    spot = source * (full * 8) + local
    if halved:
        spot = jnp.where(
            local < full * 8, spot, pieces * full * 8 + source * 4 + local - full * 8
        )
    spot = spot + ((owner % 2) ^ ci) * plane_rows
    lanes = lax.broadcasted_iota(jnp.int32, (tokens, plane_rows), 1)
    own_ref[...] = (lanes == spot).astype(jnp.bfloat16)
    away_ref[...] = (lanes == spot - plane_rows).astype(jnp.bfloat16)
    mask_ref[...] = (pair == pair_row).astype(jnp.float32)


def attention_kernel(width, pick_ref, pick_away_ref, mask_ref, own_ref, away_ref, ctx_ref, col_ref):
    tokens = pick_ref.shape[0]
    packed = dot(pick_ref[...], own_ref[...]) + dot(pick_away_ref[...], away_ref[...])
    col_ref[...] = packed[:, 256 : 256 + width].astype(jnp.bfloat16)
    query, key, value = (
        packed[:, i * HDIM : (i + 1) * HDIM].astype(jnp.bfloat16) for i in range(3)
    )
    scores = by_rows(query, key) * HDIM ** (-0.5)
    scores = jnp.where(mask_ref[...] > 0.5, scores, -1e30)
    weights = jnp.exp(scores - jnp.max(scores, axis=-1, keepdims=True))
    probability = (weights / jnp.sum(weights, axis=-1, keepdims=True)).astype(jnp.bfloat16)
    context = dot(probability, value)
    ctx_ref[...] = jnp.concatenate(
        [context[: tokens // 2], context[tokens // 2 :]], axis=1
    ).astype(jnp.bfloat16)


def gate_kernel(rows_here, chunk_rows, own, *refs):
    count = len(refs) - 8
    pieces = refs[:count]
    (
        gain_ref,
        gate_ref,
        up_ref,
        share_ref,
        out_ref,
        kept_ref,
        order_ref,
        rows_ref,
    ) = refs[count:]
    _, zi, yi, ci = place()
    nz = lax.axis_size(AXIS) // 4
    tokens, width = pieces[0].shape
    half = 2 * nz * width
    total = order_ref.shape[0]
    row = lax.broadcasted_iota(jnp.int32, (total, 1), 0)
    core = ci if own else 1 - ci
    chunk = row // chunk_rows
    device = (zi ^ (chunk // 2)) * 4 + ((chunk % 2) ^ yi) * 2 + core
    wanted = device * rows_here + jnp.minimum(row % chunk_rows, rows_here - 1)
    lanes = lax.broadcasted_iota(jnp.int32, (total, tokens), 1)
    order_ref[...] = (lanes == wanted).astype(jnp.bfloat16)
    squares = jnp.zeros((total, 1), jnp.float32)
    for dz in range(nz):
        near, far = pieces[2 * dz][...], pieces[2 * dz + 1][...]
        pair = jnp.where(
            yi == 0,
            jnp.concatenate([near, far], axis=1),
            jnp.concatenate([far, near], axis=1),
        )
        start = pl.multiple_of((zi ^ dz) * (2 * width), 128)
        values = dot(order_ref[...], pair)
        squares = squares + jnp.sum(values * values, axis=-1, keepdims=True)
        kept_ref[:, pl.ds(start, 2 * width)] = values[0:chunk_rows].astype(jnp.bfloat16)
        gain = gain_ref[:, pl.ds(pl.multiple_of(ci * half + start, 128), 2 * width)]
        rows_ref[:, pl.ds(start, 2 * width)] = (values * gain).astype(jnp.bfloat16)
    mine = pl.ds(pl.multiple_of(ci * half, 128), half)
    rows = rows_ref[...]
    units = gate_ref.shape[0]
    gate = by_rows(rows, gate_ref[:, mine])
    up = by_rows(rows, up_ref[:, mine])
    gate_other = by_rows(rows, share_ref[:units, :half])
    up_other = by_rows(rows, share_ref[:units, half:])
    spread = jnp.broadcast_to(squares, (total, out_ref.shape[1] - 4 * units))
    parts = (gate, gate_other, up, up_other) if own else (gate_other, gate, up_other, up)
    out_ref[...] = jnp.concatenate([*parts, spread], axis=1)


def packed(rows):
    count, features = rows.shape
    groups = [rows[i : i + 8] for i in range(0, count // 8 * 8, 8)]
    first = count // 8 * 8
    for size in (4, 2, 1):
        if (count - first) & size:
            step = features * size // 8
            groups.append(
                jnp.concatenate(
                    [
                        rows[first : first + size, j * step : (j + 1) * step]
                        for j in range(8 // size)
                    ],
                    axis=0,
                )
            )
            first += size
    return jnp.concatenate(groups, axis=1) if len(groups) > 1 else groups[0]


def unpack(value, target):
    count, features = target.shape
    for i in range(count // 8):
        target[i * 8 : i * 8 + 8, :] = value[:, i * features : (i + 1) * features]
    first, lane = count // 8 * 8, count // 8 * features
    for size in (4, 2, 1):
        if (count - first) & size:
            step = features * size // 8
            for j in range(8 // size):
                target[first : first + size, j * step : (j + 1) * step] = value[
                    j * size : (j + 1) * size, lane : lane + step
                ]
            first, lane = first + size, lane + step


def hidden_kernel(features, chunk_rows, rows_here, keep_ref, came_ref, down_ref, share_ref, *refs):
    hidden_ref = refs[-1]
    units = down_ref.shape[0]
    summed = keep_ref[...] + came_ref[...]
    scale = lax.rsqrt(summed[:, 4 * units : 4 * units + 1] / features + 1e-06)
    gate = summed[:, 0 : 2 * units] * scale
    up = summed[:, 2 * units : 4 * units] * scale
    hidden = (jax.nn.gelu(gate, approximate=True) * up).astype(jnp.bfloat16)
    hidden_ref[...] = hidden
    far = jnp.concatenate(
        [
            hidden[(2 * dz + 1) * chunk_rows : (2 * dz + 2) * chunk_rows]
            for dz in range(len(refs) - 1)
        ],
        axis=0,
    )
    result = dot(far[:, :units], down_ref[...]) + dot(far[:, units:], share_ref[units:, :])
    for dz in range(len(refs) - 1):
        first = dz * chunk_rows
        refs[dz][...] = packed(result[first : first + rows_here]).astype(jnp.bfloat16)


def down_kernel(chunk_rows, rows_here, hidden_ref, down_ref, share_ref, *out_refs):
    units = down_ref.shape[0]
    hidden = hidden_ref[...]
    near = jnp.concatenate(
        [
            hidden[2 * dz * chunk_rows : (2 * dz + 1) * chunk_rows]
            for dz in range(len(out_refs))
        ],
        axis=0,
    )
    result = dot(near[:, :units], down_ref[...]) + dot(near[:, units:], share_ref[units:, :])
    for dz in range(len(out_refs)):
        first = dz * chunk_rows
        out_refs[dz][...] = packed(result[first : first + rows_here])


def add_kernel(near_ref, far_ref, out_ref):
    out_ref[...] = (near_ref[...] + far_ref[...].astype(jnp.float32)).astype(jnp.bfloat16)


def last_kernel(count, *refs):
    near_ref, far_ref = refs[0], refs[1]
    arrived = refs[2 : 2 + count]
    kept_ref, kept_other_ref, out_ref, total_ref = refs[2 + count :]
    ci = place()[3]
    rows = out_ref.shape[0]
    half = kept_ref.shape[1]
    kept, other = kept_ref[...].astype(jnp.float32), kept_other_ref[...].astype(jnp.float32)
    total = near_ref[...] + far_ref[...].astype(jnp.float32)
    for ref in arrived:
        total = total + ref[...].astype(jnp.float32)
    low, high = jnp.where(ci == 0, kept, other), jnp.where(ci == 0, other, kept)
    unpack(total, total_ref)
    out_ref[:, :half] = (low[:rows] + total_ref[:, :half]).astype(jnp.bfloat16)
    out_ref[:, half:] = (high[:rows] + total_ref[:, half:]).astype(jnp.bfloat16)


def body(
    queries,
    corpus,
    block_owner,
    slot_row,
    segment,
    query_weight,
    key_weight,
    value_weight,
    out_weight,
    gain_attn,
    gain_ffn,
    gate_weight,
    up_weight,
    down_weight,
):
    devices = lax.axis_size(AXIS)
    nz = devices // 4
    _, zi, yi, ci = place()
    z_order = list(range(nz - 1, 0, -1))

    def along_z(value, k):
        return lax.ppermute(value, AXIS, [(i, i ^ (4 * k)) for i in range(devices)])

    def across_y(value):
        return lax.ppermute(value, AXIS, [(i, i ^ 2) for i in range(devices)])

    def across_core(value):
        return lax.ppermute(value, AXIS, [(i, i ^ 1) for i in range(devices)])

    def plane_gather(value, value_across=None, fence=None):
        near = {0: value}
        for k in range(1, nz):
            near[k] = along_z(value, k)
        if fence is not None:
            for k in near:
                near[k], fence = lax.optimization_barrier((near[k], fence))
        if value_across is None:
            value_across = near[0]
        return near, {
            k: across_y(near[k] if k else value_across) for k in range(nz)
        }

    def paired(near, far):
        return [piece for k in range(nz) for piece in (near[k], far[k])]

    owners = block_owner[:, 0]
    features = queries.shape[1]
    half = features // 2
    query_rows = queries.shape[0]
    tokens = query_rows * devices + owners.shape[0] * BLK
    width = features // devices
    heads_rows = query_weight.shape[0]
    units = gate_weight.shape[0]
    rows_here = tokens // devices
    chunk_rows = -(-rows_here // 16) * 16
    bf16, f32 = jnp.bfloat16, jnp.float32
    shape = jax.ShapeDtypeStruct

    full, halved = piece_layout(query_rows + CAP * BLK)
    piece = kernel_call(
        fetch_kernel,
        shape((8, full * features + halved * half), bf16),
        [SMEM, SMEM, ANY, ANY],
        [
            pltpu.VMEM((CAP, BLK, features), bf16),
            pltpu.VMEM((query_rows, features), bf16),
            pltpu.VMEM((full * 8 + halved * 8, features), f32),
            pltpu.SemaphoreType.DMA((CAP + 1,)),
        ],
        name="fetch",
        limit=60 * 1024 * 1024,
    )(owners, slot_row, corpus, queries)

    projections = [query_weight, key_weight, value_weight]
    plane_rows = 2 * nz * (full * 8 + halved * 4)
    wide = 256 + -(-width // 128) * 128
    *tied, _ = lax.optimization_barrier((*projections, piece))
    stacked = kernel_call(
        stack_kernel,
        shape((3 * heads_rows, features), bf16),
        [VMEM] * 3,
        name="stack",
        micros=20,
    )(*tied)
    piece_wide = piece.shape[1]
    value_across = kernel_call(
        across_kernel,
        shape((8, piece_wide + heads_rows // 8 * 2 * nz * width), bf16),
        [VMEM] * 2,
        name="across",
    )(piece, out_weight)
    near, far = plane_gather(piece, value_across, stacked)
    projections_other = across_core(stacked)
    own, away = kernel_call(
        functools.partial(projection_kernel, query_rows + CAP * BLK),
        (shape((plane_rows, wide), bf16), shape((plane_rows, wide), bf16)),
        [VMEM] * (2 * nz + 5),
        [pltpu.VMEM((plane_rows, features), bf16)],
        name="project",
        micros=10,
    )(*paired(near, far), gain_attn[None, :], *projections, projections_other)

    out_keep, out_send = kernel_call(
        functools.partial(pair_kernel, piece_wide),
        (shape((2 * heads_rows, nz * width), bf16),) * 2,
        [VMEM] * 2,
        name="pairs",
    )(out_weight, far[0])
    out_came = across_core(out_send)
    own, out_came = lax.optimization_barrier((own, out_came))

    plan = kernel_call(
        functools.partial(plan_kernel, query_rows),
        (
            shape((tokens, plane_rows), bf16),
            shape((tokens, plane_rows), bf16),
            shape((tokens, tokens), f32),
        ),
        [SMEM, SMEM],
        name="plan",
    )(owners, segment)
    context, columns = kernel_call(
        functools.partial(attention_kernel, width),
        (shape((tokens // 2, 2 * HDIM), bf16), shape((tokens, width), bf16)),
        [VMEM] * 5,
        name="attend",
    )(*plan, own, across_core(away))
    contexts = [
        context,
        across_y(context),
        across_core(context),
        lax.ppermute(context, AXIS, [(i, i ^ 3) for i in range(devices)]),
    ]
    attended, *parts = kernel_call(
        out_kernel,
        (shape((tokens, width), f32),) + (shape((tokens, width), bf16),) * (nz - 1),
        [VMEM] * 6,
        name="out",
    )(*contexts, out_keep, out_came)
    middle = columns.astype(f32) + attended
    for d in z_order:
        middle = middle + along_z(parts[d - 1], d).astype(f32)
    middle = middle.astype(bf16)
    share_gate, share_up, share_down, _ = lax.optimization_barrier(
        (gate_weight, up_weight, down_weight, middle)
    )
    share = across_core(
        kernel_call(
            share_kernel, shape((2 * units, features), bf16), [VMEM] * 3, name="share"
        )(share_gate, share_up, share_down)
    )


    slots = 2 * nz * chunk_rows
    lanes = -(-(4 * units + 1) // 128) * 128
    blocks = paired(*plane_gather(middle))

    def gate_up(own, blocks):
        return kernel_call(
            functools.partial(gate_kernel, rows_here, chunk_rows, own),
            (shape((slots, lanes), f32), shape((chunk_rows, half), bf16)),
            [VMEM] * (2 * nz + 4),
            [pltpu.VMEM((slots, tokens), bf16), pltpu.VMEM((slots, half), bf16)],
            name="gate_up_own" if own else "gate_up",
        )(*blocks, gain_ffn[None, :], gate_weight, up_weight, share)

    send, kept_send = gate_up(False, blocks)
    first, _ = lax.optimization_barrier((blocks[0], send))
    keep, kept = gate_up(True, [first, *blocks[1:]])
    came = across_core(send)
    kept_other = across_core(kept_send)

    chunk = shape((8, rows_here * features // 8), bf16)
    *far, hidden = kernel_call(
        functools.partial(hidden_kernel, features, chunk_rows, rows_here),
        (chunk,) * nz + (shape((slots, 2 * units), bf16),),
        [VMEM] * 4,
        name="hidden",
    )(keep, came, down_weight, share)
    moved = {k: across_y(far[k]) for k in [*range(1, nz), 0]}
    near = kernel_call(
        functools.partial(down_kernel, chunk_rows, rows_here),
        (shape(chunk.shape, f32),) * nz,
        [VMEM] * 3,
        name="down",
    )(hidden, down_weight, share)
    arrived = []
    for k in range(1, nz):
        part = kernel_call(add_kernel, chunk, [VMEM, VMEM], name="add")(near[k], moved[k])
        arrived.append(along_z(part, k))
    return kernel_call(
        functools.partial(last_kernel, len(arrived)),
        shape((rows_here, features), bf16),
        [VMEM] * (len(arrived) + 4),
        [pltpu.VMEM((rows_here, features), f32)],
        name="last",
    )(near[0], moved[0], *arrived, kept, kept_other)


def solution(mesh):
    placed = (
        P(("groups", "tensor"), None),
        P(("groups", "tensor"), None, None),
        P("groups", None),
        P("groups"),
        P("groups"),
        P("tensor", None),
        P("tensor", None),
        P("tensor", None),
        P("tensor", None),
        P(),
        P(),
        P("tensor", None),
        P("tensor", None),
        P("tensor", None),
    )
    return jax.shard_map(
        body, mesh=mesh, in_specs=placed, out_specs=P(("groups", "tensor"), None), check_vma=False
    )
```
